32 devices in a mesh: frag: 8 (over z, y), tile: 4 (over x, core).
Axes of the slice: x: 2, y: 2, z: 4, core: 2. Of those that a mesh axis runs over, the one named last changes fastest.
Arguments:
- core_fock: float32 [64, 256, 256], P('frag', 'tile'), as said below
- intersection: float32 [64, 256, 256], P('frag', 'tile'), as said below
- gamma_tile: float32 [64, 256, 256], P('frag', 'tile'), may hold values from -0.375 to 0.375
- charge_old: float32 [64, 256], P('frag'), may hold values from -6 to 6
- embed_old: float32 [64, 256], P('frag'), may hold values from -4 to 4
- core_pop: float32 [64, 256], P('frag'), may hold values from 0 to 1
- centres: float32 [64, 3, 256], P('frag'), may hold values from -10 to 10
- frag_sizes: int32 [64], P('frag'), may hold values from 20 to 256, as said below
- near_list: int32 [64, 8], P('frag'), may hold values from 0 to 63, as said below
- far_list: int32 [64, 8], P('frag'), may hold values from 0 to 63
Outputs:
- density: float32 [64, 256, 256], P('frag', 'tile')
- esp_matrix: float32 [64, 256, 256], P('frag', 'tile')
The draws below stay inside these ranges and needn't reach their ends.
Inputs may be any that keep to these rules, and one draw needn't show every extreme that they name: `frag_sizes`: each fragment uses at least 20 basis functions; some fragment uses exactly 256. near_list[f, k] is a fragment whose index differs from f by 1 to 8; the distance 8 occurs. `core_fock`: symmetric in its last two dimensions. `intersection`: symmetric in its last two dimensions.
All inputs are finite; a program needn't handle non-finite values.
Results may differ from the reference program's by a relative error of at most 0.0003.
Values sent between devices are 32-bit elements; how exact they have to be, the bound alone decides.
No kernel may reach another device: no remote copies, remote signals or barrier semaphores. Data moves between devices by JAX's collectives and lax.ppermute only.
A program may use at most 64 MiB of HBM per device.

```python
import math
import jax
import jax.numpy as jnp
from jax import lax

BASIS = 256
NEAR = 8
FAR = 8
PC = 8
ITERS = 12
SPAN = 8
FRAGS = 64


def draw_core_fock(key, part):
    first, second = jax.random.split(jax.random.fold_in(key, 11))
    noise = jax.random.normal(first, (FRAGS, BASIS, BASIS), jnp.float32)
    symmetric = (noise + jnp.transpose(noise, (0, 2, 1))) * (0.5 / math.sqrt(BASIS))
    levels = jax.random.uniform(second, (FRAGS, BASIS), jnp.float32, -1.5, 1.5)
    result = symmetric + levels[:, :, None] * jnp.eye(BASIS, dtype=jnp.float32)[None]
    return result


def draw_intersection(key, part):
    noise = jax.random.normal(jax.random.fold_in(key, 23), (FRAGS, BASIS, BASIS), jnp.float32)
    symmetric = (noise + jnp.transpose(noise, (0, 2, 1))) * (0.2 / math.sqrt(BASIS))
    return jnp.eye(BASIS, dtype=jnp.float32)[None] + symmetric


def draw_frag_sizes(key, part):
    first, second = jax.random.split(jax.random.fold_in(key, 37))
    counts = jax.random.randint(first, (FRAGS,), 20, BASIS + 1)
    spot = jax.random.randint(second, (), 0, FRAGS)
    return counts.at[spot].set(BASIS).astype(jnp.int32)


def draw_near_list(key, part):
    first, second = jax.random.split(jax.random.fold_in(key, 41))
    offsets = jax.random.randint(first, (FRAGS, NEAR), 1, SPAN + 1)
    upward = jax.random.randint(second, (FRAGS, NEAR), 0, 2)
    anchor = jnp.arange(FRAGS, dtype=jnp.int32)[:, None]
    higher = anchor + offsets
    lower = anchor - offsets
    chosen = jnp.where(upward > 0, higher, lower)
    outside = (chosen < 0) | (chosen >= FRAGS)
    other = jnp.where(upward > 0, lower, higher)
    return jnp.where(outside, other, chosen).astype(jnp.int32)


def with_ends(array, stream_key, least, largest):
    extent = array.shape
    spot = [jax.random.randint(jax.random.fold_in(stream_key, axis), (), 0, extent[axis]) for axis in range(len(extent))]
    array = array.at[tuple(spot)].set(least)
    longest = extent.index(max(extent))
    spot[longest] = (spot[longest] + 1) % extent[longest]
    return array.at[tuple(spot)].set(largest)


def block_levels(key, dims, cuts, smallest, largest):
    factor_of, own = 1.0, jax.random.fold_in(key, 6)
    for position, parts in cuts:
        draws = jnp.exp(jax.random.uniform(jax.random.fold_in(own, position), (parts,), jnp.float32, smallest / len(cuts), largest / len(cuts)))
        factor_of = factor_of * jnp.repeat(draws, dims[position] // parts).reshape([-1 if axis == position else 1 for axis in range(len(dims))])
    return factor_of


def bell_draw(key, shape, scale, limit, pieces=(), kind=jnp.bfloat16):
    values = jax.random.normal(key, shape, jnp.float32) * scale
    if len(pieces) > 0:
        values = block_levels(key, shape, pieces, -0.22, 0.18) * values
    return jnp.clip(values, min=-limit, max=limit).astype(kind)


def setup_inputs(seed: int = 0) -> dict:
    streams_of = jax.random.split(jax.random.key(seed), 11)
    return {
        "core_fock": draw_core_fock(jax.random.fold_in(streams_of[10], 71), 0),
        "intersection": draw_intersection(jax.random.fold_in(streams_of[10], 71), 0),
        "gamma_tile": bell_draw(streams_of[2], (FRAGS, BASIS, BASIS), BASIS ** -0.5, 0.375, ((0, 8), (1, 4)), jnp.float32),
        "charge_old": bell_draw(streams_of[3], (FRAGS, BASIS), 1.0, 6.0, ((0, 8),), jnp.float32),
        "embed_old": bell_draw(streams_of[4], (FRAGS, BASIS), 0.5, 4.0, ((0, 8),), jnp.float32),
        "core_pop": jnp.clip(1.0 * jax.random.uniform(streams_of[5], (FRAGS, BASIS), jnp.float32) ** block_levels(streams_of[5], (FRAGS, BASIS), ((0, 8),), -0.2, 0.2), 0.0, 1.0),
        "centres": bell_draw(streams_of[6], (FRAGS, 3, BASIS), 2.0, 10.0, ((0, 8),), jnp.float32),
        "frag_sizes": draw_frag_sizes(jax.random.fold_in(streams_of[10], 71), 0),
        "near_list": draw_near_list(jax.random.fold_in(streams_of[10], 71), 0),
        "far_list": with_ends(jax.random.randint(streams_of[9], (FRAGS, FAR), 0, FRAGS), jax.random.fold_in(streams_of[9], 1), 0, FRAGS - 1).astype(jnp.int32),
    }


precise = lax.Precision.HIGHEST
screening = 0.25

def coulomb(centre_set, source):
    dist_sq = (centre_set[0][:, None] - source[1][None, :]) ** 2
    dist_sq = dist_sq + (centre_set[1][:, None] - source[2][None, :]) ** 2
    dist_sq = dist_sq + (centre_set[2][:, None] - source[3][None, :]) ** 2
    return lax.optimization_barrier(jnp.sum(source[0][None, :] * lax.rsqrt(dist_sq + 1.0), axis=1))

def purify(fock_matrix, frag_size):
    column_index = jnp.arange(BASIS, dtype=jnp.int32)
    active = (column_index < frag_size).astype(jnp.float32)
    masked = fock_matrix * active[:, None] * active[None, :]
    frob_norm = jnp.sqrt(jnp.sum(masked * masked) + 1e-06)
    identity = jnp.eye(BASIS, dtype=jnp.float32)
    sign_est = masked / frob_norm + identity * (1.0 - active)[:, None]
    for sweep_index in range(ITERS):
        squared = jnp.dot(sign_est, sign_est, precision=precise)
        sign_est = 1.5 * sign_est - 0.5 * jnp.dot(squared, sign_est, precision=precise)
    return 0.5 * (identity - sign_est)

def reference(core_fock, intersection, gamma_tile, charge_old, embed_old, core_pop, centres, frag_sizes, near_list, far_list):

    def one_fragment(inputs):
        core_one, over_one, gamma_one, charge_one, embed_one, size_one = inputs
        field = jnp.dot(gamma_one, charge_one, precision=precise) + embed_one
        fock_matrix = core_one + 0.5 * over_one * (field[:, None] + field[None, :])
        return purify(fock_matrix, size_one)
    density = lax.map(one_fragment, (core_fock, intersection, gamma_tile, charge_old, embed_old, frag_sizes))
    charges = lax.optimization_barrier(jnp.sum(density * intersection, axis=2)) - core_pop
    table = jnp.concatenate([charges[:, None, :], centres], axis=1)
    group = BASIS // PC
    block_charge = lax.optimization_barrier(jnp.sum(charges.reshape(FRAGS, PC, group), axis=2))
    block_place = lax.optimization_barrier(jnp.mean(centres.reshape(FRAGS, 3, PC, group), axis=3))
    blocks = jnp.concatenate([block_charge[:, None, :], block_place], axis=1)

    def potential_of(inputs):
        centre_set, near_ids, far_ids = inputs

        def add_near(summed, neighbour):
            return (summed + coulomb(centre_set, table[neighbour]), None)
        summed, unused = lax.scan(add_near, jnp.zeros((BASIS,), jnp.float32), near_ids)
        far_source = jnp.transpose(blocks[far_ids], (1, 0, 2)).reshape(4, -1)
        return screening * (summed + coulomb(centre_set, far_source))
    potential = lax.map(potential_of, (centres, near_list, far_list))
    esp_matrix = 0.5 * intersection * (potential[:, :, None] + potential[:, None, :])
    return (density, esp_matrix)
```

```python
import functools

import jax
import jax.numpy as jnp
from jax import lax
from jax.experimental import pallas as pl
from jax.experimental.pallas import tpu as pltpu
from jax.sharding import PartitionSpec as P

PC = 8
ITERS = 12
SCREENING = 0.25
VMEM = pl.BlockSpec(memory_space=pltpu.VMEM)
SMEM = pl.BlockSpec(memory_space=pltpu.SMEM)


def floats(*shape):
    return jax.ShapeDtypeStruct(shape, jnp.float32)


def own_rows(rows, basis, tile_at):
    row = lax.broadcasted_iota(jnp.int32, (rows, basis), 0)
    column = lax.broadcasted_iota(jnp.int32, (rows, basis), 1)
    return column == row + tile_at * rows


def half_fock_kernel(core_ref, over_ref, gamma_ref, charge_ref, embed_ref, *outs):
    tiles = lax.axis_size("tile")
    tile_at = lax.axis_index("tile")
    frag_dev, rows, basis = core_ref.shape
    share = frag_dev // tiles
    pick = own_rows(rows, basis, tile_at)
    for shift in range(tiles):
        target = lax.rem(tile_at + shift, tiles)
        for place in range(share):
            frag = target * share + place
            over = over_ref[frag]
            terms = gamma_ref[frag] * charge_ref[pl.ds(frag, 1), :]
            terms = terms + jnp.where(pick, embed_ref[pl.ds(frag, 1), :], 0.0)
            field = jnp.sum(terms, axis=1, keepdims=True)
            outs[shift][place] = 0.5 * (core_ref[frag] + over * field)
            outs[tiles + shift][place] = over


def split(x):
    high = x.astype(jnp.bfloat16)
    low = (x - high.astype(jnp.float32)).astype(jnp.bfloat16)
    return high, low


def product(left, right):
    lh, ll = left
    rh, rl = right
    dot = functools.partial(jnp.dot, preferred_element_type=jnp.float32)
    return dot(lh, rh) + (dot(lh, rl) + dot(ll, rh))


def density_kernel(tiles, sizes_ref, pop_ref, *refs):
    halves, overs = refs[:tiles], refs[tiles : 2 * tiles]
    chunks, charge_ref = refs[2 * tiles : 3 * tiles], refs[3 * tiles]
    x_ref, s_ref = refs[3 * tiles + 1 :]
    tile_at = lax.axis_index("tile")
    share, rows, basis = halves[0].shape
    for shift in range(tiles):
        source = lax.rem(tile_at + tiles - shift, tiles)
        span = pl.ds(pl.multiple_of(source * rows, rows), rows)
        for place in range(share):
            x_ref[place, span, :] = halves[shift][place]
            s_ref[place, span, :] = overs[shift][place]
    row = lax.broadcasted_iota(jnp.int32, (basis, basis), 0)
    column = lax.broadcasted_iota(jnp.int32, (basis, basis), 1)
    for place in range(share):
        size = sizes_ref[tile_at * share + place]
        half = x_ref[place]
        fock = half + half.T
        masked = jnp.where((row < size) & (column < size), fock, 0.0)
        frob = jnp.sqrt(jnp.sum(masked * masked, keepdims=True) + 1e-06)
        x_ref[place] = masked / frob + jnp.where((row == column) & (row >= size), 1.0, 0.0)

    def sweep(index, carry):
        estimates = [x_ref[place] for place in range(share)]
        parts = [split(x) for x in estimates]
        squares = [split(0.5 * product(p, p)) for p in parts]
        cubes = [product(y, p) for y, p in zip(squares, parts)]
        for place in range(share):
            x_ref[place] = 1.5 * estimates[place] - cubes[place]
        return carry

    lax.fori_loop(0, ITERS, sweep, 0)
    devices = charge_ref.shape[0]
    for place in range(share):
        density = jnp.where(row == column, 0.5, 0.0) - 0.5 * x_ref[place]
        x_ref[place] = density
        charge = jnp.sum(density * s_ref[place], axis=0, keepdims=True)
        charge = charge - pop_ref[pl.ds(tile_at * share + place, 1), :]
        charge_ref[:, place : place + 1, :] = jnp.broadcast_to(charge[None], (devices, 1, basis))
    for shift in range(tiles):
        target = lax.rem(tile_at + shift, tiles)
        span = pl.ds(pl.multiple_of(target * rows, rows), rows)
        for place in range(share):
            chunks[shift][place] = x_ref[place, span, :]


def block_mask(group, basis):
    block = lax.broadcasted_iota(jnp.int32, (PC, basis), 0)
    column = lax.broadcasted_iota(jnp.int32, (PC, basis), 1)
    return (column >= block * group) & (column < (block + 1) * group)


def coulomb_kernel(near_ref, far_ref, place_ref, column_ref, table_ref, near_out, far_out):
    frag_dev, basis, _ = column_ref.shape
    near, far = near_ref.shape[1], far_ref.shape[1]
    group = basis // PC
    mask = block_mask(group, basis)

    def one_fragment(frag, carry):
        spots = column_ref[frag]
        columns = [spots[:, axis : axis + 1] for axis in range(3)]
        rows = [place_ref[frag, axis : axis + 1, :] for axis in range(3)]
        for k in range(near):
            other = near_ref[frag, k]
            total = 1.0
            for axis in range(3):
                gap = columns[axis] - table_ref[other, axis : axis + 1, :]
                total = total + gap * gap
            near_out[frag, k] = lax.rsqrt(total)
        for m in range(far):
            other = far_ref[frag, m]
            total = 1.0
            for axis in range(3):
                inside = jnp.where(mask, table_ref[other, axis : axis + 1, :], 0.0)
                spot = jnp.sum(inside, axis=1, keepdims=True) * (1.0 / group)
                gap = rows[axis] - spot
                total = total + gap * gap
            far_out[frag, m] = lax.rsqrt(total)
        return carry

    lax.fori_loop(0, frag_dev, one_fragment, 0)


def potential_kernel(tiles, near_ref, far_ref, charge_ref, near_part, far_part, over_ref, *refs):
    chunks, density_ref, esp_ref = refs[:tiles], refs[tiles], refs[tiles + 1]
    tile_at = lax.axis_index("tile")
    frag_dev, rows, basis = over_ref.shape
    share = frag_dev // tiles
    near, far = near_ref.shape[1], far_ref.shape[1]
    pick = own_rows(rows, basis, tile_at)
    mask = block_mask(basis // PC, basis)
    for shift in range(tiles):
        source = lax.rem(tile_at + tiles - shift, tiles)
        for place in range(share):
            density_ref[source * share + place] = chunks[shift][place]

    def one_fragment(frag, carry):
        total = jnp.zeros((basis, basis), jnp.float32)
        for k in range(near):
            total = total + near_part[frag, k] * charge_ref[pl.ds(near_ref[frag, k], 1), :]
        folded = total[:, :128]
        for start in range(128, basis, 128):
            folded = folded + total[:, start : start + 128]
        blocks = jnp.zeros((PC, basis), jnp.float32)
        for m in range(far):
            inside = jnp.where(mask, charge_ref[pl.ds(far_ref[frag, m], 1), :], 0.0)
            blocks = blocks + jnp.sum(inside, axis=1, keepdims=True) * far_part[frag, m]
        potential = jnp.sum(folded.T, axis=0, keepdims=True) + jnp.sum(blocks, axis=0, keepdims=True)
        potential = (0.5 * SCREENING) * potential
        mine = jnp.sum(jnp.where(pick, potential, 0.0), axis=1, keepdims=True)
        esp_ref[frag] = over_ref[frag] * (mine + potential)
        return carry

    lax.fori_loop(0, frag_dev, one_fragment, 0)


def call(kernel, outs, inputs, specs, scratch=()):
    return pl.pallas_call(
        kernel,
        out_shape=outs,
        in_specs=specs,
        out_specs=[VMEM] * len(outs),
        scratch_shapes=list(scratch),
        compiler_params=pltpu.CompilerParams(vmem_limit_bytes=48 * 1024 * 1024),
    )(*inputs)


def shifted(chunks, axis):
    peers = lax.axis_size(axis)
    moved = [chunks[0]]
    for shift in range(1, peers):
        pairs = [(i, (i + shift) % peers) for i in range(peers)]
        moved.append(lax.ppermute(chunks[shift], axis, pairs))
    return moved


def per_device(
    core_fock,
    intersection,
    gamma_tile,
    charge_old,
    embed_old,
    core_pop,
    centres,
    frag_sizes,
    near_list,
    far_list,
):
    frag_dev, rows, basis = core_fock.shape
    tiles, peers = lax.axis_size("tile"), lax.axis_size("frag")
    devices, share = tiles * peers, frag_dev // tiles
    chunk = floats(share, rows, basis)
    sent = call(
        half_fock_kernel,
        [chunk] * (2 * tiles),
        (core_fock, intersection, gamma_tile, charge_old, embed_old),
        [VMEM] * 5,
    )
    halves = shifted(sent[:tiles], "tile")
    overs = shifted(sent[tiles:], "tile")
    copies = jnp.broadcast_to(centres[None], (peers,) + centres.shape)
    table = lax.all_to_all(copies, "frag", split_axis=0, concat_axis=0, tiled=True)
    table = table.reshape((peers * frag_dev,) + centres.shape[1:])
    near_part, far_part = call(
        coulomb_kernel,
        [floats(frag_dev, near_list.shape[1], basis, basis), floats(frag_dev, far_list.shape[1], PC, basis)],
        (near_list, far_list, centres, jnp.transpose(centres, (0, 2, 1)), table),
        [SMEM, SMEM, VMEM, VMEM, VMEM],
    )
    *pieces, charges = call(
        functools.partial(density_kernel, tiles),
        [chunk] * tiles + [floats(devices, share, basis)],
        (frag_sizes, core_pop, *halves, *overs),
        [SMEM] + [VMEM] * (1 + 2 * tiles),
        [pltpu.VMEM((share, basis, basis), jnp.float32)] * 2,
    )
    charges = lax.all_to_all(charges, ("frag", "tile"), split_axis=0, concat_axis=0, tiled=True)
    charges = charges.reshape(devices * share, basis)
    pieces = shifted(pieces, "tile")
    density, esp_matrix = call(
        functools.partial(potential_kernel, tiles),
        [floats(frag_dev, rows, basis)] * 2,
        (near_list, far_list, charges, near_part, far_part, intersection, *pieces),
        [SMEM, SMEM] + [VMEM] * (4 + tiles),
    )
    return (density, esp_matrix)


def solution(mesh):
    in_specs = (
        P("frag", "tile", None),
        P("frag", "tile", None),
        P("frag", "tile", None),
        P("frag", None),
        P("frag", None),
        P("frag", None),
        P("frag", None, None),
        P("frag"),
        P("frag", None),
        P("frag", None),
    )
    out_specs = (P("frag", "tile", None), P("frag", "tile", None))
    return jax.shard_map(
        per_device, mesh=mesh, in_specs=in_specs, out_specs=out_specs, check_vma=False
    )
```

```python
import functools

import jax
import jax.numpy as jnp
from jax import lax
from jax.experimental import pallas as pl
from jax.experimental.pallas import tpu as pltpu
from jax.sharding import PartitionSpec as P

PC = 8
ITERS = 12
SCREENING = 0.25
SPAN = 8
VMEM = pl.BlockSpec(memory_space=pltpu.VMEM)
SMEM = pl.BlockSpec(memory_space=pltpu.SMEM)
HBM = pl.BlockSpec(memory_space=pltpu.HBM)
ANY = pl.BlockSpec(memory_space=pl.ANY)


def floats(*shape):
    return jax.ShapeDtypeStruct(shape, jnp.float32)


def own_rows(rows, basis, tile_at):
    row = lax.broadcasted_iota(jnp.int32, (rows, basis), 0)
    column = lax.broadcasted_iota(jnp.int32, (rows, basis), 1)
    return column == row + tile_at * rows


def half_fock_kernel(*refs):
    inputs, outs, buffers, sems = refs[:8], refs[8:-9], refs[-9:-1], refs[-1]
    copies = [
        pltpu.make_async_copy(source, buffer, sems.at[at])
        for at, (source, buffer) in enumerate(zip(inputs, buffers))
    ]
    for copy in copies:
        copy.start()
    for copy in copies:
        copy.wait()
    sizes_ref, charge_ref, embed_ref, pop_ref, place_ref, gamma_ref, over_ref, core_ref = buffers
    tiles = lax.axis_size("tile")
    tile_at = lax.axis_index("tile")
    frag_dev, rows, basis = core_ref.shape
    share = frag_dev // tiles
    for peer in range(outs[-1].shape[0]):
        outs[-1][peer] = place_ref[...]
    pick = own_rows(rows, basis, tile_at)
    row = lax.broadcasted_iota(jnp.int32, (rows, basis), 0) + tile_at * rows
    column = lax.broadcasted_iota(jnp.int32, (rows, basis), 1)
    lane = lax.broadcasted_iota(jnp.int32, (1, basis), 1)
    for shift in range(tiles):
        target = lax.rem(tile_at + shift, tiles)
        for place in range(share):
            frag = target * share + place
            over = over_ref[frag]
            terms = gamma_ref[frag] * charge_ref[pl.ds(frag, 1), :]
            terms = terms + jnp.where(pick, embed_ref[pl.ds(frag, 1), :], 0.0)
            field = jnp.sum(terms, axis=1, keepdims=True)
            half = 0.5 * (core_ref[frag] + over * field)
            size = sizes_ref[frag]
            outs[shift][place] = jnp.where((row < size) & (column < size), half, 0.0)
            outs[tiles + shift][place] = over
            if shift == 0:
                outs[-2][place : place + 1, :] = (lane >= size).astype(jnp.float32)
                outs[-2][share + place : share + place + 1, :] = pop_ref[pl.ds(frag, 1), :]


def split(x):
    high = x.astype(jnp.bfloat16)
    low = (x - high.astype(jnp.float32)).astype(jnp.bfloat16)
    return high, low


def product(left, right):
    lh, ll = left
    rh, rl = right
    dot = functools.partial(jnp.dot, preferred_element_type=jnp.float32)
    return dot(lh, rh) + (dot(lh, rl) + dot(ll, rh))


def density_kernel(tiles, facts_ref, *refs):
    halves, chunks, x_ref = refs[:tiles], refs[-tiles - 1 : -1], refs[-1]
    tile_at = lax.axis_index("tile")
    share, rows, basis = halves[0].shape
    for shift in range(tiles):
        source = lax.rem(tile_at + tiles - shift, tiles)
        span = pl.ds(pl.multiple_of(source * rows, rows), rows)
        for place in range(share):
            x_ref[place, span, :] = halves[shift][place]
    row = lax.broadcasted_iota(jnp.int32, (basis, basis), 0)
    column = lax.broadcasted_iota(jnp.int32, (basis, basis), 1)
    for place in range(share):
        half = x_ref[place]
        masked = half + half.T
        frob = jnp.sqrt(jnp.sum(masked * masked, keepdims=True) + 1e-06)
        x_ref[place] = masked / frob + jnp.where(row == column, facts_ref[place : place + 1, :], 0.0)

    def sweep(index, carry):
        estimates = [x_ref[place] for place in range(share)]
        parts = [split(x) for x in estimates]
        squares = [split(0.5 * product(p, p)) for p in parts]
        cubes = [product(y, p) for y, p in zip(squares, parts)]
        for place in range(share):
            x_ref[place] = 1.5 * estimates[place] - cubes[place]
        return carry

    lax.fori_loop(0, ITERS, sweep, 0)
    for place in range(share):
        x_ref[place] = jnp.where(row == column, 0.5, 0.0) - 0.5 * x_ref[place]
    for shift in range(tiles):
        target = lax.rem(tile_at + shift, tiles)
        span = pl.ds(pl.multiple_of(target * rows, rows), rows)
        for place in range(share):
            chunks[shift][place] = x_ref[place, span, :]


def charge_kernel(tiles, facts_ref, *refs):
    overs, chunks, charge_ref = refs[:tiles], refs[tiles : 2 * tiles], refs[-1]
    share, rows, basis = overs[0].shape
    devices = charge_ref.shape[0]
    for place in range(share):
        terms = chunks[0][place] * overs[0][place]
        for shift in range(1, tiles):
            terms = terms + chunks[shift][place] * overs[tiles - shift][place]
        charge = jnp.sum(terms, axis=0, keepdims=True) - facts_ref[share + place : share + place + 1, :]
        charge_ref[:, place : place + 1, :] = jnp.broadcast_to(charge[None], (devices, 1, basis))


def block_mask(group, basis):
    block = lax.broadcasted_iota(jnp.int32, (PC, basis), 0)
    column = lax.broadcasted_iota(jnp.int32, (PC, basis), 1)
    return (column >= block * group) & (column < (block + 1) * group)


def pieces_of(x):
    out = []
    for _ in range(3):
        piece = x.astype(jnp.bfloat16).astype(jnp.float32)
        out.append(piece)
        x = x - piece
    return out


PAIRS = ((0, 0), (0, 1), (1, 0), (0, 2), (1, 1), (2, 0))
DEPTH = 32


def geometry_kernel(near_ref, far_ref, own_ref, table_ref, *refs):
    left_out, right_out, far_out, near_hot, far_hot, side_ref, table_side = refs[-7:]
    frag_dev, near = near_ref.shape
    far = far_ref.shape[1]
    peers, _, _, basis = table_ref.shape
    group = basis // PC
    mask = block_mask(group, basis)
    frags = peers * frag_dev
    lane = lax.broadcasted_iota(jnp.int32, (1, frags), 1)
    ones = jnp.ones((frag_dev, basis), jnp.float32)
    frag_at = lax.axis_index("frag")
    reach = table_side.shape[0] // frag_dev // 2

    def fill(target, first, places, scale, extra, which):
        rows = []
        for place in places:
            parts = pieces_of(place)
            rows += [scale * parts[pair[which]] for pair in PAIRS]
        norm = places[0] * places[0] + places[1] * places[1] + places[2] * places[2] + extra
        sides = [pieces_of(norm), [ones] * 3]
        rows += sides[which] + sides[1 - which]
        rows += [0.0 * ones] * (DEPTH - len(rows))
        for at, row in enumerate(rows):
            for frag in range(frag_dev):
                target[first + frag, at : at + 1, :] = row[frag : frag + 1, :]

    fill(side_ref, 0, [own_ref[axis] for axis in range(3)], -2.0, 1.0, 0)
    for frag in range(frag_dev):
        left_out[frag] = side_ref[frag].astype(jnp.bfloat16)
    for step in range(2 * reach + 1):
        peer = jnp.clip(frag_at + step - reach, 0, peers - 1)
        fill(table_side, step * frag_dev, [table_ref[peer, axis] for axis in range(3)], 1.0, 0.0, 1)

    def one_fragment(frag, carry):
        rows = [own_ref[axis, pl.ds(frag, 1), :] for axis in range(3)]
        for k in range(near):
            other = near_ref[frag, k]
            near_hot[frag, k : k + 1, :] = (lane == other).astype(jnp.float32)
            slot = other - (frag_at - reach) * frag_dev
            right_out[frag, k] = table_side[slot].astype(jnp.bfloat16)
        for m in range(far):
            other = far_ref[frag, m]
            far_hot[frag, m : m + 1, :] = (lane == other).astype(jnp.float32)
            peer, place = other // frag_dev, lax.rem(other, frag_dev)
            total = 1.0
            for axis in range(3):
                inside = jnp.where(mask, table_ref[peer, axis, pl.ds(place, 1), :], 0.0)
                spot = jnp.sum(inside, axis=1, keepdims=True) * (1.0 / group)
                gap = rows[axis] - spot
                total = total + gap * gap
            far_out[frag, m] = lax.rsqrt(total)
        return carry

    lax.fori_loop(0, frag_dev, one_fragment, 0)


def potential_kernel(tiles, charge_ref, left_ref, right_ref, far_part, near_hot, far_hot, *refs):
    overs, chunks = refs[:tiles], refs[tiles : 2 * tiles]
    density_ref, esp_ref, near_charge, far_charge, esp_rows, sems = refs[2 * tiles :]
    tile_at = lax.axis_index("tile")
    share, rows, basis = overs[0].shape
    frag_dev, near = near_hot.shape[:2]
    far = far_hot.shape[1]
    copies = []
    for shift in range(tiles):
        source = lax.rem(tile_at + tiles - shift, tiles)
        target = density_ref.at[pl.ds(source * share, share)]
        copies.append(pltpu.make_async_copy(chunks[shift], target, sems.at[shift]))
    for copy in copies:
        copy.start()
    pick = own_rows(rows, basis, tile_at)
    mask = block_mask(basis // PC, basis)
    charges = charge_ref[...].reshape(-1, basis)
    for hot, gathered in ((near_hot, near_charge), (far_hot, far_charge)):
        every = hot[...].reshape(-1, hot.shape[2])
        picked = jnp.dot(every, charges, precision=lax.Precision.HIGHEST, preferred_element_type=jnp.float32)
        gathered[...] = picked.reshape(gathered.shape)
    for shift in range(tiles):
        target = lax.rem(tile_at + shift, tiles)
        for place in range(share):
            frag = target * share + place
            folded = jnp.zeros((basis, 128), jnp.float32)
            for k in range(near):
                square = lax.dot_general(
                    left_ref[frag],
                    right_ref[frag, k],
                    (((0,), (0,)), ((), ())),
                    preferred_element_type=jnp.float32,
                )
                terms = lax.rsqrt(square) * near_charge[frag, k : k + 1, :]
                for start in range(0, basis, 128):
                    folded = folded + terms[:, start : start + 128]
            blocks = jnp.zeros((PC, basis), jnp.float32)
            for m in range(far):
                inside = jnp.where(mask, far_charge[frag, m : m + 1, :], 0.0)
                blocks = blocks + jnp.sum(inside, axis=1, keepdims=True) * far_part[frag, m]
            potential = jnp.sum(folded.T, axis=0, keepdims=True) + jnp.sum(blocks, axis=0, keepdims=True)
            potential = (0.5 * SCREENING) * potential
            mine = jnp.sum(jnp.where(pick, potential, 0.0), axis=1, keepdims=True)
            esp_rows[shift, place] = overs[shift][place] * (mine + potential)
        copies.append(
            pltpu.make_async_copy(
                esp_rows.at[shift], esp_ref.at[pl.ds(target * share, share)], sems.at[tiles + shift]
            )
        )
        copies[-1].start()
    for copy in copies:
        copy.wait()


def call(kernel, outs, inputs, specs, scratch=(), cost=None, out_spec=VMEM):
    return pl.pallas_call(
        kernel,
        out_shape=outs,
        in_specs=specs,
        out_specs=[out_spec] * len(outs),
        scratch_shapes=list(scratch),
        cost_estimate=cost,
        compiler_params=pltpu.CompilerParams(vmem_limit_bytes=24 * 1024 * 1024),
    )(*inputs)


def shifted(chunks, axis):
    peers = lax.axis_size(axis)
    moved = [chunks[0]]
    for shift in range(1, peers):
        pairs = [(i, (i + shift) % peers) for i in range(peers)]
        moved.append(lax.ppermute(chunks[shift], axis, pairs))
    return moved


def per_device(
    core_fock,
    intersection,
    gamma_tile,
    charge_old,
    embed_old,
    core_pop,
    centres,
    frag_sizes,
    near_list,
    far_list,
):
    frag_dev, rows, basis = core_fock.shape
    tiles, peers = lax.axis_size("tile"), lax.axis_size("frag")
    devices, share = tiles * peers, frag_dev // tiles
    chunk = floats(share, rows, basis)
    places = jnp.transpose(centres, (1, 0, 2))
    inputs = (frag_sizes, charge_old, embed_old, core_pop, places, gamma_tile, intersection, core_fock)
    *sent, facts, copies = call(
        half_fock_kernel,
        [chunk] * (2 * tiles) + [floats(2 * share, basis), floats(peers, *places.shape)],
        [pltpu.with_memory_space_constraint(x, pltpu.HBM) for x in inputs],
        [HBM] * len(inputs),
        [pltpu.SMEM(frag_sizes.shape, jnp.int32)]
        + [pltpu.VMEM(x.shape, jnp.float32) for x in inputs[1:]]
        + [pltpu.SemaphoreType.DMA((len(inputs),))],
    )
    halves = shifted(sent[:tiles], "tile")
    table = lax.all_to_all(copies, "frag", split_axis=0, concat_axis=0, tiled=True)
    overs = shifted(sent[tiles:], "tile")
    pieces = call(
        functools.partial(density_kernel, tiles),
        [chunk] * tiles,
        (facts, *halves, table),
        [VMEM] * (1 + tiles) + [ANY],
        [pltpu.VMEM((share, basis, basis), jnp.float32)],
        pl.CostEstimate(flops=12 * ITERS * share * basis**3, bytes_accessed=0, transcendentals=0),
    )
    (charges,) = call(
        functools.partial(charge_kernel, tiles),
        [floats(devices, share, basis)],
        (facts, *overs, *pieces),
        [VMEM] * (1 + 2 * tiles),
    )
    near, far, frags = near_list.shape[1], far_list.shape[1], peers * frag_dev
    reach = -(-SPAN // frag_dev)
    parts = call(
        geometry_kernel,
        [
            jax.ShapeDtypeStruct((frag_dev, DEPTH, basis), jnp.bfloat16),
            jax.ShapeDtypeStruct((frag_dev, near, DEPTH, basis), jnp.bfloat16),
            floats(frag_dev, far, PC, basis),
            floats(frag_dev, near, frags),
            floats(frag_dev, far, frags),
        ],
        (near_list, far_list, places, table, pieces[0]),
        [SMEM, SMEM, VMEM, VMEM, ANY],
        [
            pltpu.VMEM((frag_dev, DEPTH, basis), jnp.float32),
            pltpu.VMEM(((2 * reach + 1) * frag_dev, DEPTH, basis), jnp.float32),
        ],
        pl.CostEstimate(flops=10**7, bytes_accessed=10**7, transcendentals=0),
    )
    charges, *pieces = lax.optimization_barrier((charges, *pieces))
    charges = lax.all_to_all(charges, ("frag", "tile"), split_axis=0, concat_axis=0, tiled=True)
    moved = shifted(pieces, "tile")
    density, esp_matrix = call(
        functools.partial(potential_kernel, tiles),
        [floats(frag_dev, rows, basis)] * 2,
        (charges, *parts, *sent[tiles:], *moved),
        [VMEM] * (6 + 2 * tiles),
        [
            pltpu.VMEM((frag_dev, near, basis), jnp.float32),
            pltpu.VMEM((frag_dev, far, basis), jnp.float32),
            pltpu.VMEM((tiles, share, rows, basis), jnp.float32),
            pltpu.SemaphoreType.DMA((2 * tiles,)),
        ],
        out_spec=HBM,
    )
    return (density, esp_matrix)


def solution(mesh):
    in_specs = (
        P("frag", "tile", None),
        P("frag", "tile", None),
        P("frag", "tile", None),
        P("frag", None),
        P("frag", None),
        P("frag", None),
        P("frag", None, None),
        P("frag"),
        P("frag", None),
        P("frag", None),
    )
    out_specs = (P("frag", "tile", None), P("frag", "tile", None))
    return jax.shard_map(
        per_device, mesh=mesh, in_specs=in_specs, out_specs=out_specs, check_vma=False
    )
```

```python
import functools

import jax
import jax.numpy as jnp
from jax import lax
from jax.experimental import pallas as pl
from jax.experimental.pallas import tpu as pltpu
from jax.sharding import PartitionSpec as P

PC = 8
ITERS = 12
SCREENING = 0.25
SPAN = 8
LANES = 128
CHUNK = 128
VMEM = pl.BlockSpec(memory_space=pltpu.VMEM)
SMEM = pl.BlockSpec(memory_space=pltpu.SMEM)
HBM = pl.BlockSpec(memory_space=pltpu.HBM)
ANY = pl.BlockSpec(memory_space=pl.ANY)


def floats(*shape):
    return jax.ShapeDtypeStruct(shape, jnp.float32)


def block_mask(basis):
    group = basis // PC
    block = lax.broadcasted_iota(jnp.int32, (PC, basis), 0)
    column = lax.broadcasted_iota(jnp.int32, (PC, basis), 1)
    return (column >= block * group) & (column < (block + 1) * group)


def block_lanes(at):
    block = lax.broadcasted_iota(jnp.int32, (PC, LANES), 0)
    lane = lax.broadcasted_iota(jnp.int32, (PC, LANES), 1)
    return lane == block + at * PC


def block_row(rows, first):
    mask = block_mask(rows[0].shape[1])
    total = jnp.zeros((PC, LANES), jnp.float32)
    for at, row in enumerate(rows):
        sums = jnp.sum(jnp.where(mask, row, 0.0), axis=1, keepdims=True)
        total = total + jnp.where(block_lanes(first + at), sums, 0.0)
    return jnp.sum(total, axis=0, keepdims=True)


def own_rows(rows, basis, first):
    row = lax.broadcasted_iota(jnp.int32, (rows, basis), 0)
    column = lax.broadcasted_iota(jnp.int32, (rows, basis), 1)
    return column == row + first


def seat(tiles):
    places = tiles // 2
    tile_at = lax.axis_index("tile")
    return tile_at // places, lax.rem(tile_at, places), places


def partner(shift, tiles, sign=1):
    half, place, places = seat(tiles)
    other = half if shift < places else 1 - half
    return other * places + lax.rem(place + places + sign * (shift % places), places)


def swapped(half, x):
    middle = x.shape[-1] // 2
    left, right = x[..., :middle], x[..., middle:]
    return jnp.where(half == 0, left, right), jnp.where(half == 0, right, left)


def half_fock_kernel(tiles, *refs):
    inputs, outs, buffers, sems = refs[:8], refs[8:-9], refs[-9:-1], refs[-1]
    copies = [
        pltpu.make_async_copy(source, buffer, sems.at[at])
        for at, (source, buffer) in enumerate(zip(inputs, buffers))
    ]
    for copy in copies:
        copy.start()
    for copy in copies:
        copy.wait()
    sizes_ref, charge_ref, embed_ref, pop_ref, place_ref, gamma_ref, over_ref, core_ref = buffers
    half, place_at, places = seat(tiles)
    frag_dev, rows, basis = core_ref.shape
    share, middle = frag_dev // tiles, basis // 2
    pick = own_rows(rows, basis, lax.axis_index("tile") * rows)
    pick_half = own_rows(rows, middle, place_at * rows)
    row = lax.broadcasted_iota(jnp.int32, (rows, middle), 0) + lax.axis_index("tile") * rows
    column = lax.broadcasted_iota(jnp.int32, (rows, middle), 1)
    mine, others = column + half * middle, column + (1 - half) * middle
    lane = lax.broadcasted_iota(jnp.int32, (1, basis), 1)
    for shift in range(tiles):
        target = partner(shift, tiles)
        for spot in range(share):
            frag = target * share + spot
            size = sizes_ref[frag]
            terms = gamma_ref[frag] * charge_ref[pl.ds(frag, 1), :]
            terms = terms + jnp.where(pick, embed_ref[pl.ds(frag, 1), :], 0.0)
            field = jnp.sum(terms, axis=1, keepdims=True)
            core, core_far = swapped(half, core_ref[frag])
            over, over_far = swapped(half, over_ref[frag])
            inside = (row < size) & (mine < size)
            over = jnp.where(inside, over, 0.0)
            near_part = jnp.where(inside, 0.5 * core, 0.0) + over * (0.5 * field)
            out = outs[shift]
            if shift < places:
                inside = (row < size) & (others < size)
                over_far = jnp.where(inside, over_far, 0.0)
                out[0, spot, :, :middle] = near_part
                out[0, spot, :, middle:] = jnp.where(inside, core_far, 0.0) + over_far * (0.5 * field)
                out[1, spot, :, :middle] = over
                out[1, spot, :, middle:] = over_far
            else:
                out[spot, :rows] = near_part
                out[spot, rows : 2 * rows] = over
                field_row = jnp.sum(jnp.where(pick_half, field, 0.0), axis=0, keepdims=True)
                out[spot, 2 * rows :] = jnp.broadcast_to(field_row, (out.shape[1] - 2 * rows, middle))
            if shift == 0:
                facts = outs[-1]
                idle = swapped(half, (lane >= size).astype(jnp.float32))
                facts[spot : spot + 1, :middle] = idle[0]
                facts[spot : spot + 1, middle:] = idle[1]
                facts[share + spot : share + spot + 1, :] = pop_ref[pl.ds(frag, 1), :]
                spots = [place_ref[axis, pl.ds(frag, 1), :] for axis in range(3)]
                means = block_row(spots, 0) * (PC / basis)
                facts[2 * share + spot : 2 * share + spot + 1, :LANES] = means


def split(x):
    high = x.astype(jnp.bfloat16)
    low = (x - high.astype(jnp.float32)).astype(jnp.bfloat16)
    return high, low


def product(left, right):
    lh, ll = left
    rh, rl = right
    dot = functools.partial(jnp.dot, preferred_element_type=jnp.float32)
    return dot(lh, rh) + (dot(lh, rl) + dot(ll, rh))


def density_kernel(tiles, facts_ref, *refs):
    places = tiles // 2
    near_parts, far_parts = refs[:places], refs[places:tiles]
    chunks, charge_ref = refs[tiles : 2 * tiles], refs[2 * tiles]
    x_ref, s_ref = refs[2 * tiles + 1 :]
    half, place_at, _ = seat(tiles)
    _, share, rows, basis = near_parts[0].shape
    middle = basis // 2
    for shift in range(places):
        source = lax.rem(place_at + places - shift, places) * rows
        span = pl.ds(pl.multiple_of(source, rows), rows)
        far_span = pl.ds(pl.multiple_of(source + middle, rows), rows)
        for spot in range(share):
            x_ref[spot, span, :] = near_parts[shift][0, spot]
            s_ref[spot, span, :] = near_parts[shift][1, spot]
            x_ref[spot, far_span, middle:] = far_parts[shift][spot, :rows]
            s_ref[spot, far_span, middle:] = far_parts[shift][spot, rows : 2 * rows]
    row = lax.broadcasted_iota(jnp.int32, (basis, basis), 0)
    column = lax.broadcasted_iota(jnp.int32, (basis, basis), 1)
    near, far = slice(0, middle), slice(middle, basis)
    for spot in range(share):
        field = far_parts[0][spot, 2 * rows : 2 * rows + 1, :]
        for part in far_parts[1:]:
            field = field + part[spot, 2 * rows : 2 * rows + 1, :]
        corner, last = x_ref[spot, near, near], x_ref[spot, far, far]
        side = x_ref[spot, near, far] + s_ref[spot, near, far] * (0.5 * field)
        corner, last = corner + corner.T, last + last.T
        total = corner * corner + last * last + 2.0 * (side * side)
        scale = 1.0 / jnp.sqrt(jnp.sum(total, keepdims=True) + 1e-06)
        idle = jnp.where(row == column, facts_ref[spot : spot + 1, :], 0.0)
        x_ref[spot, near, near] = corner * scale + idle[near, near]
        x_ref[spot, near, far] = side * scale
        x_ref[spot, far, near] = side.T * scale
        x_ref[spot, far, far] = last * scale + idle[far, far]

    chunk = min(CHUNK, basis)
    spans = [(spot, slice(at, at + chunk)) for spot in range(share) for at in range(0, basis, chunk)]
    for _ in range(ITERS):
        estimates = [x_ref[spot] for spot in range(share)]
        parts = [split(x) for x in estimates]
        squares = []
        for spot, span in spans:
            left = [part[span] for part in parts[spot]]
            squares.append(split(0.5 * product(left, parts[spot])))
        for square, (spot, span) in zip(squares, spans):
            x_ref[spot, span] = 1.5 * estimates[spot][span] - product(square, parts[spot])

    for spot in range(share):
        density = jnp.where(row == column, 0.5, 0.0) - 0.5 * x_ref[spot]
        x_ref[spot] = density
        side = density[near, far] * s_ref[spot, near, far]
        corner = density[near, near] * s_ref[spot, near, near] + side.T
        last = density[far, far] * s_ref[spot, far, far] + side
        sums = [jnp.sum(block, axis=0, keepdims=True) for block in (corner, last)]
        charge = jnp.concatenate(swapped(half, jnp.concatenate(sums, axis=1)), axis=1)
        charge = charge - facts_ref[share + spot : share + spot + 1, :]
        blocks = block_row([charge], 3) + facts_ref[2 * share + spot : 2 * share + spot + 1, :LANES]
        whole = jnp.concatenate([charge, blocks], axis=1)
        charge_ref[:, spot : spot + 1, :] = jnp.broadcast_to(whole[None], (charge_ref.shape[0],) + whole.shape)
    for shift in range(tiles):
        first = partner(shift, tiles) % places * rows + (0 if shift < places else middle)
        span = pl.ds(pl.multiple_of(first, rows), rows)
        for spot in range(share):
            left, right = swapped(half, x_ref[spot, span, :])
            chunks[shift][spot, :, :middle] = left
            chunks[shift][spot, :, middle:] = right


def pieces_of(x):
    out = []
    for _ in range(3):
        piece = x.astype(jnp.bfloat16).astype(jnp.float32)
        out.append(piece)
        x = x - piece
    return out


PAIRS = ((0, 0), (0, 1), (1, 0), (0, 2), (1, 1), (2, 0))
DEPTH = 32


def geometry_kernel(around, near_ref, far_ref, own_ref, *refs):
    sources = refs[:around]
    left_out, right_out, near_hot, far_hot, side_ref, table_side = refs[-6:]
    frag_dev, near = near_ref.shape
    far = far_ref.shape[1]
    basis = own_ref.shape[2]
    lane = lax.broadcasted_iota(jnp.int32, (1, near_hot.shape[2]), 1)
    ones = jnp.ones((frag_dev, basis), jnp.float32)
    first_frag = (lax.axis_index("frag") - around // 2) * frag_dev

    def fill(target, first, place_ref, scale, extra, which):
        places = [place_ref[axis] for axis in range(3)]
        rows = []
        for place in places:
            parts = pieces_of(place)
            rows += [scale * parts[pair[which]] for pair in PAIRS]
        norm = places[0] * places[0] + places[1] * places[1] + places[2] * places[2] + extra
        sides = [pieces_of(norm), [ones] * 3]
        rows += sides[which] + sides[1 - which]
        rows += [0.0 * ones] * (DEPTH - len(rows))
        for at, row in enumerate(rows):
            for frag in range(frag_dev):
                target[first + frag, at : at + 1, :] = row[frag : frag + 1, :]

    fill(side_ref, 0, own_ref, -2.0, 1.0, 0)
    left_out[...] = side_ref[...].astype(jnp.bfloat16)
    for step in range(around):
        fill(table_side, step * frag_dev, sources[step], 1.0, 0.0, 1)
    for frag in range(frag_dev):
        for k in range(near):
            other = near_ref[frag, k]
            near_hot[frag, k : k + 1, :] = (lane == other).astype(jnp.float32)
            right_out[frag, k] = table_side[other - first_frag].astype(jnp.bfloat16)
        for m in range(far):
            far_hot[frag, m : m + 1, :] = (lane == far_ref[frag, m]).astype(jnp.float32)


def gather_kernel(tiles, *refs):
    chunks, density_ref, sems = refs[:tiles], refs[tiles], refs[tiles + 1]
    share = chunks[0].shape[0]
    copies = []
    for shift in range(tiles):
        target = density_ref.at[pl.ds(partner(shift, tiles, -1) * share, share)]
        copies.append(pltpu.make_async_copy(chunks[shift], target, sems.at[shift]))
        copies[-1].start()
    for copy in copies:
        copy.wait()


def potential_kernel(tiles, charge_ref, own_ref, left_ref, right_ref, near_hot, far_hot, over_ref, *refs):
    esp_ref, near_charge, far_block, esp_rows, sems = refs[1:]
    frag_dev, rows, basis = over_ref.shape
    share = frag_dev // tiles
    near, far = near_hot.shape[1], far_hot.shape[1]
    copies = []
    pick = own_rows(rows, basis, lax.axis_index("tile") * rows)
    table = charge_ref[...].reshape(-1, basis + LANES)
    for hot, gathered, part in (
        (near_hot, near_charge, table[:, :basis]),
        (far_hot, far_block, table[:, basis:]),
    ):
        every = hot[...].reshape(-1, hot.shape[2])
        picked = jnp.dot(every, part, precision=lax.Precision.HIGHEST, preferred_element_type=jnp.float32)
        gathered[...] = picked.reshape(gathered.shape)
    quantities = [block_lanes(at) for at in range(4)]
    for part in range(tiles):
        for frag in range(part * share, (part + 1) * share):
            folded = jnp.zeros((basis, 128), jnp.float32)
            for k in range(near):
                square = lax.dot_general(
                    left_ref[frag],
                    right_ref[frag, k],
                    (((0,), (0,)), ((), ())),
                    preferred_element_type=jnp.float32,
                )
                terms = lax.rsqrt(square) * near_charge[frag, k : k + 1, :]
                for start in range(0, basis, 128):
                    folded = folded + terms[:, start : start + 128]
            blocks = jnp.zeros((PC, basis), jnp.float32)
            spots = [own_ref[axis, frag : frag + 1, :] for axis in range(3)]
            for m in range(far):
                row = far_block[frag, m : m + 1, :]
                x, y, z, charge = [
                    jnp.sum(jnp.where(lanes, row, 0.0), axis=1, keepdims=True) for lanes in quantities
                ]
                total = (spots[0] - x) ** 2 + (spots[1] - y) ** 2 + (spots[2] - z) ** 2
                blocks = blocks + charge * lax.rsqrt(total + 1.0)
            potential = jnp.sum(folded.T, axis=0, keepdims=True) + jnp.sum(blocks, axis=0, keepdims=True)
            potential = (0.5 * SCREENING) * potential
            mine = jnp.sum(jnp.where(pick, potential, 0.0), axis=1, keepdims=True)
            esp_rows[frag] = over_ref[frag] * (mine + potential)
        span = pl.ds(part * share, share)
        copies.append(pltpu.make_async_copy(esp_rows.at[span], esp_ref.at[span], sems.at[part]))
        copies[-1].start()
    for copy in copies:
        copy.wait()


def call(kernel, outs, inputs, specs, scratch=(), cost=None, out_spec=VMEM):
    return pl.pallas_call(
        kernel,
        out_shape=outs,
        in_specs=specs,
        out_specs=[out_spec] * len(outs),
        scratch_shapes=list(scratch),
        cost_estimate=cost,
        compiler_params=pltpu.CompilerParams(vmem_limit_bytes=24 * 1024 * 1024),
    )(*inputs)


def exchanged(chunks):
    tiles = lax.axis_size("tile")
    places = tiles // 2
    moved = [chunks[0]]
    for shift in range(1, tiles):
        pairs = []
        for tile in range(tiles):
            half = tile // places if shift < places else 1 - tile // places
            pairs.append((tile, half * places + (tile + shift) % places))
        moved.append(lax.ppermute(chunks[shift], "tile", pairs))
    return moved


def neighbours(x, axis, reach):
    peers = lax.axis_size(axis)
    found = []
    for step in range(-reach, reach + 1):
        pairs = [(i, i - step) for i in range(peers) if 0 <= i - step < peers]
        found.append(x if step == 0 else lax.ppermute(x, axis, pairs))
    return found


def per_device(
    core_fock,
    intersection,
    gamma_tile,
    charge_old,
    embed_old,
    core_pop,
    centres,
    frag_sizes,
    near_list,
    far_list,
):
    frag_dev, rows, basis = core_fock.shape
    tiles, peers = lax.axis_size("tile"), lax.axis_size("frag")
    devices, share = tiles * peers, frag_dev // tiles
    chunk = floats(share, rows, basis)
    places = jnp.transpose(centres, (1, 0, 2))
    inputs = (frag_sizes, charge_old, embed_old, core_pop, places, gamma_tile, intersection, core_fock)
    near_part = floats(2, share, rows, basis)
    far_part = floats(share, 2 * rows + 8, basis // 2)
    *sent, facts = call(
        functools.partial(half_fock_kernel, tiles),
        [near_part] * (tiles // 2) + [far_part] * (tiles // 2) + [floats(3 * share, basis)],
        [pltpu.with_memory_space_constraint(x, pltpu.HBM) for x in inputs],
        [HBM] * len(inputs),
        [pltpu.SMEM(frag_sizes.shape, jnp.int32)]
        + [pltpu.VMEM(x.shape, jnp.float32) for x in inputs[1:]]
        + [pltpu.SemaphoreType.DMA((len(inputs),))],
    )
    sent = exchanged(sent)
    sources = neighbours(places, "frag", -(-SPAN // frag_dev))
    sent, sources = lax.optimization_barrier((sent, sources))
    *pieces, charges = call(
        functools.partial(density_kernel, tiles),
        [chunk] * tiles + [floats(devices, share, basis + LANES)],
        (facts, *sent),
        [VMEM] * (1 + tiles),
        [pltpu.VMEM((share, basis, basis), jnp.float32)] * 2,
        pl.CostEstimate(flops=12 * ITERS * share * basis**3, bytes_accessed=0, transcendentals=0),
    )
    near, far, frags = near_list.shape[1], far_list.shape[1], peers * frag_dev
    parts = call(
        functools.partial(geometry_kernel, len(sources)),
        [
            jax.ShapeDtypeStruct((frag_dev, DEPTH, basis), jnp.bfloat16),
            jax.ShapeDtypeStruct((frag_dev, near, DEPTH, basis), jnp.bfloat16),
            floats(frag_dev, near, frags),
            floats(frag_dev, far, frags),
        ],
        (near_list, far_list, places, *sources, pieces[0]),
        [SMEM, SMEM] + [VMEM] * (1 + len(sources)) + [ANY],
        [
            pltpu.VMEM((frag_dev, DEPTH, basis), jnp.float32),
            pltpu.VMEM((len(sources) * frag_dev, DEPTH, basis), jnp.float32),
        ],
        pl.CostEstimate(flops=10**9, bytes_accessed=10**7, transcendentals=0),
    )
    moved = exchanged(pieces)
    charges = lax.all_to_all(charges, ("frag", "tile"), split_axis=0, concat_axis=0, tiled=True)
    (density,) = call(
        functools.partial(gather_kernel, tiles),
        [floats(frag_dev, rows, basis)],
        moved,
        [VMEM] * tiles,
        [pltpu.SemaphoreType.DMA((tiles,))],
        pl.CostEstimate(flops=10**11, bytes_accessed=10**7, transcendentals=0),
        HBM,
    )
    (esp_matrix,) = call(
        functools.partial(potential_kernel, tiles),
        [floats(frag_dev, rows, basis)],
        (charges, places, *parts, intersection, pltpu.with_memory_space_constraint(density, pltpu.HBM)),
        [VMEM] * 7 + [HBM],
        [
            pltpu.VMEM((frag_dev, near, basis), jnp.float32),
            pltpu.VMEM((frag_dev, far, LANES), jnp.float32),
            pltpu.VMEM((frag_dev, rows, basis), jnp.float32),
            pltpu.SemaphoreType.DMA((tiles,)),
        ],
        out_spec=HBM,
    )
    return (density, esp_matrix)


def solution(mesh):
    in_specs = (
        P("frag", "tile", None),
        P("frag", "tile", None),
        P("frag", "tile", None),
        P("frag", None),
        P("frag", None),
        P("frag", None),
        P("frag", None, None),
        P("frag"),
        P("frag", None),
        P("frag", None),
    )
    out_specs = (P("frag", "tile", None), P("frag", "tile", None))
    return jax.shard_map(
        per_device, mesh=mesh, in_specs=in_specs, out_specs=out_specs, check_vma=False
    )
```

```python
import functools

import jax
import jax.numpy as jnp
from jax import lax
from jax.experimental import pallas as pl
from jax.experimental.pallas import tpu as pltpu
from jax.sharding import PartitionSpec as P

PC = 8
ITERS = 12
SCREENING = 0.25
SPAN = 8
LANES = 128
CHUNK = 128
VMEM = pl.BlockSpec(memory_space=pltpu.VMEM)
SMEM = pl.BlockSpec(memory_space=pltpu.SMEM)
HBM = pl.BlockSpec(memory_space=pltpu.HBM)
ANY = pl.BlockSpec(memory_space=pl.ANY)


def floats(*shape):
    return jax.ShapeDtypeStruct(shape, jnp.float32)


def block_mask(basis):
    group = basis // PC
    block = lax.broadcasted_iota(jnp.int32, (PC, basis), 0)
    column = lax.broadcasted_iota(jnp.int32, (PC, basis), 1)
    return (column >= block * group) & (column < (block + 1) * group)


def block_lanes(at):
    block = lax.broadcasted_iota(jnp.int32, (PC, LANES), 0)
    lane = lax.broadcasted_iota(jnp.int32, (PC, LANES), 1)
    return lane == block + at * PC


def block_row(rows, first):
    mask = block_mask(rows[0].shape[1])
    total = jnp.zeros((PC, LANES), jnp.float32)
    for at, row in enumerate(rows):
        sums = jnp.sum(jnp.where(mask, row, 0.0), axis=1, keepdims=True)
        total = total + jnp.where(block_lanes(first + at), sums, 0.0)
    return jnp.sum(total, axis=0, keepdims=True)


def own_rows(rows, basis, first):
    row = lax.broadcasted_iota(jnp.int32, (rows, basis), 0)
    column = lax.broadcasted_iota(jnp.int32, (rows, basis), 1)
    return column == row + first


def seat(tiles):
    places = tiles // 2
    tile_at = lax.axis_index("tile")
    return tile_at // places, lax.rem(tile_at, places), places


def partner(shift, tiles, sign=1):
    half, place, places = seat(tiles)
    other = half if shift < places else 1 - half
    return other * places + lax.rem(place + places + sign * (shift % places), places)


def swapped(half, x):
    middle = x.shape[-1] // 2
    left, right = x[..., :middle], x[..., middle:]
    return jnp.where(half == 0, left, right), jnp.where(half == 0, right, left)


def half_fock_kernel(tiles, *refs):
    inputs, outs, buffers, sems = refs[:8], refs[8:-9], refs[-9:-1], refs[-1]
    copies = [
        pltpu.make_async_copy(source, buffer, sems.at[at])
        for at, (source, buffer) in enumerate(zip(inputs, buffers))
    ]
    for copy in copies:
        copy.start()
    for copy in copies:
        copy.wait()
    sizes_ref, charge_ref, embed_ref, pop_ref, place_ref, gamma_ref, over_ref, core_ref = buffers
    half, place_at, places = seat(tiles)
    frag_dev, rows, basis = core_ref.shape
    share, middle = frag_dev // tiles, basis // 2
    pick = own_rows(rows, basis, lax.axis_index("tile") * rows)
    pick_half = own_rows(rows, middle, place_at * rows)
    row = lax.broadcasted_iota(jnp.int32, (rows, middle), 0) + lax.axis_index("tile") * rows
    column = lax.broadcasted_iota(jnp.int32, (rows, middle), 1)
    mine, others = column + half * middle, column + (1 - half) * middle
    lane = lax.broadcasted_iota(jnp.int32, (1, basis), 1)
    for shift in range(tiles):
        target = partner(shift, tiles)
        for spot in range(share):
            frag = target * share + spot
            size = sizes_ref[frag]
            terms = gamma_ref[frag] * charge_ref[pl.ds(frag, 1), :]
            terms = terms + jnp.where(pick, embed_ref[pl.ds(frag, 1), :], 0.0)
            field = jnp.sum(terms, axis=1, keepdims=True)
            core, core_far = swapped(half, core_ref[frag])
            over, over_far = swapped(half, over_ref[frag])
            inside = (row < size) & (mine < size)
            core, over = jnp.where(inside, core, 0.0), jnp.where(inside, over, 0.0)
            out = outs[shift]
            if shift < places:
                inside = (row < size) & (others < size)
                over_far = jnp.where(inside, over_far, 0.0)
                out[0, spot, :, :middle] = 0.5 * (core + over * field)
                out[0, spot, :, middle:] = jnp.where(inside, core_far, 0.0) + over_far * (0.5 * field)
                out[1, spot, :, :middle] = over
                out[1, spot, :, middle:] = over_far
            else:
                out[spot, :rows] = jnp.where(mine >= row, core, over)
                field_row = jnp.sum(jnp.where(pick_half, field, 0.0), axis=0, keepdims=True)
                diagonal = jnp.sum(jnp.where(pick_half, over, 0.0), axis=0, keepdims=True)
                rest = jnp.zeros((out.shape[1] - rows - 2, middle), jnp.float32)
                out[spot, rows:] = jnp.concatenate([field_row, diagonal, rest], axis=0)
            if shift == 0:
                facts = outs[-1]
                idle = swapped(half, (lane >= size).astype(jnp.float32))
                facts[spot : spot + 1, :middle] = idle[0]
                facts[spot : spot + 1, middle:] = idle[1]
                facts[share + spot : share + spot + 1, :] = pop_ref[pl.ds(frag, 1), :]
                spots = [place_ref[axis, pl.ds(frag, 1), :] for axis in range(3)]
                means = block_row(spots, 0) * (PC / basis)
                facts[2 * share + spot : 2 * share + spot + 1, :LANES] = means


def split(x):
    high = x.astype(jnp.bfloat16)
    low = (x - high.astype(jnp.float32)).astype(jnp.bfloat16)
    return high, low


def product(left, right):
    lh, ll = left
    rh, rl = right
    dot = functools.partial(jnp.dot, preferred_element_type=jnp.float32)
    return dot(lh, rh) + (dot(lh, rl) + dot(ll, rh))


def density_kernel(tiles, facts_ref, *refs):
    places = tiles // 2
    near_parts, far_parts = refs[:places], refs[places:tiles]
    chunks, charge_ref = refs[tiles : 2 * tiles], refs[2 * tiles]
    x_ref, s_ref = refs[2 * tiles + 1 :]
    half, place_at, _ = seat(tiles)
    _, share, rows, basis = near_parts[0].shape
    middle = basis // 2
    for shift in range(places):
        source = lax.rem(place_at + places - shift, places) * rows
        span = pl.ds(pl.multiple_of(source, rows), rows)
        far_span = pl.ds(pl.multiple_of(source + middle, rows), rows)
        for spot in range(share):
            x_ref[spot, span, :] = near_parts[shift][0, spot]
            s_ref[spot, span, :] = near_parts[shift][1, spot]
            x_ref[spot, far_span, middle:] = far_parts[shift][spot, :rows]
    row = lax.broadcasted_iota(jnp.int32, (basis, basis), 0)
    column = lax.broadcasted_iota(jnp.int32, (basis, basis), 1)
    near, far = slice(0, middle), slice(middle, basis)
    for spot in range(share):
        extra = far_parts[0][spot, rows:]
        for part in far_parts[1:]:
            extra = extra + part[spot, rows:]
        field = extra[:1]
        corner, packed = x_ref[spot, near, near], x_ref[spot, far, far]
        turned = packed.T
        down, along = row[near, near], column[near, near]
        over = jnp.where(along < down, packed, jnp.where(along == down, extra[1:2], turned))
        last = 0.5 * (jnp.where(along >= down, packed, turned) + over * field)
        s_ref[spot, far, far] = over
        side = x_ref[spot, near, far] + s_ref[spot, near, far] * (0.5 * field)
        corner, last = corner + corner.T, last + last.T
        total = corner * corner + last * last + 2.0 * (side * side)
        scale = 1.0 / jnp.sqrt(jnp.sum(total, keepdims=True) + 1e-06)
        idle = jnp.where(row == column, facts_ref[spot : spot + 1, :], 0.0)
        x_ref[spot, near, near] = corner * scale + idle[near, near]
        x_ref[spot, near, far] = side * scale
        x_ref[spot, far, near] = side.T * scale
        x_ref[spot, far, far] = last * scale + idle[far, far]

    chunk = min(CHUNK, basis)
    spans = [(spot, slice(at, at + chunk)) for spot in range(share) for at in range(0, basis, chunk)]
    for _ in range(ITERS):
        estimates = [x_ref[spot] for spot in range(share)]
        parts = [split(x) for x in estimates]
        squares = []
        for spot, span in spans:
            left = [part[span] for part in parts[spot]]
            squares.append(split(0.5 * product(left, parts[spot])))
        for square, (spot, span) in zip(squares, spans):
            x_ref[spot, span] = 1.5 * estimates[spot][span] - product(square, parts[spot])

    for spot in range(share):
        density = jnp.where(row == column, 0.5, 0.0) - 0.5 * x_ref[spot]
        x_ref[spot] = density
        side = density[near, far] * s_ref[spot, near, far]
        corner = density[near, near] * s_ref[spot, near, near] + side.T
        last = density[far, far] * s_ref[spot, far, far] + side
        sums = [jnp.sum(block, axis=0, keepdims=True) for block in (corner, last)]
        charge = jnp.concatenate(swapped(half, jnp.concatenate(sums, axis=1)), axis=1)
        charge = charge - facts_ref[share + spot : share + spot + 1, :]
        blocks = block_row([charge], 3) + facts_ref[2 * share + spot : 2 * share + spot + 1, :LANES]
        whole = jnp.concatenate([charge, blocks], axis=1)
        charge_ref[:, spot : spot + 1, :] = jnp.broadcast_to(whole[None], (charge_ref.shape[0],) + whole.shape)
    for shift in range(tiles):
        first = partner(shift, tiles) % places * rows + (0 if shift < places else middle)
        span = pl.ds(pl.multiple_of(first, rows), rows)
        for spot in range(share):
            left, right = swapped(half, x_ref[spot, span, :])
            chunks[shift][spot, :, :middle] = left
            chunks[shift][spot, :, middle:] = right


def pieces_of(x):
    out = []
    for _ in range(3):
        piece = x.astype(jnp.bfloat16).astype(jnp.float32)
        out.append(piece)
        x = x - piece
    return out


PAIRS = ((0, 0), (0, 1), (1, 0), (0, 2), (1, 1), (2, 0))
DEPTH = 32


def geometry_kernel(around, near_ref, far_ref, own_ref, *refs):
    sources = refs[:around]
    left_out, right_out, near_hot, far_hot, side_ref, table_side = refs[-6:]
    frag_dev, near = near_ref.shape
    far = far_ref.shape[1]
    basis = own_ref.shape[2]
    lane = lax.broadcasted_iota(jnp.int32, (1, near_hot.shape[2]), 1)
    ones = jnp.ones((frag_dev, basis), jnp.float32)
    frag_at, reach = lax.axis_index("frag"), around // 2
    first_frag = (frag_at - reach) * frag_dev

    def fill(target, first, place_ref, scale, extra, which):
        places = [place_ref[axis] for axis in range(3)]
        rows = []
        for place in places:
            parts = pieces_of(place)
            rows += [scale * parts[pair[which]] for pair in PAIRS]
        norm = places[0] * places[0] + places[1] * places[1] + places[2] * places[2] + extra
        sides = [pieces_of(norm), [ones] * 3]
        rows += sides[which] + sides[1 - which]
        rows += [0.0 * ones] * (DEPTH - len(rows))
        for at, row in enumerate(rows):
            for frag in range(frag_dev):
                target[first + frag, at : at + 1, :] = row[frag : frag + 1, :]

    fill(side_ref, 0, own_ref, -2.0, 1.0, 0)
    left_out[...] = side_ref[...].astype(jnp.bfloat16)
    fill(table_side, reach * frag_dev, sources[0], 1.0, 0.0, 1)
    for at in range(1, around):
        step = (at + 1) // 2
        side = lax.rem(frag_at // step + at + 1, 2)
        spot = reach + step * (1 - 2 * side)
        fill(table_side, spot * frag_dev, sources[at], 1.0, 0.0, 1)
    for frag in range(frag_dev):
        for k in range(near):
            other = near_ref[frag, k]
            near_hot[frag, k : k + 1, :] = (lane == other).astype(jnp.float32)
            right_out[frag, k] = table_side[other - first_frag].astype(jnp.bfloat16)
        for m in range(far):
            far_hot[frag, m : m + 1, :] = (lane == far_ref[frag, m]).astype(jnp.float32)


def gather_kernel(tiles, *refs):
    chunks, (density_ref, sems) = refs[:tiles], refs[tiles + 1 :]
    share = chunks[0].shape[0]
    copies = []
    for shift in range(tiles):
        target = density_ref.at[pl.ds(partner(shift, tiles, -1) * share, share)]
        copies.append(pltpu.make_async_copy(chunks[shift], target, sems.at[shift]))
        copies[-1].start()
    for copy in copies:
        copy.wait()


def potential_kernel(tiles, charge_ref, own_ref, left_ref, right_ref, near_hot, far_hot, over_ref, *refs):
    esp_ref, near_charge, far_block, esp_rows, sems = refs
    frag_dev, rows, basis = over_ref.shape
    share = frag_dev // tiles
    near, far = near_hot.shape[1], far_hot.shape[1]
    copies = []
    pick = own_rows(rows, basis, lax.axis_index("tile") * rows)
    table = charge_ref[...].reshape(-1, basis + LANES)
    for hot, gathered, part in (
        (near_hot, near_charge, table[:, :basis]),
        (far_hot, far_block, table[:, basis:]),
    ):
        every = hot[...].reshape(-1, hot.shape[2])
        picked = jnp.dot(every, part, precision=lax.Precision.HIGHEST, preferred_element_type=jnp.float32)
        gathered[...] = picked.reshape(gathered.shape)
    quantities = [block_lanes(at) for at in range(4)]
    for part in range(tiles):
        for frag in range(part * share, (part + 1) * share):
            folded = jnp.zeros((basis, 128), jnp.float32)
            for k in range(near):
                square = lax.dot_general(
                    left_ref[frag],
                    right_ref[frag, k],
                    (((0,), (0,)), ((), ())),
                    preferred_element_type=jnp.float32,
                )
                terms = lax.rsqrt(square) * near_charge[frag, k : k + 1, :]
                for start in range(0, basis, 128):
                    folded = folded + terms[:, start : start + 128]
            blocks = jnp.zeros((PC, basis), jnp.float32)
            spots = [own_ref[axis, frag : frag + 1, :] for axis in range(3)]
            for m in range(far):
                row = far_block[frag, m : m + 1, :]
                x, y, z, charge = [
                    jnp.sum(jnp.where(lanes, row, 0.0), axis=1, keepdims=True) for lanes in quantities
                ]
                total = (spots[0] - x) ** 2 + (spots[1] - y) ** 2 + (spots[2] - z) ** 2
                blocks = blocks + charge * lax.rsqrt(total + 1.0)
            potential = jnp.sum(folded.T, axis=0, keepdims=True) + jnp.sum(blocks, axis=0, keepdims=True)
            potential = (0.5 * SCREENING) * potential
            mine = jnp.sum(jnp.where(pick, potential, 0.0), axis=1, keepdims=True)
            esp_rows[frag] = over_ref[frag] * (mine + potential)
        span = pl.ds(part * share, share)
        copies.append(pltpu.make_async_copy(esp_rows.at[span], esp_ref.at[span], sems.at[part]))
        copies[-1].start()
    for copy in copies:
        copy.wait()


def call(kernel, outs, inputs, specs, scratch=(), cost=None, out_spec=VMEM):
    return pl.pallas_call(
        kernel,
        out_shape=outs,
        in_specs=specs,
        out_specs=[out_spec] * len(outs),
        scratch_shapes=list(scratch),
        cost_estimate=cost,
        compiler_params=pltpu.CompilerParams(vmem_limit_bytes=24 * 1024 * 1024),
    )(*inputs)


def exchanged(chunks):
    tiles = lax.axis_size("tile")
    places = tiles // 2
    moved = [chunks[0]]
    for shift in range(1, tiles):
        pairs = []
        for tile in range(tiles):
            half = tile // places if shift < places else 1 - tile // places
            pairs.append((tile, half * places + (tile + shift) % places))
        moved.append(lax.ppermute(chunks[shift], "tile", pairs))
    return moved


def neighbours(x, axis, reach):
    peers = lax.axis_size(axis)
    found = [x]
    for step in range(1, reach + 1):
        for parity in range(2):
            ups = [(i, i + step) for i in range(peers - step) if (i // step) % 2 == parity]
            found.append(lax.ppermute(x, axis, ups + [(j, i) for i, j in ups]))
    return found


def per_device(
    core_fock,
    intersection,
    gamma_tile,
    charge_old,
    embed_old,
    core_pop,
    centres,
    frag_sizes,
    near_list,
    far_list,
):
    frag_dev, rows, basis = core_fock.shape
    tiles, peers = lax.axis_size("tile"), lax.axis_size("frag")
    devices, share = tiles * peers, frag_dev // tiles
    chunk = floats(share, rows, basis)
    places = jnp.transpose(centres, (1, 0, 2))
    inputs = (frag_sizes, charge_old, embed_old, core_pop, places, gamma_tile, intersection, core_fock)
    near_part = floats(2, share, rows, basis)
    far_part = floats(share, rows + 8, basis // 2)
    *sent, facts = call(
        functools.partial(half_fock_kernel, tiles),
        [near_part] * (tiles // 2) + [far_part] * (tiles // 2) + [floats(3 * share, basis)],
        [pltpu.with_memory_space_constraint(x, pltpu.HBM) for x in inputs],
        [HBM] * len(inputs),
        [pltpu.SMEM(frag_sizes.shape, jnp.int32)]
        + [pltpu.VMEM(x.shape, jnp.float32) for x in inputs[1:]]
        + [pltpu.SemaphoreType.DMA((len(inputs),))],
    )
    sent = exchanged(sent)
    sources = neighbours(places, "frag", -(-SPAN // frag_dev))
    *pieces, charges = call(
        functools.partial(density_kernel, tiles),
        [chunk] * tiles + [floats(devices, share, basis + LANES)],
        (facts, *sent),
        [VMEM] * (1 + tiles),
        [pltpu.VMEM((share, basis, basis), jnp.float32)] * 2,
        pl.CostEstimate(flops=0, bytes_accessed=0, transcendentals=0),
    )
    moved = exchanged(pieces)
    charges, sources = lax.optimization_barrier((charges, sources))
    charges = lax.all_to_all(charges, ("frag", "tile"), split_axis=0, concat_axis=0, tiled=True)
    near, far, frags = near_list.shape[1], far_list.shape[1], peers * frag_dev
    parts = call(
        functools.partial(geometry_kernel, len(sources)),
        [
            jax.ShapeDtypeStruct((frag_dev, DEPTH, basis), jnp.bfloat16),
            jax.ShapeDtypeStruct((frag_dev, near, DEPTH, basis), jnp.bfloat16),
            floats(frag_dev, near, frags),
            floats(frag_dev, far, frags),
        ],
        (near_list, far_list, places, *sources, pieces[0]),
        [SMEM, SMEM] + [VMEM] * (1 + len(sources)) + [ANY],
        [
            pltpu.VMEM((frag_dev, DEPTH, basis), jnp.float32),
            pltpu.VMEM((len(sources) * frag_dev, DEPTH, basis), jnp.float32),
        ],
        pl.CostEstimate(flops=0, bytes_accessed=0, transcendentals=0),
    )
    (esp_matrix,) = call(
        functools.partial(potential_kernel, tiles),
        [floats(frag_dev, rows, basis)],
        (charges, places, *parts, intersection),
        [VMEM] * 7,
        [
            pltpu.VMEM((frag_dev, near, basis), jnp.float32),
            pltpu.VMEM((frag_dev, far, LANES), jnp.float32),
            pltpu.VMEM((frag_dev, rows, basis), jnp.float32),
            pltpu.SemaphoreType.DMA((tiles,)),
        ],
        pl.CostEstimate(flops=0, bytes_accessed=0, transcendentals=0),
        HBM,
    )
    (density,) = call(
        functools.partial(gather_kernel, tiles),
        [floats(frag_dev, rows, basis)],
        (*moved, pltpu.with_memory_space_constraint(esp_matrix, pltpu.HBM)),
        [VMEM] * tiles + [HBM],
        [pltpu.SemaphoreType.DMA((tiles,))],
        pl.CostEstimate(flops=0, bytes_accessed=0, transcendentals=0),
        HBM,
    )
    return (density, esp_matrix)


def solution(mesh):
    in_specs = (
        P("frag", "tile", None),
        P("frag", "tile", None),
        P("frag", "tile", None),
        P("frag", None),
        P("frag", None),
        P("frag", None),
        P("frag", None, None),
        P("frag"),
        P("frag", None),
        P("frag", None),
    )
    out_specs = (P("frag", "tile", None), P("frag", "tile", None))
    return jax.shard_map(
        per_device, mesh=mesh, in_specs=in_specs, out_specs=out_specs, check_vma=False
    )
```

```python
import functools

import jax
import jax.numpy as jnp
from jax import lax
from jax.experimental import pallas as pl
from jax.experimental.pallas import tpu as pltpu
from jax.sharding import PartitionSpec as P

PC = 8
ITERS = 12
SCREENING = 0.25
SPAN = 8
LANES = 128
CHUNK = 128
COARSE = jnp.float8_e4m3fn
WHOLE_SCALE = 256.0
REST_SCALE = 65536.0
VMEM = pl.BlockSpec(memory_space=pltpu.VMEM)
SMEM = pl.BlockSpec(memory_space=pltpu.SMEM)
HBM = pl.BlockSpec(memory_space=pltpu.HBM)
ANY = pl.BlockSpec(memory_space=pl.ANY)


def floats(*shape):
    return jax.ShapeDtypeStruct(shape, jnp.float32)


def block_mask(basis):
    group = basis // PC
    block = lax.broadcasted_iota(jnp.int32, (PC, basis), 0)
    column = lax.broadcasted_iota(jnp.int32, (PC, basis), 1)
    return (column >= block * group) & (column < (block + 1) * group)


def block_lanes(at):
    block = lax.broadcasted_iota(jnp.int32, (PC, LANES), 0)
    lane = lax.broadcasted_iota(jnp.int32, (PC, LANES), 1)
    return lane == block + at * PC


def block_row(rows, first):
    mask = block_mask(rows[0].shape[1])
    total = jnp.zeros((PC, LANES), jnp.float32)
    for at, row in enumerate(rows):
        sums = jnp.sum(jnp.where(mask, row, 0.0), axis=1, keepdims=True)
        total = total + jnp.where(block_lanes(first + at), sums, 0.0)
    return jnp.sum(total, axis=0, keepdims=True)


def own_rows(rows, basis, first):
    row = lax.broadcasted_iota(jnp.int32, (rows, basis), 0)
    column = lax.broadcasted_iota(jnp.int32, (rows, basis), 1)
    return column == row + first


def seat(tiles):
    places = tiles // 2
    tile_at = lax.axis_index("tile")
    return tile_at // places, lax.rem(tile_at, places), places


def partner(shift, tiles, sign=1):
    half, place, places = seat(tiles)
    other = half if shift < places else 1 - half
    return other * places + lax.rem(place + places + sign * (shift % places), places)


def swapped(half, x):
    middle = x.shape[-1] // 2
    left, right = x[..., :middle], x[..., middle:]
    return jnp.where(half == 0, left, right), jnp.where(half == 0, right, left)


def half_fock_kernel(tiles, *refs):
    inputs, outs, buffers, sems = refs[:8], refs[8:-9], refs[-9:-1], refs[-1]
    copies = [
        pltpu.make_async_copy(source, buffer, sems.at[at])
        for at, (source, buffer) in enumerate(zip(inputs, buffers))
    ]
    for copy in copies:
        copy.start()
    for copy in copies:
        copy.wait()
    sizes_ref, charge_ref, embed_ref, pop_ref, place_ref, gamma_ref, over_ref, core_ref = buffers
    half, place_at, places = seat(tiles)
    frag_dev, rows, basis = core_ref.shape
    share, middle = frag_dev // tiles, basis // 2
    pick = own_rows(rows, basis, lax.axis_index("tile") * rows)
    pick_half = own_rows(rows, middle, place_at * rows)
    row = lax.broadcasted_iota(jnp.int32, (rows, middle), 0) + lax.axis_index("tile") * rows
    column = lax.broadcasted_iota(jnp.int32, (rows, middle), 1)
    mine, others = column + half * middle, column + (1 - half) * middle
    lane = lax.broadcasted_iota(jnp.int32, (1, basis), 1)
    for shift in range(tiles):
        target = partner(shift, tiles)
        for spot in range(share):
            frag = target * share + spot
            size = sizes_ref[frag]
            terms = gamma_ref[frag] * charge_ref[pl.ds(frag, 1), :]
            terms = terms + jnp.where(pick, embed_ref[pl.ds(frag, 1), :], 0.0)
            field = jnp.sum(terms, axis=1, keepdims=True)
            core, core_far = swapped(half, core_ref[frag])
            over, over_far = swapped(half, over_ref[frag])
            inside = (row < size) & (mine < size)
            core, over = jnp.where(inside, core, 0.0), jnp.where(inside, over, 0.0)
            out = outs[shift]
            if shift < places:
                inside = (row < size) & (others < size)
                over_far = jnp.where(inside, over_far, 0.0)
                out[0, spot, :, :middle] = 0.5 * (core + over * field)
                out[0, spot, :, middle:] = jnp.where(inside, core_far, 0.0) + over_far * (0.5 * field)
                out[1, spot, :, :middle] = over
                out[1, spot, :, middle:] = over_far
            else:
                out[spot, :rows] = jnp.where(mine >= row, core, over)
                field_row = jnp.sum(jnp.where(pick_half, field, 0.0), axis=0, keepdims=True)
                diagonal = jnp.sum(jnp.where(pick_half, over, 0.0), axis=0, keepdims=True)
                rest = jnp.zeros((out.shape[1] - rows - 2, middle), jnp.float32)
                out[spot, rows:] = jnp.concatenate([field_row, diagonal, rest], axis=0)
            if shift == 0:
                facts = outs[-1]
                idle = swapped(half, (lane >= size).astype(jnp.float32))
                facts[spot : spot + 1, :middle] = idle[0]
                facts[spot : spot + 1, middle:] = idle[1]
                facts[share + spot : share + spot + 1, :] = pop_ref[pl.ds(frag, 1), :]
                spots = [place_ref[axis, pl.ds(frag, 1), :] for axis in range(3)]
                means = block_row(spots, 0) * (PC / basis)
                facts[2 * share + spot : 2 * share + spot + 1, :LANES] = means


def split(x):
    high = x.astype(jnp.bfloat16)
    low = x - high.astype(jnp.float32)
    return high, (x * WHOLE_SCALE).astype(COARSE), (low * REST_SCALE).astype(COARSE)


def product(left, right):
    dot = functools.partial(jnp.dot, preferred_element_type=jnp.float32)
    rest = dot(left[1], right[2]) + dot(left[2], right[1])
    return dot(left[0], right[0]) + rest * (1.0 / (WHOLE_SCALE * REST_SCALE))


def density_kernel(tiles, facts_ref, *refs):
    places = tiles // 2
    near_parts, far_parts = refs[:places], refs[places:tiles]
    chunks, charge_ref = refs[tiles : 2 * tiles], refs[2 * tiles]
    x_ref, s_ref = refs[2 * tiles + 1 :]
    half, place_at, _ = seat(tiles)
    _, share, rows, basis = near_parts[0].shape
    middle = basis // 2
    for shift in range(places):
        source = lax.rem(place_at + places - shift, places) * rows
        span = pl.ds(pl.multiple_of(source, rows), rows)
        far_span = pl.ds(pl.multiple_of(source + middle, rows), rows)
        for spot in range(share):
            x_ref[spot, span, :] = near_parts[shift][0, spot]
            s_ref[spot, span, :] = near_parts[shift][1, spot]
            x_ref[spot, far_span, middle:] = far_parts[shift][spot, :rows]
    row = lax.broadcasted_iota(jnp.int32, (basis, basis), 0)
    column = lax.broadcasted_iota(jnp.int32, (basis, basis), 1)
    near, far = slice(0, middle), slice(middle, basis)
    for spot in range(share):
        extra = far_parts[0][spot, rows:]
        for part in far_parts[1:]:
            extra = extra + part[spot, rows:]
        field = extra[:1]
        corner, packed = x_ref[spot, near, near], x_ref[spot, far, far]
        turned = packed.T
        down, along = row[near, near], column[near, near]
        over = jnp.where(along < down, packed, jnp.where(along == down, extra[1:2], turned))
        last = 0.5 * (jnp.where(along >= down, packed, turned) + over * field)
        s_ref[spot, far, far] = over
        side = x_ref[spot, near, far] + s_ref[spot, near, far] * (0.5 * field)
        corner, last = corner + corner.T, last + last.T
        total = corner * corner + last * last + 2.0 * (side * side)
        scale = 1.0 / jnp.sqrt(jnp.sum(total, keepdims=True) + 1e-06)
        idle = jnp.where(row == column, facts_ref[spot : spot + 1, :], 0.0)
        x_ref[spot, near, near] = corner * scale + idle[near, near]
        x_ref[spot, near, far] = side * scale
        x_ref[spot, far, near] = side.T * scale
        x_ref[spot, far, far] = last * scale + idle[far, far]

    chunk = min(CHUNK, basis)
    spans = [(spot, slice(at, at + chunk)) for spot in range(share) for at in range(0, basis, chunk)]
    for _ in range(ITERS):
        estimates = [x_ref[spot] for spot in range(share)]
        parts = [split(x) for x in estimates]
        squares = []
        for spot, span in spans:
            left = [part[span] for part in parts[spot]]
            squares.append(split(0.5 * product(left, parts[spot])))
        for square, (spot, span) in zip(squares, spans):
            x_ref[spot, span] = 1.5 * estimates[spot][span] - product(square, parts[spot])

    for spot in range(share):
        density = jnp.where(row == column, 0.5, 0.0) - 0.5 * x_ref[spot]
        x_ref[spot] = density
        side = density[near, far] * s_ref[spot, near, far]
        corner = density[near, near] * s_ref[spot, near, near] + side.T
        last = density[far, far] * s_ref[spot, far, far] + side
        sums = [jnp.sum(block, axis=0, keepdims=True) for block in (corner, last)]
        charge = jnp.concatenate(swapped(half, jnp.concatenate(sums, axis=1)), axis=1)
        charge = charge - facts_ref[share + spot : share + spot + 1, :]
        blocks = block_row([charge], 3) + facts_ref[2 * share + spot : 2 * share + spot + 1, :LANES]
        whole = jnp.concatenate([charge, blocks], axis=1)
        charge_ref[:, spot : spot + 1, :] = jnp.broadcast_to(whole[None], (charge_ref.shape[0],) + whole.shape)
    for shift in range(tiles):
        first = partner(shift, tiles) % places * rows + (0 if shift < places else middle)
        span = pl.ds(pl.multiple_of(first, rows), rows)
        for spot in range(share):
            left, right = swapped(half, x_ref[spot, span, :])
            chunks[shift][spot, :, :middle] = left
            chunks[shift][spot, :, middle:] = right


def pieces_of(x):
    out = []
    for _ in range(3):
        piece = x.astype(jnp.bfloat16).astype(jnp.float32)
        out.append(piece)
        x = x - piece
    return out


PAIRS = ((0, 0), (0, 1), (1, 0), (0, 2), (1, 1), (2, 0))
DEPTH = 32


def geometry_kernel(around, near_ref, far_ref, own_ref, *refs):
    sources = refs[:around]
    left_out, right_out, near_hot, far_hot, side_ref, table_side = refs[-6:]
    frag_dev, near = near_ref.shape
    far = far_ref.shape[1]
    basis = own_ref.shape[2]
    lane = lax.broadcasted_iota(jnp.int32, (1, near_hot.shape[2]), 1)
    ones = jnp.ones((frag_dev, basis), jnp.float32)
    frag_at, reach = lax.axis_index("frag"), around // 2
    first_frag = (frag_at - reach) * frag_dev

    def fill(target, first, place_ref, scale, extra, which):
        places = [place_ref[axis] for axis in range(3)]
        rows = []
        for place in places:
            parts = pieces_of(place)
            rows += [scale * parts[pair[which]] for pair in PAIRS]
        norm = places[0] * places[0] + places[1] * places[1] + places[2] * places[2] + extra
        sides = [pieces_of(norm), [ones] * 3]
        rows += sides[which] + sides[1 - which]
        rows += [0.0 * ones] * (DEPTH - len(rows))
        for at, row in enumerate(rows):
            for frag in range(frag_dev):
                target[first + frag, at : at + 1, :] = row[frag : frag + 1, :]

    fill(side_ref, 0, own_ref, -2.0, 1.0, 0)
    left_out[...] = side_ref[...].astype(jnp.bfloat16)
    fill(table_side, reach * frag_dev, sources[0], 1.0, 0.0, 1)
    for at in range(1, around):
        step = (at + 1) // 2
        side = lax.rem(frag_at // step + at + 1, 2)
        spot = reach + step * (1 - 2 * side)
        fill(table_side, spot * frag_dev, sources[at], 1.0, 0.0, 1)
    for frag in range(frag_dev):
        for k in range(near):
            other = near_ref[frag, k]
            near_hot[frag, k : k + 1, :] = (lane == other).astype(jnp.float32)
            right_out[frag, k] = table_side[other - first_frag].astype(jnp.bfloat16)
        for m in range(far):
            far_hot[frag, m : m + 1, :] = (lane == far_ref[frag, m]).astype(jnp.float32)


def esp_rows_of(first, count, charge_ref, own_ref, left_ref, right_ref, near_hot, far_hot, over_ref, near_charge, far_block):
    _, rows, basis = over_ref.shape
    near, far = near_hot.shape[1], far_hot.shape[1]
    pick = own_rows(rows, basis, lax.axis_index("tile") * rows)
    table = charge_ref[...].reshape(-1, basis + LANES)
    for hot, gathered, part in (
        (near_hot, near_charge, table[:, :basis]),
        (far_hot, far_block, table[:, basis:]),
    ):
        every = hot[first : first + count].reshape(-1, hot.shape[2])
        picked = jnp.dot(every, part, precision=lax.Precision.HIGHEST, preferred_element_type=jnp.float32)
        gathered[...] = picked.reshape(gathered.shape)
    quantities = [block_lanes(at) for at in range(4)]
    for at in range(count):
        frag = first + at
        folded = jnp.zeros((basis, LANES), jnp.float32)
        for k in range(near):
            square = lax.dot_general(
                left_ref[frag],
                right_ref[frag, k],
                (((0,), (0,)), ((), ())),
                preferred_element_type=jnp.float32,
            )
            terms = lax.rsqrt(square) * near_charge[at, k : k + 1, :]
            for start in range(0, basis, LANES):
                folded = folded + terms[:, start : start + LANES]
        blocks = jnp.zeros((PC, basis), jnp.float32)
        spots = [own_ref[axis, frag : frag + 1, :] for axis in range(3)]
        for m in range(far):
            row = far_block[at, m : m + 1, :]
            x, y, z, charge = [
                jnp.sum(jnp.where(lanes, row, 0.0), axis=1, keepdims=True) for lanes in quantities
            ]
            total = (spots[0] - x) ** 2 + (spots[1] - y) ** 2 + (spots[2] - z) ** 2
            blocks = blocks + charge * lax.rsqrt(total + 1.0)
        potential = jnp.sum(folded.T, axis=0, keepdims=True) + jnp.sum(blocks, axis=0, keepdims=True)
        potential = (0.5 * SCREENING) * potential
        mine = jnp.sum(jnp.where(pick, potential, 0.0), axis=1, keepdims=True)
        yield frag, over_ref[frag] * (mine + potential)


def first_esp_kernel(*refs):
    inputs, esp_ref, scratch = refs[:7], refs[7], refs[8:]
    for frag, rows in esp_rows_of(0, esp_ref.shape[0], *inputs, *scratch):
        esp_ref[frag] = rows


def last_esp_kernel(tiles, *refs):
    inputs, done_ref, chunks = refs[:7], refs[7], refs[8 : 8 + tiles]
    density_ref, esp_ref, rest_ref, near_charge, far_block, sems = refs[8 + tiles :]
    share, done = chunks[0].shape[0], done_ref.shape[0]
    copies = [pltpu.make_async_copy(done_ref, esp_ref.at[pl.ds(0, done)], sems.at[tiles])]
    for shift in range(tiles):
        target = density_ref.at[pl.ds(partner(shift, tiles, -1) * share, share)]
        copies.append(pltpu.make_async_copy(chunks[shift], target, sems.at[shift]))
    for copy in copies:
        copy.start()
    rest = rest_ref.shape[0]
    for frag, rows in esp_rows_of(done, rest, *inputs, near_charge, far_block):
        rest_ref[frag - done] = rows
    copies.append(pltpu.make_async_copy(rest_ref, esp_ref.at[pl.ds(done, rest)], sems.at[tiles + 1]))
    copies[-1].start()
    for copy in copies:
        copy.wait()


def call(kernel, outs, inputs, specs, scratch=(), cost=None, out_spec=VMEM):
    return pl.pallas_call(
        kernel,
        out_shape=outs,
        in_specs=specs,
        out_specs=[out_spec] * len(outs),
        scratch_shapes=list(scratch),
        cost_estimate=cost,
        compiler_params=pltpu.CompilerParams(vmem_limit_bytes=24 * 1024 * 1024),
    )(*inputs)


def exchanged(chunks):
    tiles = lax.axis_size("tile")
    places = tiles // 2
    moved = [chunks[0]]
    for shift in range(1, tiles):
        pairs = []
        for tile in range(tiles):
            half = tile // places if shift < places else 1 - tile // places
            pairs.append((tile, half * places + (tile + shift) % places))
        moved.append(lax.ppermute(chunks[shift], "tile", pairs))
    return moved


def neighbours(x, axis, reach):
    peers = lax.axis_size(axis)
    found = [x]
    for step in range(1, reach + 1):
        for parity in range(2):
            ups = [(i, i + step) for i in range(peers - step) if (i // step) % 2 == parity]
            found.append(lax.ppermute(x, axis, ups + [(j, i) for i, j in ups]))
    return found


def per_device(
    core_fock,
    intersection,
    gamma_tile,
    charge_old,
    embed_old,
    core_pop,
    centres,
    frag_sizes,
    near_list,
    far_list,
):
    frag_dev, rows, basis = core_fock.shape
    tiles, peers = lax.axis_size("tile"), lax.axis_size("frag")
    devices, share = tiles * peers, frag_dev // tiles
    chunk = floats(share, rows, basis)
    places = jnp.transpose(centres, (1, 0, 2))
    inputs = (frag_sizes, charge_old, embed_old, core_pop, places, gamma_tile, intersection, core_fock)
    near_part = floats(2, share, rows, basis)
    far_part = floats(share, rows + 8, basis // 2)
    *sent, facts = call(
        functools.partial(half_fock_kernel, tiles),
        [near_part] * (tiles // 2) + [far_part] * (tiles // 2) + [floats(3 * share, basis)],
        [pltpu.with_memory_space_constraint(x, pltpu.HBM) for x in inputs],
        [HBM] * len(inputs),
        [pltpu.SMEM(frag_sizes.shape, jnp.int32)]
        + [pltpu.VMEM(x.shape, jnp.float32) for x in inputs[1:]]
        + [pltpu.SemaphoreType.DMA((len(inputs),))],
    )
    sent = exchanged(sent)
    sources = neighbours(places, "frag", -(-SPAN // frag_dev))
    *pieces, charges = call(
        functools.partial(density_kernel, tiles),
        [chunk] * tiles + [floats(devices, share, basis + LANES)],
        (facts, *sent),
        [VMEM] * (1 + tiles),
        [pltpu.VMEM((share, basis, basis), jnp.float32)] * 2,
        pl.CostEstimate(flops=0, bytes_accessed=0, transcendentals=0),
    )
    moved = exchanged(pieces)
    charges, sources = lax.optimization_barrier((charges, sources))
    charges = lax.all_to_all(charges, ("frag", "tile"), split_axis=0, concat_axis=0, tiled=True)
    near, far, frags = near_list.shape[1], far_list.shape[1], peers * frag_dev
    parts = call(
        functools.partial(geometry_kernel, len(sources)),
        [
            jax.ShapeDtypeStruct((frag_dev, DEPTH, basis), jnp.bfloat16),
            jax.ShapeDtypeStruct((frag_dev, near, DEPTH, basis), jnp.bfloat16),
            floats(frag_dev, near, frags),
            floats(frag_dev, far, frags),
        ],
        (near_list, far_list, places, *sources, pieces[0]),
        [SMEM, SMEM] + [VMEM] * (1 + len(sources)) + [ANY],
        [
            pltpu.VMEM((frag_dev, DEPTH, basis), jnp.float32),
            pltpu.VMEM((len(sources) * frag_dev, DEPTH, basis), jnp.float32),
        ],
        pl.CostEstimate(flops=0, bytes_accessed=0, transcendentals=0),
    )
    inputs = (charges, places, *parts, intersection)
    done = frag_dev // 2
    rest = frag_dev - done
    (esp_rows,) = call(
        first_esp_kernel,
        [floats(done, rows, basis)],
        inputs,
        [VMEM] * 7,
        [pltpu.VMEM((done, near, basis), jnp.float32), pltpu.VMEM((done, far, LANES), jnp.float32)],
        pl.CostEstimate(flops=0, bytes_accessed=0, transcendentals=0),
    )
    density, esp_matrix = call(
        functools.partial(last_esp_kernel, tiles),
        [floats(frag_dev, rows, basis)] * 2,
        (*inputs, esp_rows, *moved),
        [VMEM] * (8 + tiles),
        [
            pltpu.VMEM((rest, rows, basis), jnp.float32),
            pltpu.VMEM((rest, near, basis), jnp.float32),
            pltpu.VMEM((rest, far, LANES), jnp.float32),
            pltpu.SemaphoreType.DMA((tiles + 2,)),
        ],
        pl.CostEstimate(flops=0, bytes_accessed=0, transcendentals=0),
        HBM,
    )
    return (density, esp_matrix)


def solution(mesh):
    in_specs = (
        P("frag", "tile", None),
        P("frag", "tile", None),
        P("frag", "tile", None),
        P("frag", None),
        P("frag", None),
        P("frag", None),
        P("frag", None, None),
        P("frag"),
        P("frag", None),
        P("frag", None),
    )
    out_specs = (P("frag", "tile", None), P("frag", "tile", None))
    return jax.shard_map(
        per_device, mesh=mesh, in_specs=in_specs, out_specs=out_specs, check_vma=False
    )
```

```python
import functools

import jax
import jax.numpy as jnp
from jax import lax
from jax.experimental import pallas as pl
from jax.experimental.pallas import tpu as pltpu
from jax.sharding import PartitionSpec as P

PC = 8
ITERS = 12
SCREENING = 0.25
SPAN = 8
LANES = 128
CHUNK = 128
COARSE = jnp.float8_e4m3fn
WHOLE_SCALE = 256.0
REST_SCALE = 65536.0
VMEM = pl.BlockSpec(memory_space=pltpu.VMEM)
SMEM = pl.BlockSpec(memory_space=pltpu.SMEM)
HBM = pl.BlockSpec(memory_space=pltpu.HBM)
ANY = pl.BlockSpec(memory_space=pl.ANY)


def floats(*shape):
    return jax.ShapeDtypeStruct(shape, jnp.float32)


def block_mask(basis):
    group = basis // PC
    block = lax.broadcasted_iota(jnp.int32, (PC, basis), 0)
    column = lax.broadcasted_iota(jnp.int32, (PC, basis), 1)
    return (column >= block * group) & (column < (block + 1) * group)


def block_lanes(at):
    block = lax.broadcasted_iota(jnp.int32, (PC, LANES), 0)
    lane = lax.broadcasted_iota(jnp.int32, (PC, LANES), 1)
    return lane == block + at * PC


def block_row(rows, first):
    mask = block_mask(rows[0].shape[1])
    total = jnp.zeros((PC, LANES), jnp.float32)
    for at, row in enumerate(rows):
        sums = jnp.sum(jnp.where(mask, row, 0.0), axis=1, keepdims=True)
        total = total + jnp.where(block_lanes(first + at), sums, 0.0)
    return jnp.sum(total, axis=0, keepdims=True)


def own_rows(rows, basis, first):
    row = lax.broadcasted_iota(jnp.int32, (rows, basis), 0)
    column = lax.broadcasted_iota(jnp.int32, (rows, basis), 1)
    return column == row + first


def seat(tiles):
    places = tiles // 2
    tile_at = lax.axis_index("tile")
    return tile_at // places, lax.rem(tile_at, places), places


def partner(shift, tiles, sign=1):
    half, place, places = seat(tiles)
    other = half if shift < places else 1 - half
    return other * places + lax.rem(place + places + sign * (shift % places), places)


def swapped(half, x):
    middle = x.shape[-1] // 2
    left, right = x[..., :middle], x[..., middle:]
    return jnp.where(half == 0, left, right), jnp.where(half == 0, right, left)


def half_fock_kernel(tiles, *refs):
    inputs, outs, buffers, sems = refs[:8], refs[8:-9], refs[-9:-1], refs[-1]
    copies = [
        pltpu.make_async_copy(source, buffer, sems.at[at])
        for at, (source, buffer) in enumerate(zip(inputs, buffers))
    ]
    for copy in copies:
        copy.start()
    for copy in copies:
        copy.wait()
    sizes_ref, charge_ref, embed_ref, pop_ref, place_ref, gamma_ref, over_ref, core_ref = buffers
    half, place_at, places = seat(tiles)
    frag_dev, rows, basis = core_ref.shape
    share, middle = frag_dev // tiles, basis // 2
    pick = own_rows(rows, basis, lax.axis_index("tile") * rows)
    pick_half = own_rows(rows, middle, place_at * rows)
    row = lax.broadcasted_iota(jnp.int32, (rows, middle), 0) + lax.axis_index("tile") * rows
    column = lax.broadcasted_iota(jnp.int32, (rows, middle), 1)
    mine, others = column + half * middle, column + (1 - half) * middle
    lane = lax.broadcasted_iota(jnp.int32, (1, basis), 1)
    for shift in range(tiles):
        target = partner(shift, tiles)
        for spot in range(share):
            frag = target * share + spot
            size = sizes_ref[frag]
            terms = gamma_ref[frag] * charge_ref[pl.ds(frag, 1), :]
            terms = terms + jnp.where(pick, embed_ref[pl.ds(frag, 1), :], 0.0)
            field = jnp.sum(terms, axis=1, keepdims=True)
            core, core_far = swapped(half, core_ref[frag])
            over, over_far = swapped(half, over_ref[frag])
            inside = (row < size) & (mine < size)
            core, over = jnp.where(inside, core, 0.0), jnp.where(inside, over, 0.0)
            out = outs[shift]
            if shift < places:
                inside = (row < size) & (others < size)
                over_far = jnp.where(inside, over_far, 0.0)
                out[0, spot, :, :middle] = 0.5 * (core + over * field)
                out[0, spot, :, middle:] = jnp.where(inside, core_far, 0.0) + over_far * (0.5 * field)
                out[1, spot, :, :middle] = over
                out[1, spot, :, middle:] = over_far
            else:
                out[spot, :rows] = jnp.where(mine >= row, core, over)
                field_row = jnp.sum(jnp.where(pick_half, field, 0.0), axis=0, keepdims=True)
                diagonal = jnp.sum(jnp.where(pick_half, over, 0.0), axis=0, keepdims=True)
                rest = jnp.zeros((out.shape[1] - rows - 2, middle), jnp.float32)
                out[spot, rows:] = jnp.concatenate([field_row, diagonal, rest], axis=0)
            if shift == 0:
                facts = outs[-1]
                idle = swapped(half, (lane >= size).astype(jnp.float32))
                facts[spot : spot + 1, :middle] = idle[0]
                facts[spot : spot + 1, middle:] = idle[1]
                facts[share + spot : share + spot + 1, :] = pop_ref[pl.ds(frag, 1), :]
                spots = [place_ref[axis, pl.ds(frag, 1), :] for axis in range(3)]
                means = block_row(spots, 0) * (PC / basis)
                facts[2 * share + spot : 2 * share + spot + 1, :LANES] = means


def split(x):
    high = x.astype(jnp.bfloat16)
    rest = (x - high.astype(jnp.float32)).astype(jnp.bfloat16)
    coarse = (high * jnp.bfloat16(WHOLE_SCALE)).astype(COARSE)
    return high, coarse, (rest * jnp.bfloat16(REST_SCALE)).astype(COARSE)


def product(left, right):
    dot = functools.partial(jnp.dot, preferred_element_type=jnp.float32)
    rest = dot(left[1], right[2]) + dot(left[2], right[1])
    return dot(left[0], right[0]) + rest * (1.0 / (WHOLE_SCALE * REST_SCALE))


def density_kernel(tiles, facts_ref, *refs):
    places = tiles // 2
    near_parts, far_parts = refs[:places], refs[places:tiles]
    chunks, charge_ref = refs[tiles : 2 * tiles], refs[2 * tiles]
    x_ref, s_ref = refs[2 * tiles + 1 :]
    half, place_at, _ = seat(tiles)
    _, share, rows, basis = near_parts[0].shape
    middle = basis // 2
    for shift in range(places):
        source = lax.rem(place_at + places - shift, places) * rows
        span = pl.ds(pl.multiple_of(source, rows), rows)
        far_span = pl.ds(pl.multiple_of(source + middle, rows), rows)
        for spot in range(share):
            x_ref[spot, span, :] = near_parts[shift][0, spot]
            s_ref[spot, span, :] = near_parts[shift][1, spot]
            x_ref[spot, far_span, middle:] = far_parts[shift][spot, :rows]
    row = lax.broadcasted_iota(jnp.int32, (basis, basis), 0)
    column = lax.broadcasted_iota(jnp.int32, (basis, basis), 1)
    near, far = slice(0, middle), slice(middle, basis)
    for spot in range(share):
        extra = far_parts[0][spot, rows:]
        for part in far_parts[1:]:
            extra = extra + part[spot, rows:]
        field = extra[:1]
        corner, packed = x_ref[spot, near, near], x_ref[spot, far, far]
        turned = packed.T
        down, along = row[near, near], column[near, near]
        over = jnp.where(along < down, packed, jnp.where(along == down, extra[1:2], turned))
        last = 0.5 * (jnp.where(along >= down, packed, turned) + over * field)
        s_ref[spot, far, far] = over
        side = x_ref[spot, near, far] + s_ref[spot, near, far] * (0.5 * field)
        corner, last = corner + corner.T, last + last.T
        total = corner * corner + last * last + 2.0 * (side * side)
        scale = 1.0 / jnp.sqrt(jnp.sum(total, keepdims=True) + 1e-06)
        idle = jnp.where(row == column, facts_ref[spot : spot + 1, :], 0.0)
        x_ref[spot, near, near] = corner * scale + idle[near, near]
        x_ref[spot, near, far] = side * scale
        x_ref[spot, far, near] = side.T * scale
        x_ref[spot, far, far] = last * scale + idle[far, far]

    chunk = min(CHUNK, basis)
    spans = [(spot, slice(at, at + chunk)) for spot in range(share) for at in range(0, basis, chunk)]
    for _ in range(ITERS):
        estimates = [x_ref[spot] for spot in range(share)]
        parts = [split(x) for x in estimates]
        squares = []
        for spot, span in spans:
            left = [part[span] for part in parts[spot]]
            squares.append(split(0.5 * product(left, parts[spot])))
        for square, (spot, span) in zip(squares, spans):
            x_ref[spot, span] = 1.5 * estimates[spot][span] - product(square, parts[spot])

    for spot in range(share):
        density = jnp.where(row == column, 0.5, 0.0) - 0.5 * x_ref[spot]
        x_ref[spot] = density
        side = density[near, far] * s_ref[spot, near, far]
        corner = density[near, near] * s_ref[spot, near, near] + side.T
        last = density[far, far] * s_ref[spot, far, far] + side
        sums = [jnp.sum(block, axis=0, keepdims=True) for block in (corner, last)]
        charge = jnp.concatenate(swapped(half, jnp.concatenate(sums, axis=1)), axis=1)
        charge = charge - facts_ref[share + spot : share + spot + 1, :]
        blocks = block_row([charge], 3) + facts_ref[2 * share + spot : 2 * share + spot + 1, :LANES]
        whole = jnp.concatenate([charge, blocks], axis=1)
        charge_ref[:, spot : spot + 1, :] = jnp.broadcast_to(whole[None], (charge_ref.shape[0],) + whole.shape)
    for shift in range(tiles):
        first = partner(shift, tiles) % places * rows + (0 if shift < places else middle)
        span = pl.ds(pl.multiple_of(first, rows), rows)
        for spot in range(share):
            left, right = swapped(half, x_ref[spot, span, :])
            chunks[shift][spot, :, :middle] = left
            chunks[shift][spot, :, middle:] = right


def pieces_of(x):
    out = []
    for _ in range(3):
        piece = x.astype(jnp.bfloat16).astype(jnp.float32)
        out.append(piece)
        x = x - piece
    return out


PAIRS = ((0, 0), (0, 1), (1, 0), (0, 2), (1, 1), (2, 0))
DEPTH = 32


def geometry_kernel(around, near_ref, far_ref, own_ref, *refs):
    sources = refs[:around]
    left_out, right_out, near_hot, far_hot, side_ref, table_side = refs[-6:]
    frag_dev, near = near_ref.shape
    far = far_ref.shape[1]
    basis = own_ref.shape[2]
    lane = lax.broadcasted_iota(jnp.int32, (1, near_hot.shape[2]), 1)
    ones = jnp.ones((frag_dev, basis), jnp.float32)
    frag_at, reach = lax.axis_index("frag"), around // 2
    first_frag = (frag_at - reach) * frag_dev

    def fill(target, first, place_ref, scale, extra, which):
        places = [place_ref[axis] for axis in range(3)]
        rows = []
        for place in places:
            parts = pieces_of(place)
            rows += [scale * parts[pair[which]] for pair in PAIRS]
        norm = places[0] * places[0] + places[1] * places[1] + places[2] * places[2] + extra
        sides = [pieces_of(norm), [ones] * 3]
        rows += sides[which] + sides[1 - which]
        rows += [0.0 * ones] * (DEPTH - len(rows))
        for at, row in enumerate(rows):
            for frag in range(frag_dev):
                target[first + frag, at : at + 1, :] = row[frag : frag + 1, :]

    fill(side_ref, 0, own_ref, -2.0, 1.0, 0)
    left_out[...] = side_ref[...].astype(jnp.bfloat16)
    fill(table_side, reach * frag_dev, sources[0], 1.0, 0.0, 1)
    for at in range(1, around):
        step = (at + 1) // 2
        side = lax.rem(frag_at // step + at + 1, 2)
        spot = reach + step * (1 - 2 * side)
        fill(table_side, spot * frag_dev, sources[at], 1.0, 0.0, 1)
    for frag in range(frag_dev):
        for k in range(near):
            other = near_ref[frag, k]
            near_hot[frag, k : k + 1, :] = (lane == other).astype(jnp.float32)
            right_out[frag, k] = table_side[other - first_frag].astype(jnp.bfloat16)
        for m in range(far):
            far_hot[frag, m : m + 1, :] = (lane == far_ref[frag, m]).astype(jnp.float32)


def esp_rows_of(first, count, charge_ref, own_ref, left_ref, right_ref, near_hot, far_hot, over_ref, near_charge, far_block):
    _, rows, basis = over_ref.shape
    near, far = near_hot.shape[1], far_hot.shape[1]
    pick = own_rows(rows, basis, lax.axis_index("tile") * rows)
    table = charge_ref[...].reshape(-1, basis + LANES)
    for hot, gathered, part in (
        (near_hot, near_charge, table[:, :basis]),
        (far_hot, far_block, table[:, basis:]),
    ):
        every = hot[first : first + count].reshape(-1, hot.shape[2])
        picked = jnp.dot(every, part, precision=lax.Precision.HIGHEST, preferred_element_type=jnp.float32)
        gathered[...] = picked.reshape(gathered.shape)
    quantities = [block_lanes(at) for at in range(4)]
    for at in range(count):
        frag = first + at
        folded = jnp.zeros((basis, LANES), jnp.float32)
        for k in range(near):
            square = lax.dot_general(
                left_ref[frag],
                right_ref[frag, k],
                (((0,), (0,)), ((), ())),
                preferred_element_type=jnp.float32,
            )
            terms = lax.rsqrt(square) * near_charge[at, k : k + 1, :]
            for start in range(0, basis, LANES):
                folded = folded + terms[:, start : start + LANES]
        blocks = jnp.zeros((PC, basis), jnp.float32)
        spots = [own_ref[axis, frag : frag + 1, :] for axis in range(3)]
        for m in range(far):
            row = far_block[at, m : m + 1, :]
            x, y, z, charge = [
                jnp.sum(jnp.where(lanes, row, 0.0), axis=1, keepdims=True) for lanes in quantities
            ]
            total = (spots[0] - x) ** 2 + (spots[1] - y) ** 2 + (spots[2] - z) ** 2
            blocks = blocks + charge * lax.rsqrt(total + 1.0)
        potential = jnp.sum(folded.T, axis=0, keepdims=True) + jnp.sum(blocks, axis=0, keepdims=True)
        potential = (0.5 * SCREENING) * potential
        mine = jnp.sum(jnp.where(pick, potential, 0.0), axis=1, keepdims=True)
        yield frag, over_ref[frag] * (mine + potential)


def first_esp_kernel(*refs):
    inputs, esp_ref, scratch = refs[:7], refs[7], refs[8:]
    for frag, rows in esp_rows_of(0, esp_ref.shape[0], *inputs, *scratch):
        esp_ref[frag] = rows


def last_esp_kernel(tiles, *refs):
    inputs, done_ref, chunks = refs[:7], refs[7], refs[8 : 8 + tiles]
    density_ref, esp_ref, rest_ref, near_charge, far_block, sems = refs[8 + tiles :]
    share, done = chunks[0].shape[0], done_ref.shape[0]
    copies = [pltpu.make_async_copy(done_ref, esp_ref.at[pl.ds(0, done)], sems.at[tiles])]
    for shift in range(tiles):
        target = density_ref.at[pl.ds(partner(shift, tiles, -1) * share, share)]
        copies.append(pltpu.make_async_copy(chunks[shift], target, sems.at[shift]))
    for copy in copies:
        copy.start()
    rest = rest_ref.shape[0]
    for frag, rows in esp_rows_of(done, rest, *inputs, near_charge, far_block):
        rest_ref[frag - done] = rows
    copies.append(pltpu.make_async_copy(rest_ref, esp_ref.at[pl.ds(done, rest)], sems.at[tiles + 1]))
    copies[-1].start()
    for copy in copies:
        copy.wait()


def call(kernel, outs, inputs, specs, scratch=(), cost=None, out_spec=VMEM):
    return pl.pallas_call(
        kernel,
        out_shape=outs,
        in_specs=specs,
        out_specs=[out_spec] * len(outs),
        scratch_shapes=list(scratch),
        cost_estimate=cost,
        compiler_params=pltpu.CompilerParams(vmem_limit_bytes=24 * 1024 * 1024),
    )(*inputs)


def exchanged(chunks):
    tiles = lax.axis_size("tile")
    places = tiles // 2
    moved = [chunks[0]]
    for shift in range(1, tiles):
        pairs = []
        for tile in range(tiles):
            half = tile // places if shift < places else 1 - tile // places
            pairs.append((tile, half * places + (tile + shift) % places))
        moved.append(lax.ppermute(chunks[shift], "tile", pairs))
    return moved


def neighbours(x, axis, reach):
    peers = lax.axis_size(axis)
    found = [x]
    for step in range(1, reach + 1):
        for parity in range(2):
            ups = [(i, i + step) for i in range(peers - step) if (i // step) % 2 == parity]
            found.append(lax.ppermute(x, axis, ups + [(j, i) for i, j in ups]))
    return found


def per_device(
    core_fock,
    intersection,
    gamma_tile,
    charge_old,
    embed_old,
    core_pop,
    centres,
    frag_sizes,
    near_list,
    far_list,
):
    frag_dev, rows, basis = core_fock.shape
    tiles, peers = lax.axis_size("tile"), lax.axis_size("frag")
    devices, share = tiles * peers, frag_dev // tiles
    chunk = floats(share, rows, basis)
    places = jnp.transpose(centres, (1, 0, 2))
    inputs = (frag_sizes, charge_old, embed_old, core_pop, places, gamma_tile, intersection, core_fock)
    near_part = floats(2, share, rows, basis)
    far_part = floats(share, rows + 8, basis // 2)
    *sent, facts = call(
        functools.partial(half_fock_kernel, tiles),
        [near_part] * (tiles // 2) + [far_part] * (tiles // 2) + [floats(3 * share, basis)],
        [pltpu.with_memory_space_constraint(x, pltpu.HBM) for x in inputs],
        [HBM] * len(inputs),
        [pltpu.SMEM(frag_sizes.shape, jnp.int32)]
        + [pltpu.VMEM(x.shape, jnp.float32) for x in inputs[1:]]
        + [pltpu.SemaphoreType.DMA((len(inputs),))],
    )
    sent = exchanged(sent)
    sources = neighbours(places, "frag", -(-SPAN // frag_dev))
    *pieces, charges = call(
        functools.partial(density_kernel, tiles),
        [chunk] * tiles + [floats(devices, share, basis + LANES)],
        (facts, *sent),
        [VMEM] * (1 + tiles),
        [pltpu.VMEM((share, basis, basis), jnp.float32)] * 2,
        pl.CostEstimate(flops=0, bytes_accessed=0, transcendentals=0),
    )
    moved = exchanged(pieces)
    charges, sources = lax.optimization_barrier((charges, sources))
    charges = lax.all_to_all(charges, ("frag", "tile"), split_axis=0, concat_axis=0, tiled=True)
    near, far, frags = near_list.shape[1], far_list.shape[1], peers * frag_dev
    parts = call(
        functools.partial(geometry_kernel, len(sources)),
        [
            jax.ShapeDtypeStruct((frag_dev, DEPTH, basis), jnp.bfloat16),
            jax.ShapeDtypeStruct((frag_dev, near, DEPTH, basis), jnp.bfloat16),
            floats(frag_dev, near, frags),
            floats(frag_dev, far, frags),
        ],
        (near_list, far_list, places, *sources, pieces[0]),
        [SMEM, SMEM] + [VMEM] * (1 + len(sources)) + [ANY],
        [
            pltpu.VMEM((frag_dev, DEPTH, basis), jnp.float32),
            pltpu.VMEM((len(sources) * frag_dev, DEPTH, basis), jnp.float32),
        ],
        pl.CostEstimate(flops=0, bytes_accessed=0, transcendentals=0),
    )
    inputs = (charges, places, *parts, intersection)
    done = frag_dev * 3 // 4
    rest = frag_dev - done
    (esp_rows,) = call(
        first_esp_kernel,
        [floats(done, rows, basis)],
        inputs,
        [VMEM] * 7,
        [pltpu.VMEM((done, near, basis), jnp.float32), pltpu.VMEM((done, far, LANES), jnp.float32)],
        pl.CostEstimate(flops=0, bytes_accessed=0, transcendentals=0),
    )
    density, esp_matrix = call(
        functools.partial(last_esp_kernel, tiles),
        [floats(frag_dev, rows, basis)] * 2,
        (*inputs, esp_rows, *moved),
        [VMEM] * (8 + tiles),
        [
            pltpu.VMEM((rest, rows, basis), jnp.float32),
            pltpu.VMEM((rest, near, basis), jnp.float32),
            pltpu.VMEM((rest, far, LANES), jnp.float32),
            pltpu.SemaphoreType.DMA((tiles + 2,)),
        ],
        pl.CostEstimate(flops=0, bytes_accessed=0, transcendentals=0),
        HBM,
    )
    return (density, esp_matrix)


def solution(mesh):
    in_specs = (
        P("frag", "tile", None),
        P("frag", "tile", None),
        P("frag", "tile", None),
        P("frag", None),
        P("frag", None),
        P("frag", None),
        P("frag", None, None),
        P("frag"),
        P("frag", None),
        P("frag", None),
    )
    out_specs = (P("frag", "tile", None), P("frag", "tile", None))
    return jax.shard_map(
        per_device, mesh=mesh, in_specs=in_specs, out_specs=out_specs, check_vma=False
    )
```

```python
import functools

import jax
import jax.numpy as jnp
from jax import lax
from jax.experimental import pallas as pl
from jax.experimental.pallas import tpu as pltpu
from jax.sharding import PartitionSpec as P

PC = 8
ITERS = 12
SCREENING = 0.25
SPAN = 8
LANES = 128
CHUNK = 128
COARSE = jnp.float8_e4m3fn
WHOLE_SCALE = 256.0
REST_SCALE = 65536.0
VMEM = pl.BlockSpec(memory_space=pltpu.VMEM)
SMEM = pl.BlockSpec(memory_space=pltpu.SMEM)
HBM = pl.BlockSpec(memory_space=pltpu.HBM)
ANY = pl.BlockSpec(memory_space=pl.ANY)


def floats(*shape):
    return jax.ShapeDtypeStruct(shape, jnp.float32)


def block_mask(basis):
    group = basis // PC
    block = lax.broadcasted_iota(jnp.int32, (PC, basis), 0)
    column = lax.broadcasted_iota(jnp.int32, (PC, basis), 1)
    return (column >= block * group) & (column < (block + 1) * group)


def block_lanes(at):
    block = lax.broadcasted_iota(jnp.int32, (PC, LANES), 0)
    lane = lax.broadcasted_iota(jnp.int32, (PC, LANES), 1)
    return lane == block + at * PC


def block_row(rows, first):
    mask = block_mask(rows[0].shape[1])
    total = jnp.zeros((PC, LANES), jnp.float32)
    for at, row in enumerate(rows):
        sums = jnp.sum(jnp.where(mask, row, 0.0), axis=1, keepdims=True)
        total = total + jnp.where(block_lanes(first + at), sums, 0.0)
    return jnp.sum(total, axis=0, keepdims=True)


def own_rows(rows, basis, first):
    row = lax.broadcasted_iota(jnp.int32, (rows, basis), 0)
    column = lax.broadcasted_iota(jnp.int32, (rows, basis), 1)
    return column == row + first


def seat(tiles):
    places = tiles // 2
    tile_at = lax.axis_index("tile")
    return tile_at // places, lax.rem(tile_at, places), places


def partner(shift, tiles, sign=1):
    half, place, places = seat(tiles)
    other = half if shift < places else 1 - half
    return other * places + lax.rem(place + places + sign * (shift % places), places)


def swapped(half, x):
    middle = x.shape[-1] // 2
    left, right = x[..., :middle], x[..., middle:]
    return jnp.where(half == 0, left, right), jnp.where(half == 0, right, left)


def half_fock_kernel(tiles, *refs):
    inputs, outs, buffers, sems = refs[:8], refs[8:-9], refs[-9:-1], refs[-1]
    copies = [
        pltpu.make_async_copy(source, buffer, sems.at[at])
        for at, (source, buffer) in enumerate(zip(inputs, buffers))
    ]
    for copy in copies:
        copy.start()
    for copy in copies:
        copy.wait()
    sizes_ref, charge_ref, embed_ref, pop_ref, place_ref, gamma_ref, over_ref, core_ref = buffers
    half, place_at, places = seat(tiles)
    frag_dev, rows, basis = core_ref.shape
    share, middle = frag_dev // tiles, basis // 2
    pick = own_rows(rows, basis, lax.axis_index("tile") * rows)
    pick_half = own_rows(rows, middle, place_at * rows)
    row = lax.broadcasted_iota(jnp.int32, (rows, middle), 0) + lax.axis_index("tile") * rows
    column = lax.broadcasted_iota(jnp.int32, (rows, middle), 1)
    mine, others = column + half * middle, column + (1 - half) * middle
    lane = lax.broadcasted_iota(jnp.int32, (1, basis), 1)
    for shift in range(tiles):
        target = partner(shift, tiles)
        for spot in range(share):
            frag = target * share + spot
            size = sizes_ref[frag]
            terms = gamma_ref[frag] * charge_ref[pl.ds(frag, 1), :]
            terms = terms + jnp.where(pick, embed_ref[pl.ds(frag, 1), :], 0.0)
            field = jnp.sum(terms, axis=1, keepdims=True)
            core, core_far = swapped(half, core_ref[frag])
            over, over_far = swapped(half, over_ref[frag])
            inside = (row < size) & (mine < size)
            core, over = jnp.where(inside, core, 0.0), jnp.where(inside, over, 0.0)
            out = outs[shift]
            if shift < places:
                inside = (row < size) & (others < size)
                over_far = jnp.where(inside, over_far, 0.0)
                out[0, spot, :, :middle] = 0.5 * (core + over * field)
                out[0, spot, :, middle:] = jnp.where(inside, core_far, 0.0) + over_far * (0.5 * field)
                out[1, spot, :, :middle] = over
                out[1, spot, :, middle:] = over_far
            else:
                out[spot, :rows] = jnp.where(mine >= row, core, over)
                field_row = jnp.sum(jnp.where(pick_half, field, 0.0), axis=0, keepdims=True)
                diagonal = jnp.sum(jnp.where(pick_half, over, 0.0), axis=0, keepdims=True)
                rest = jnp.zeros((out.shape[1] - rows - 2, middle), jnp.float32)
                out[spot, rows:] = jnp.concatenate([field_row, diagonal, rest], axis=0)
            if shift == 0:
                facts = outs[-1]
                idle = swapped(half, (lane >= size).astype(jnp.float32))
                facts[spot : spot + 1, :middle] = idle[0]
                facts[spot : spot + 1, middle:] = idle[1]
                facts[share + spot : share + spot + 1, :] = pop_ref[pl.ds(frag, 1), :]
                spots = [place_ref[axis, pl.ds(frag, 1), :] for axis in range(3)]
                means = block_row(spots, 0) * (PC / basis)
                facts[2 * share + spot : 2 * share + spot + 1, :LANES] = means


def split(x):
    high = x.astype(jnp.bfloat16)
    rest = (x - high.astype(jnp.float32)).astype(jnp.bfloat16)
    coarse = (high * jnp.bfloat16(WHOLE_SCALE)).astype(COARSE)
    return high, coarse, (rest * jnp.bfloat16(REST_SCALE)).astype(COARSE)


def product(left, right):
    dot = functools.partial(jnp.dot, preferred_element_type=jnp.float32)
    rest = dot(left[1], right[2]) + dot(left[2], right[1])
    return dot(left[0], right[0]) + rest * (1.0 / (WHOLE_SCALE * REST_SCALE))


def density_kernel(tiles, facts_ref, *refs):
    places = tiles // 2
    near_parts, far_parts = refs[:places], refs[places:tiles]
    chunks, charge_ref = refs[tiles : 2 * tiles], refs[2 * tiles]
    x_ref, s_ref = refs[2 * tiles + 1 :]
    half, place_at, _ = seat(tiles)
    _, share, rows, basis = near_parts[0].shape
    middle = basis // 2
    for shift in range(places):
        source = lax.rem(place_at + places - shift, places) * rows
        span = pl.ds(pl.multiple_of(source, rows), rows)
        far_span = pl.ds(pl.multiple_of(source + middle, rows), rows)
        for spot in range(share):
            x_ref[spot, span, :] = near_parts[shift][0, spot]
            s_ref[spot, span, :] = near_parts[shift][1, spot]
            x_ref[spot, far_span, middle:] = far_parts[shift][spot, :rows]
    row = lax.broadcasted_iota(jnp.int32, (basis, basis), 0)
    column = lax.broadcasted_iota(jnp.int32, (basis, basis), 1)
    near, far = slice(0, middle), slice(middle, basis)
    for spot in range(share):
        extra = far_parts[0][spot, rows:]
        for part in far_parts[1:]:
            extra = extra + part[spot, rows:]
        field = extra[:1]
        corner, packed = x_ref[spot, near, near], x_ref[spot, far, far]
        turned = packed.T
        down, along = row[near, near], column[near, near]
        over = jnp.where(along < down, packed, jnp.where(along == down, extra[1:2], turned))
        last = 0.5 * (jnp.where(along >= down, packed, turned) + over * field)
        s_ref[spot, far, far] = over
        side = x_ref[spot, near, far] + s_ref[spot, near, far] * (0.5 * field)
        corner, last = corner + corner.T, last + last.T
        total = corner * corner + last * last + 2.0 * (side * side)
        scale = 1.0 / jnp.sqrt(jnp.sum(total, keepdims=True) + 1e-06)
        idle = jnp.where(row == column, facts_ref[spot : spot + 1, :], 0.0)
        x_ref[spot, near, near] = corner * scale + idle[near, near]
        x_ref[spot, near, far] = side * scale
        x_ref[spot, far, near] = side.T * scale
        x_ref[spot, far, far] = last * scale + idle[far, far]

    chunk = min(CHUNK, basis)
    spans = [(spot, slice(at, at + chunk)) for spot in range(share) for at in range(0, basis, chunk)]
    for _ in range(ITERS):
        estimates = [x_ref[spot] for spot in range(share)]
        parts = [split(x) for x in estimates]
        squares = []
        for spot, span in spans:
            left = [part[span] for part in parts[spot]]
            squares.append(split(0.5 * product(left, parts[spot])))
        for square, (spot, span) in zip(squares, spans):
            x_ref[spot, span] = 1.5 * estimates[spot][span] - product(square, parts[spot])

    for spot in range(share):
        density = jnp.where(row == column, 0.5, 0.0) - 0.5 * x_ref[spot]
        x_ref[spot] = density
        side = density[near, far] * s_ref[spot, near, far]
        corner = density[near, near] * s_ref[spot, near, near] + side.T
        last = density[far, far] * s_ref[spot, far, far] + side
        sums = [jnp.sum(block, axis=0, keepdims=True) for block in (corner, last)]
        charge = jnp.concatenate(swapped(half, jnp.concatenate(sums, axis=1)), axis=1)
        charge = charge - facts_ref[share + spot : share + spot + 1, :]
        blocks = block_row([charge], 3) + facts_ref[2 * share + spot : 2 * share + spot + 1, :LANES]
        whole = jnp.concatenate([charge, blocks], axis=1)
        charge_ref[:, spot : spot + 1, :] = jnp.broadcast_to(whole[None], (charge_ref.shape[0],) + whole.shape)
    for shift in range(tiles):
        first = partner(shift, tiles) % places * rows + (0 if shift < places else middle)
        span = pl.ds(pl.multiple_of(first, rows), rows)
        for spot in range(share):
            left, right = swapped(half, x_ref[spot, span, :])
            chunks[shift][spot, :, :middle] = left
            chunks[shift][spot, :, middle:] = right


def pieces_of(x):
    out = []
    for _ in range(3):
        piece = x.astype(jnp.bfloat16).astype(jnp.float32)
        out.append(piece)
        x = x - piece
    return out


PAIRS = ((0, 0), (0, 1), (1, 0), (0, 2), (1, 1), (2, 0))
DEPTH = 32


def geometry_kernel(around, near_ref, far_ref, own_ref, *refs):
    sources = refs[:around]
    left_out, right_out, near_hot, far_hot, side_ref, table_side = refs[-6:]
    frag_dev, near = near_ref.shape
    far = far_ref.shape[1]
    basis = own_ref.shape[2]
    lane = lax.broadcasted_iota(jnp.int32, (1, near_hot.shape[2]), 1)
    ones = jnp.ones((frag_dev, basis), jnp.float32)
    frag_at, reach = lax.axis_index("frag"), around // 2
    first_frag = (frag_at - reach) * frag_dev

    def fill(target, first, place_ref, scale, extra, which):
        places = [place_ref[axis] for axis in range(3)]
        rows = []
        for place in places:
            parts = pieces_of(place)
            rows += [scale * parts[pair[which]] for pair in PAIRS]
        norm = places[0] * places[0] + places[1] * places[1] + places[2] * places[2] + extra
        sides = [pieces_of(norm), [ones] * 3]
        rows += sides[which] + sides[1 - which]
        rows += [0.0 * ones] * (DEPTH - len(rows))
        for at, row in enumerate(rows):
            for frag in range(frag_dev):
                target[first + frag, at : at + 1, :] = row[frag : frag + 1, :]

    fill(side_ref, 0, own_ref, -2.0, 1.0, 0)
    left_out[...] = side_ref[...].astype(jnp.bfloat16)
    fill(table_side, reach * frag_dev, sources[0], 1.0, 0.0, 1)
    for at in range(1, around):
        step = (at - 1) % reach + 1
        side = lax.rem(frag_at // step + lax.axis_index("tile") + (at - 1) // reach, 2)
        spot = reach + step * (1 - 2 * side)
        fill(table_side, spot * frag_dev, sources[at], 1.0, 0.0, 1)
    for frag in range(frag_dev):
        for k in range(near):
            other = near_ref[frag, k]
            near_hot[frag, k : k + 1, :] = (lane == other).astype(jnp.float32)
            right_out[frag, k] = table_side[other - first_frag].astype(jnp.bfloat16)
        for m in range(far):
            far_hot[frag, m : m + 1, :] = (lane == far_ref[frag, m]).astype(jnp.float32)


def gather_charges(charge_ref, near_hot, far_hot, near_charge, far_block):
    basis = near_charge.shape[2]
    table = charge_ref[...].reshape(-1, basis + LANES)
    for hot, gathered, part in (
        (near_hot, near_charge, table[:, :basis]),
        (far_hot, far_block, table[:, basis:]),
    ):
        every = hot[...].reshape(-1, hot.shape[2])
        picked = jnp.dot(every, part, precision=lax.Precision.HIGHEST, preferred_element_type=jnp.float32)
        gathered[...] = picked.reshape(gathered.shape)


def esp_rows_of(first, count, own_ref, left_ref, right_ref, over_ref, near_charge, far_block):
    _, rows, basis = over_ref.shape
    near, far = near_charge.shape[1], far_block.shape[1]
    pick = own_rows(rows, basis, lax.axis_index("tile") * rows)
    quantities = [block_lanes(at) for at in range(4)]
    for frag in range(first, first + count):
        folded = jnp.zeros((basis, LANES), jnp.float32)
        for k in range(near):
            square = lax.dot_general(
                left_ref[frag],
                right_ref[frag, k],
                (((0,), (0,)), ((), ())),
                preferred_element_type=jnp.float32,
            )
            terms = lax.rsqrt(square) * near_charge[frag, k : k + 1, :]
            for start in range(0, basis, LANES):
                folded = folded + terms[:, start : start + LANES]
        blocks = jnp.zeros((PC, basis), jnp.float32)
        spots = [own_ref[axis, frag : frag + 1, :] for axis in range(3)]
        for m in range(far):
            row = far_block[frag, m : m + 1, :]
            x, y, z, charge = [
                jnp.sum(jnp.where(lanes, row, 0.0), axis=1, keepdims=True) for lanes in quantities
            ]
            total = (spots[0] - x) ** 2 + (spots[1] - y) ** 2 + (spots[2] - z) ** 2
            blocks = blocks + charge * lax.rsqrt(total + 1.0)
        potential = jnp.sum(folded.T, axis=0, keepdims=True) + jnp.sum(blocks, axis=0, keepdims=True)
        potential = (0.5 * SCREENING) * potential
        mine = jnp.sum(jnp.where(pick, potential, 0.0), axis=1, keepdims=True)
        yield frag, over_ref[frag] * (mine + potential)


def first_esp_kernel(charge_ref, near_hot, far_hot, *refs):
    inputs, (esp_ref, near_charge, far_block) = refs[:4], refs[4:]
    gather_charges(charge_ref, near_hot, far_hot, near_charge, far_block)
    for frag, rows in esp_rows_of(0, esp_ref.shape[0], *inputs, near_charge, far_block):
        esp_ref[frag] = rows


def last_esp_kernel(tiles, *refs):
    inputs, done_ref, chunks = refs[:6], refs[6], refs[7 : 7 + tiles]
    density_ref, esp_ref, rest_ref, sems = refs[7 + tiles :]
    share, done = chunks[0].shape[0], done_ref.shape[0]
    copies = [pltpu.make_async_copy(done_ref, esp_ref.at[pl.ds(0, done)], sems.at[tiles])]
    for shift in range(tiles):
        target = density_ref.at[pl.ds(partner(shift, tiles, -1) * share, share)]
        copies.append(pltpu.make_async_copy(chunks[shift], target, sems.at[shift]))
    for copy in copies:
        copy.start()
    rest = rest_ref.shape[0]
    for frag, rows in esp_rows_of(done, rest, *inputs):
        rest_ref[frag - done] = rows
    copies.append(pltpu.make_async_copy(rest_ref, esp_ref.at[pl.ds(done, rest)], sems.at[tiles + 1]))
    copies[-1].start()
    for copy in copies:
        copy.wait()


def call(kernel, outs, inputs, specs, scratch=(), cost=None, out_spec=VMEM):
    return pl.pallas_call(
        kernel,
        out_shape=outs,
        in_specs=specs,
        out_specs=[out_spec] * len(outs),
        scratch_shapes=list(scratch),
        cost_estimate=cost,
        compiler_params=pltpu.CompilerParams(vmem_limit_bytes=24 * 1024 * 1024),
    )(*inputs)


def exchanged(chunks):
    tiles = lax.axis_size("tile")
    places = tiles // 2
    moved = [chunks[0]]
    for shift in range(1, tiles):
        pairs = []
        for tile in range(tiles):
            half = tile // places if shift < places else 1 - tile // places
            pairs.append((tile, half * places + (tile + shift) % places))
        moved.append(lax.ppermute(chunks[shift], "tile", pairs))
    return moved


def neighbours(x, reach):
    peers, tiles = lax.axis_size("frag"), lax.axis_size("tile")
    found = []
    for step in range(1, reach + 1):
        pairs = []
        for low in range(peers - step):
            for tile in range(low // step % 2, tiles, 2):
                ends = low * tiles + tile, (low + step) * tiles + tile
                pairs += [ends, ends[::-1]]
        found.append(lax.ppermute(x, ("frag", "tile"), pairs))
    return found


def from_next_tile(x):
    tiles = lax.axis_size("tile")
    return lax.ppermute(x, "tile", [(tile, tile ^ 1) for tile in range(tiles)])


def per_device(
    core_fock,
    intersection,
    gamma_tile,
    charge_old,
    embed_old,
    core_pop,
    centres,
    frag_sizes,
    near_list,
    far_list,
):
    frag_dev, rows, basis = core_fock.shape
    tiles, peers = lax.axis_size("tile"), lax.axis_size("frag")
    devices, share = tiles * peers, frag_dev // tiles
    chunk = floats(share, rows, basis)
    places = jnp.transpose(centres, (1, 0, 2))
    inputs = (frag_sizes, charge_old, embed_old, core_pop, places, gamma_tile, intersection, core_fock)
    near_part = floats(2, share, rows, basis)
    far_part = floats(share, rows + 8, basis // 2)
    *sent, facts = call(
        functools.partial(half_fock_kernel, tiles),
        [near_part] * (tiles // 2) + [far_part] * (tiles // 2) + [floats(3 * share, basis)],
        [pltpu.with_memory_space_constraint(x, pltpu.HBM) for x in inputs],
        [HBM] * len(inputs),
        [pltpu.SMEM(frag_sizes.shape, jnp.int32)]
        + [pltpu.VMEM(x.shape, jnp.float32) for x in inputs[1:]]
        + [pltpu.SemaphoreType.DMA((len(inputs),))],
    )
    sent = exchanged(sent)
    swaps = neighbours(places, -(-SPAN // frag_dev))
    *pieces, charges = call(
        functools.partial(density_kernel, tiles),
        [chunk] * tiles + [floats(devices, share, basis + LANES)],
        (facts, *sent),
        [VMEM] * (1 + tiles),
        [pltpu.VMEM((share, basis, basis), jnp.float32)] * 2,
        pl.CostEstimate(flops=0, bytes_accessed=0, transcendentals=0),
    )
    moved = exchanged(pieces)
    charges, swaps = lax.optimization_barrier((charges, swaps))
    sources = [places, *swaps, *[from_next_tile(x) for x in swaps]]
    charges = lax.all_to_all(charges, ("frag", "tile"), split_axis=0, concat_axis=0, tiled=True)
    near, far, frags = near_list.shape[1], far_list.shape[1], peers * frag_dev
    parts = call(
        functools.partial(geometry_kernel, len(sources)),
        [
            jax.ShapeDtypeStruct((frag_dev, DEPTH, basis), jnp.bfloat16),
            jax.ShapeDtypeStruct((frag_dev, near, DEPTH, basis), jnp.bfloat16),
            floats(frag_dev, near, frags),
            floats(frag_dev, far, frags),
        ],
        (near_list, far_list, places, *sources, pieces[0]),
        [SMEM, SMEM] + [VMEM] * (1 + len(sources)) + [ANY],
        [
            pltpu.VMEM((frag_dev, DEPTH, basis), jnp.float32),
            pltpu.VMEM((len(sources) * frag_dev, DEPTH, basis), jnp.float32),
        ],
        pl.CostEstimate(flops=0, bytes_accessed=0, transcendentals=0),
    )
    left, right, near_hot, far_hot = parts
    inputs = (places, left, right, intersection)
    done = frag_dev * 3 // 4
    rest = frag_dev - done
    esp_rows, near_charge, far_block = call(
        first_esp_kernel,
        [floats(done, rows, basis), floats(frag_dev, near, basis), floats(frag_dev, far, LANES)],
        (charges, near_hot, far_hot, *inputs),
        [VMEM] * 7,
        cost=pl.CostEstimate(flops=0, bytes_accessed=0, transcendentals=0),
    )
    density, esp_matrix = call(
        functools.partial(last_esp_kernel, tiles),
        [floats(frag_dev, rows, basis)] * 2,
        (*inputs, near_charge, far_block, esp_rows, *moved),
        [VMEM] * (7 + tiles),
        [pltpu.VMEM((rest, rows, basis), jnp.float32), pltpu.SemaphoreType.DMA((tiles + 2,))],
        pl.CostEstimate(flops=0, bytes_accessed=0, transcendentals=0),
        HBM,
    )
    return (density, esp_matrix)


def solution(mesh):
    in_specs = (
        P("frag", "tile", None),
        P("frag", "tile", None),
        P("frag", "tile", None),
        P("frag", None),
        P("frag", None),
        P("frag", None),
        P("frag", None, None),
        P("frag"),
        P("frag", None),
        P("frag", None),
    )
    out_specs = (P("frag", "tile", None), P("frag", "tile", None))
    return jax.shard_map(
        per_device, mesh=mesh, in_specs=in_specs, out_specs=out_specs, check_vma=False
    )
```

```python
import functools

import jax
import jax.numpy as jnp
from jax import lax
from jax.experimental import pallas as pl
from jax.experimental.pallas import tpu as pltpu
from jax.sharding import PartitionSpec as P

PC = 8
ITERS = 12
SCREENING = 0.25
SPAN = 8
LANES = 128
CHUNK = 128
COARSE = jnp.float8_e4m3fn
WHOLE_SCALE = 256.0
REST_SCALE = 65536.0
VMEM = pl.BlockSpec(memory_space=pltpu.VMEM)
SMEM = pl.BlockSpec(memory_space=pltpu.SMEM)
HBM = pl.BlockSpec(memory_space=pltpu.HBM)
ANY = pl.BlockSpec(memory_space=pl.ANY)


def floats(*shape):
    return jax.ShapeDtypeStruct(shape, jnp.float32)


def block_mask(basis):
    group = basis // PC
    block = lax.broadcasted_iota(jnp.int32, (PC, basis), 0)
    column = lax.broadcasted_iota(jnp.int32, (PC, basis), 1)
    return (column >= block * group) & (column < (block + 1) * group)


def block_lanes(at):
    block = lax.broadcasted_iota(jnp.int32, (PC, LANES), 0)
    lane = lax.broadcasted_iota(jnp.int32, (PC, LANES), 1)
    return lane == block + at * PC


def block_row(rows, first):
    mask = block_mask(rows[0].shape[1])
    total = jnp.zeros((PC, LANES), jnp.float32)
    for at, row in enumerate(rows):
        sums = jnp.sum(jnp.where(mask, row, 0.0), axis=1, keepdims=True)
        total = total + jnp.where(block_lanes(first + at), sums, 0.0)
    return jnp.sum(total, axis=0, keepdims=True)


def own_rows(rows, basis, first):
    row = lax.broadcasted_iota(jnp.int32, (rows, basis), 0)
    column = lax.broadcasted_iota(jnp.int32, (rows, basis), 1)
    return column == row + first


def seat(tiles):
    places = tiles // 2
    tile_at = lax.axis_index("tile")
    return tile_at // places, lax.rem(tile_at, places), places


def partner(shift, tiles, sign=1):
    half, place, places = seat(tiles)
    other = half if shift < places else 1 - half
    return other * places + lax.rem(place + places + sign * (shift % places), places)


def swapped(half, x):
    middle = x.shape[-1] // 2
    left, right = x[..., :middle], x[..., middle:]
    return jnp.where(half == 0, left, right), jnp.where(half == 0, right, left)


def half_fock_kernel(tiles, *refs):
    inputs, outs, buffers, sems = refs[:8], refs[8:-11], refs[-11:-1], refs[-1]
    sizes_ref, charge_ref, embed_ref, pop_ref, place_ref, gamma_ref = buffers[:6]
    over_near, core_near, over_there, core_there = buffers[6:]
    half, place_at, places = seat(tiles)
    count, rows, basis = over_near.shape
    share, middle = count // places, basis // 2
    here, there = pl.ds(half * count, count), pl.ds((1 - half) * count, count)
    columns = pl.ds(pl.multiple_of(half * middle, middle), middle)
    sources = [*inputs[:6], *[source.at[here] for source in inputs[6:]]]
    sources += [source.at[there, :, columns] for source in inputs[6:]]
    copies = [
        pltpu.make_async_copy(source, buffer, sems.at[at])
        for at, (source, buffer) in enumerate(zip(sources, buffers))
    ]
    for copy in copies:
        copy.start()
    for copy in copies:
        copy.wait()
    pick = own_rows(rows, basis, lax.axis_index("tile") * rows)
    pick_half = own_rows(rows, middle, place_at * rows)
    row = lax.broadcasted_iota(jnp.int32, (rows, middle), 0) + lax.axis_index("tile") * rows
    column = lax.broadcasted_iota(jnp.int32, (rows, middle), 1)
    mine, others = column + half * middle, column + (1 - half) * middle
    lane = lax.broadcasted_iota(jnp.int32, (1, basis), 1)
    for shift in range(tiles):
        target = partner(shift, tiles)
        for spot in range(share):
            frag = target * share + spot
            size = sizes_ref[frag]
            terms = gamma_ref[frag] * charge_ref[pl.ds(frag, 1), :]
            terms = terms + jnp.where(pick, embed_ref[pl.ds(frag, 1), :], 0.0)
            field = jnp.sum(terms, axis=1, keepdims=True)
            at = lax.rem(place_at + shift, places) * share + spot
            if shift < places:
                core, core_far = swapped(half, core_near[at])
                over, over_far = swapped(half, over_near[at])
            else:
                core, over = core_there[at], over_there[at]
            inside = (row < size) & (mine < size)
            core, over = jnp.where(inside, core, 0.0), jnp.where(inside, over, 0.0)
            out = outs[shift]
            if shift < places:
                inside = (row < size) & (others < size)
                over_far = jnp.where(inside, over_far, 0.0)
                out[0, spot, :, :middle] = 0.5 * (core + over * field)
                out[0, spot, :, middle:] = jnp.where(inside, core_far, 0.0) + over_far * (0.5 * field)
                out[1, spot, :, :middle] = over
                out[1, spot, :, middle:] = over_far
            else:
                out[spot, :rows] = jnp.where(mine >= row, core, over)
                field_row = jnp.sum(jnp.where(pick_half, field, 0.0), axis=0, keepdims=True)
                diagonal = jnp.sum(jnp.where(pick_half, over, 0.0), axis=0, keepdims=True)
                rest = jnp.zeros((out.shape[1] - rows - 2, middle), jnp.float32)
                out[spot, rows:] = jnp.concatenate([field_row, diagonal, rest], axis=0)
            if shift == 0:
                facts = outs[-1]
                idle = swapped(half, (lane >= size).astype(jnp.float32))
                facts[spot : spot + 1, :middle] = idle[0]
                facts[spot : spot + 1, middle:] = idle[1]
                facts[share + spot : share + spot + 1, :] = pop_ref[pl.ds(frag, 1), :]
                spots = [place_ref[axis, pl.ds(frag, 1), :] for axis in range(3)]
                means = block_row(spots, 0) * (PC / basis)
                facts[2 * share + spot : 2 * share + spot + 1, :LANES] = means


def split(x):
    high = x.astype(jnp.bfloat16)
    rest = (x - high.astype(jnp.float32)).astype(jnp.bfloat16)
    coarse = (high * jnp.bfloat16(WHOLE_SCALE)).astype(COARSE)
    return high, coarse, (rest * jnp.bfloat16(REST_SCALE)).astype(COARSE)


def product(left, right):
    dot = functools.partial(jnp.dot, preferred_element_type=jnp.float32)
    rest = dot(left[1], right[2]) + dot(left[2], right[1])
    return dot(left[0], right[0]) + rest * (1.0 / (WHOLE_SCALE * REST_SCALE))


def density_kernel(tiles, facts_ref, *refs):
    places = tiles // 2
    near_parts, far_parts = refs[:places], refs[places:tiles]
    chunks, charge_ref = refs[tiles : 2 * tiles], refs[2 * tiles]
    x_ref, s_ref = refs[2 * tiles + 1 :]
    half, place_at, _ = seat(tiles)
    _, share, rows, basis = near_parts[0].shape
    middle = basis // 2
    for shift in range(places):
        source = lax.rem(place_at + places - shift, places) * rows
        span = pl.ds(pl.multiple_of(source, rows), rows)
        far_span = pl.ds(pl.multiple_of(source + middle, rows), rows)
        for spot in range(share):
            x_ref[spot, span, :] = near_parts[shift][0, spot]
            s_ref[spot, span, :] = near_parts[shift][1, spot]
            x_ref[spot, far_span, middle:] = far_parts[shift][spot, :rows]
    row = lax.broadcasted_iota(jnp.int32, (basis, basis), 0)
    column = lax.broadcasted_iota(jnp.int32, (basis, basis), 1)
    near, far = slice(0, middle), slice(middle, basis)
    for spot in range(share):
        extra = far_parts[0][spot, rows:]
        for part in far_parts[1:]:
            extra = extra + part[spot, rows:]
        field = extra[:1]
        corner, packed = x_ref[spot, near, near], x_ref[spot, far, far]
        turned = packed.T
        down, along = row[near, near], column[near, near]
        over = jnp.where(along < down, packed, jnp.where(along == down, extra[1:2], turned))
        last = 0.5 * (jnp.where(along >= down, packed, turned) + over * field)
        s_ref[spot, far, far] = over
        side = x_ref[spot, near, far] + s_ref[spot, near, far] * (0.5 * field)
        corner, last = corner + corner.T, last + last.T
        total = corner * corner + last * last + 2.0 * (side * side)
        scale = 1.0 / jnp.sqrt(jnp.sum(total, keepdims=True) + 1e-06)
        idle = jnp.where(row == column, facts_ref[spot : spot + 1, :], 0.0)
        x_ref[spot, near, near] = corner * scale + idle[near, near]
        x_ref[spot, near, far] = side * scale
        x_ref[spot, far, near] = side.T * scale
        x_ref[spot, far, far] = last * scale + idle[far, far]

    chunk = min(CHUNK, basis)
    spans = [(spot, slice(at, at + chunk)) for spot in range(share) for at in range(0, basis, chunk)]
    for _ in range(ITERS):
        estimates = [x_ref[spot] for spot in range(share)]
        parts = [split(x) for x in estimates]
        squares = []
        for spot, span in spans:
            left = [part[span] for part in parts[spot]]
            squares.append(split(0.5 * product(left, parts[spot])))
        for square, (spot, span) in zip(squares, spans):
            x_ref[spot, span] = 1.5 * estimates[spot][span] - product(square, parts[spot])

    for spot in range(share):
        density = jnp.where(row == column, 0.5, 0.0) - 0.5 * x_ref[spot]
        x_ref[spot] = density
        side = density[near, far] * s_ref[spot, near, far]
        corner = density[near, near] * s_ref[spot, near, near] + side.T
        last = density[far, far] * s_ref[spot, far, far] + side
        sums = [jnp.sum(block, axis=0, keepdims=True) for block in (corner, last)]
        charge = jnp.concatenate(swapped(half, jnp.concatenate(sums, axis=1)), axis=1)
        charge = charge - facts_ref[share + spot : share + spot + 1, :]
        blocks = block_row([charge], 3) + facts_ref[2 * share + spot : 2 * share + spot + 1, :LANES]
        whole = jnp.concatenate([charge, blocks], axis=1)
        charge_ref[:, spot : spot + 1, :] = jnp.broadcast_to(whole[None], (charge_ref.shape[0],) + whole.shape)
    for shift in range(tiles):
        first = partner(shift, tiles) % places * rows + (0 if shift < places else middle)
        span = pl.ds(pl.multiple_of(first, rows), rows)
        for spot in range(share):
            left, right = swapped(half, x_ref[spot, span, :])
            chunks[shift][spot, :, :middle] = left
            chunks[shift][spot, :, middle:] = right


def pieces_of(x):
    out = []
    for _ in range(3):
        piece = x.astype(jnp.bfloat16).astype(jnp.float32)
        out.append(piece)
        x = x - piece
    return out


PAIRS = ((0, 0), (0, 1), (1, 0), (0, 2), (1, 1), (2, 0))
DEPTH = 32


def geometry_kernel(around, near_ref, far_ref, own_ref, *refs):
    sources = refs[:around]
    left_out, right_out, near_hot, far_hot, side_ref, table_side = refs[-6:]
    frag_dev, near = near_ref.shape
    far = far_ref.shape[1]
    basis = own_ref.shape[2]
    lane = lax.broadcasted_iota(jnp.int32, (1, near_hot.shape[2]), 1)
    ones = jnp.ones((frag_dev, basis), jnp.float32)
    frag_at, reach = lax.axis_index("frag"), around // 2
    tiles, peers = lax.axis_size("tile"), lax.axis_size("frag")
    share = frag_dev // tiles

    def row_of(frag):
        inside = lax.rem(frag, frag_dev)
        return (inside // share * peers + frag // frag_dev) * share + lax.rem(inside, share)

    first_frag = (frag_at - reach) * frag_dev

    def fill(target, first, place_ref, scale, extra, which):
        places = [place_ref[axis] for axis in range(3)]
        rows = []
        for place in places:
            parts = pieces_of(place)
            rows += [scale * parts[pair[which]] for pair in PAIRS]
        norm = places[0] * places[0] + places[1] * places[1] + places[2] * places[2] + extra
        sides = [pieces_of(norm), [ones] * 3]
        rows += sides[which] + sides[1 - which]
        rows += [0.0 * ones] * (DEPTH - len(rows))
        for at, row in enumerate(rows):
            for frag in range(frag_dev):
                target[first + frag, at : at + 1, :] = row[frag : frag + 1, :]

    fill(side_ref, 0, own_ref, -2.0, 1.0, 0)
    left_out[...] = side_ref[...].astype(jnp.bfloat16)
    fill(table_side, reach * frag_dev, sources[0], 1.0, 0.0, 1)
    for at in range(1, around):
        step = (at - 1) % reach + 1
        side = lax.rem(frag_at // step + lax.axis_index("tile") + (at - 1) // reach, 2)
        spot = reach + step * (1 - 2 * side)
        fill(table_side, spot * frag_dev, sources[at], 1.0, 0.0, 1)
    for frag in range(frag_dev):
        for k in range(near):
            other = near_ref[frag, k]
            near_hot[frag, k : k + 1, :] = (lane == row_of(other)).astype(jnp.float32)
            right_out[frag, k] = table_side[other - first_frag].astype(jnp.bfloat16)
        for m in range(far):
            far_hot[frag, m : m + 1, :] = (lane == row_of(far_ref[frag, m])).astype(jnp.float32)


def gather_charges(charge_ref, near_hot, far_hot, near_charge, far_block):
    basis = near_charge.shape[2]
    table = charge_ref[...].reshape(-1, basis + LANES)
    for hot, gathered, part in (
        (near_hot, near_charge, table[:, :basis]),
        (far_hot, far_block, table[:, basis:]),
    ):
        every = hot[...].reshape(-1, hot.shape[2])
        picked = jnp.dot(every, part, precision=lax.Precision.HIGHEST, preferred_element_type=jnp.float32)
        gathered[...] = picked.reshape(gathered.shape)


def esp_rows_of(first, count, own_ref, left_ref, right_ref, over_ref, near_charge, far_block):
    _, rows, basis = over_ref.shape
    near, far = near_charge.shape[1], far_block.shape[1]
    pick = own_rows(rows, basis, lax.axis_index("tile") * rows)
    quantities = [block_lanes(at) for at in range(4)]
    for frag in range(first, first + count):
        folded = jnp.zeros((basis, LANES), jnp.float32)
        for k in range(near):
            square = lax.dot_general(
                left_ref[frag],
                right_ref[frag, k],
                (((0,), (0,)), ((), ())),
                preferred_element_type=jnp.float32,
            )
            terms = lax.rsqrt(square) * near_charge[frag, k : k + 1, :]
            for start in range(0, basis, LANES):
                folded = folded + terms[:, start : start + LANES]
        blocks = jnp.zeros((PC, basis), jnp.float32)
        spots = [own_ref[axis, frag : frag + 1, :] for axis in range(3)]
        for m in range(far):
            row = far_block[frag, m : m + 1, :]
            x, y, z, charge = [
                jnp.sum(jnp.where(lanes, row, 0.0), axis=1, keepdims=True) for lanes in quantities
            ]
            total = (spots[0] - x) ** 2 + (spots[1] - y) ** 2 + (spots[2] - z) ** 2
            blocks = blocks + charge * lax.rsqrt(total + 1.0)
        potential = jnp.sum(folded.T, axis=0, keepdims=True) + jnp.sum(blocks, axis=0, keepdims=True)
        potential = (0.5 * SCREENING) * potential
        mine = jnp.sum(jnp.where(pick, potential, 0.0), axis=1, keepdims=True)
        yield frag, over_ref[frag] * (mine + potential)


def first_esp_kernel(charge_ref, near_hot, far_hot, *refs):
    inputs, (esp_ref, near_charge, far_block) = refs[:4], refs[4:]
    gather_charges(charge_ref, near_hot, far_hot, near_charge, far_block)
    for frag, rows in esp_rows_of(0, esp_ref.shape[0], *inputs, near_charge, far_block):
        esp_ref[frag] = rows


def last_esp_kernel(tiles, *refs):
    inputs, done_ref, chunks = refs[:6], refs[6], refs[7 : 7 + tiles]
    density_ref, esp_ref, rest_ref, sems = refs[7 + tiles :]
    share, done = chunks[0].shape[0], done_ref.shape[0]
    copies = [pltpu.make_async_copy(done_ref, esp_ref.at[pl.ds(0, done)], sems.at[tiles])]
    for shift in range(tiles):
        target = density_ref.at[pl.ds(partner(shift, tiles, -1) * share, share)]
        copies.append(pltpu.make_async_copy(chunks[shift], target, sems.at[shift]))
    for copy in copies:
        copy.start()
    rest = rest_ref.shape[0]
    for frag, rows in esp_rows_of(done, rest, *inputs):
        rest_ref[frag - done] = rows
    copies.append(pltpu.make_async_copy(rest_ref, esp_ref.at[pl.ds(done, rest)], sems.at[tiles + 1]))
    copies[-1].start()
    for copy in copies:
        copy.wait()


def call(kernel, outs, inputs, specs, scratch=(), cost=None, out_spec=VMEM):
    return pl.pallas_call(
        kernel,
        out_shape=outs,
        in_specs=specs,
        out_specs=[out_spec] * len(outs),
        scratch_shapes=list(scratch),
        cost_estimate=cost,
        compiler_params=pltpu.CompilerParams(vmem_limit_bytes=24 * 1024 * 1024),
    )(*inputs)


def exchanged(chunks):
    tiles = lax.axis_size("tile")
    places = tiles // 2
    moved = [chunks[0]]
    for shift in range(1, tiles):
        pairs = []
        for tile in range(tiles):
            half = tile // places if shift < places else 1 - tile // places
            pairs.append((tile, half * places + (tile + shift) % places))
        moved.append(lax.ppermute(chunks[shift], "tile", pairs))
    return moved


def neighbours(x, reach):
    peers, tiles = lax.axis_size("frag"), lax.axis_size("tile")
    found = []
    for step in range(1, reach + 1):
        pairs = []
        for low in range(peers - step):
            for tile in range(low // step % 2, tiles, 2):
                ends = low * tiles + tile, (low + step) * tiles + tile
                pairs += [ends, ends[::-1]]
        found.append(lax.ppermute(x, ("frag", "tile"), pairs))
    return found


def from_next_tile(x):
    tiles = lax.axis_size("tile")
    return lax.ppermute(x, "tile", [(tile, tile ^ 1) for tile in range(tiles)])


def per_device(
    core_fock,
    intersection,
    gamma_tile,
    charge_old,
    embed_old,
    core_pop,
    centres,
    frag_sizes,
    near_list,
    far_list,
):
    frag_dev, rows, basis = core_fock.shape
    tiles, peers = lax.axis_size("tile"), lax.axis_size("frag")
    devices, share = tiles * peers, frag_dev // tiles
    chunk = floats(share, rows, basis)
    places = jnp.transpose(centres, (1, 0, 2))
    inputs = (frag_sizes, charge_old, embed_old, core_pop, places, gamma_tile, intersection, core_fock)
    near_part = floats(2, share, rows, basis)
    far_part = floats(share, rows + 8, basis // 2)
    *sent, facts = call(
        functools.partial(half_fock_kernel, tiles),
        [near_part] * (tiles // 2) + [far_part] * (tiles // 2) + [floats(3 * share, basis)],
        [pltpu.with_memory_space_constraint(x, pltpu.HBM) for x in inputs],
        [HBM] * len(inputs),
        [pltpu.SMEM(frag_sizes.shape, jnp.int32)]
        + [pltpu.VMEM(x.shape, jnp.float32) for x in inputs[1:6]]
        + [pltpu.VMEM((frag_dev // 2, rows, width), jnp.float32) for width in (basis, basis, basis // 2, basis // 2)]
        + [pltpu.SemaphoreType.DMA((len(inputs) + 2,))],
    )
    sent = exchanged(sent)
    swaps = neighbours(places, -(-SPAN // frag_dev))
    *pieces, charges = call(
        functools.partial(density_kernel, tiles),
        [chunk] * tiles + [floats(devices, share, basis + LANES)],
        (facts, *sent),
        [VMEM] * (1 + tiles),
        [pltpu.VMEM((share, basis, basis), jnp.float32)] * 2,
        pl.CostEstimate(flops=0, bytes_accessed=0, transcendentals=0),
    )
    moved = exchanged(pieces)
    charges, swaps = lax.optimization_barrier((charges, swaps))
    sources = [places, *swaps, *[from_next_tile(x) for x in swaps]]
    charges = lax.all_to_all(charges, ("tile", "frag"), split_axis=0, concat_axis=0, tiled=True)
    near, far, frags = near_list.shape[1], far_list.shape[1], peers * frag_dev
    parts = call(
        functools.partial(geometry_kernel, len(sources)),
        [
            jax.ShapeDtypeStruct((frag_dev, DEPTH, basis), jnp.bfloat16),
            jax.ShapeDtypeStruct((frag_dev, near, DEPTH, basis), jnp.bfloat16),
            floats(frag_dev, near, frags),
            floats(frag_dev, far, frags),
        ],
        (near_list, far_list, places, *sources, pieces[0]),
        [SMEM, SMEM] + [VMEM] * (1 + len(sources)) + [ANY],
        [
            pltpu.VMEM((frag_dev, DEPTH, basis), jnp.float32),
            pltpu.VMEM((len(sources) * frag_dev, DEPTH, basis), jnp.float32),
        ],
        pl.CostEstimate(flops=0, bytes_accessed=0, transcendentals=0),
    )
    left, right, near_hot, far_hot = parts
    inputs = (places, left, right, intersection)
    done = frag_dev * 3 // 4
    rest = frag_dev - done
    esp_rows, near_charge, far_block = call(
        first_esp_kernel,
        [floats(done, rows, basis), floats(frag_dev, near, basis), floats(frag_dev, far, LANES)],
        (charges, near_hot, far_hot, *inputs),
        [VMEM] * 7,
        cost=pl.CostEstimate(flops=0, bytes_accessed=0, transcendentals=0),
    )
    density, esp_matrix = call(
        functools.partial(last_esp_kernel, tiles),
        [floats(frag_dev, rows, basis)] * 2,
        (*inputs, near_charge, far_block, esp_rows, *moved),
        [VMEM] * (7 + tiles),
        [pltpu.VMEM((rest, rows, basis), jnp.float32), pltpu.SemaphoreType.DMA((tiles + 2,))],
        pl.CostEstimate(flops=0, bytes_accessed=0, transcendentals=0),
        HBM,
    )
    return (density, esp_matrix)


def solution(mesh):
    in_specs = (
        P("frag", "tile", None),
        P("frag", "tile", None),
        P("frag", "tile", None),
        P("frag", None),
        P("frag", None),
        P("frag", None),
        P("frag", None, None),
        P("frag"),
        P("frag", None),
        P("frag", None),
    )
    out_specs = (P("frag", "tile", None), P("frag", "tile", None))
    return jax.shard_map(
        per_device, mesh=mesh, in_specs=in_specs, out_specs=out_specs, check_vma=False
    )
```

```python
import functools

import jax
import jax.numpy as jnp
from jax import lax
from jax.experimental import pallas as pl
from jax.experimental.pallas import tpu as pltpu
from jax.sharding import PartitionSpec as P

PC = 8
ITERS = 12
SCREENING = 0.25
SPAN = 8
LANES = 128
CHUNK = 128
COARSE = jnp.float8_e4m3fn
WHOLE_SCALE = 256.0
REST_SCALE = 65536.0
VMEM = pl.BlockSpec(memory_space=pltpu.VMEM)
SMEM = pl.BlockSpec(memory_space=pltpu.SMEM)
HBM = pl.BlockSpec(memory_space=pltpu.HBM)
ANY = pl.BlockSpec(memory_space=pl.ANY)


def floats(*shape):
    return jax.ShapeDtypeStruct(shape, jnp.float32)


def block_mask(basis):
    group = basis // PC
    block = lax.broadcasted_iota(jnp.int32, (PC, basis), 0)
    column = lax.broadcasted_iota(jnp.int32, (PC, basis), 1)
    return (column >= block * group) & (column < (block + 1) * group)


def block_lanes(at):
    block = lax.broadcasted_iota(jnp.int32, (PC, LANES), 0)
    lane = lax.broadcasted_iota(jnp.int32, (PC, LANES), 1)
    return lane == block + at * PC


def block_row(rows, first):
    mask = block_mask(rows[0].shape[1])
    total = jnp.zeros((PC, LANES), jnp.float32)
    for at, row in enumerate(rows):
        sums = jnp.sum(jnp.where(mask, row, 0.0), axis=1, keepdims=True)
        total = total + jnp.where(block_lanes(first + at), sums, 0.0)
    return jnp.sum(total, axis=0, keepdims=True)


def own_rows(rows, basis, first):
    row = lax.broadcasted_iota(jnp.int32, (rows, basis), 0)
    column = lax.broadcasted_iota(jnp.int32, (rows, basis), 1)
    return column == row + first


def seat(tiles):
    places = tiles // 2
    tile_at = lax.axis_index("tile")
    return tile_at // places, lax.rem(tile_at, places), places


def partner(shift, tiles, sign=1):
    half, place, places = seat(tiles)
    other = half if shift < places else 1 - half
    return other * places + lax.rem(place + places + sign * (shift % places), places)


def swapped(half, x):
    middle = x.shape[-1] // 2
    left, right = x[..., :middle], x[..., middle:]
    return jnp.where(half == 0, left, right), jnp.where(half == 0, right, left)


def half_fock_kernel(tiles, *refs):
    inputs, outs, buffers, sems = refs[:8], refs[8:-11], refs[-11:-1], refs[-1]
    sizes_ref, charge_ref, embed_ref, pop_ref, place_ref, gamma_ref = buffers[:6]
    over_near, core_near, over_there, core_there = buffers[6:]
    half, place_at, places = seat(tiles)
    count, rows, basis = over_near.shape
    share, middle = count // places, basis // 2
    here, there = pl.ds(half * count, count), pl.ds((1 - half) * count, count)
    columns = pl.ds(pl.multiple_of(half * middle, middle), middle)
    sources = [*inputs[:6], *[source.at[here] for source in inputs[6:]]]
    sources += [source.at[there, :, columns] for source in inputs[6:]]
    copies = [
        pltpu.make_async_copy(source, buffer, sems.at[at])
        for at, (source, buffer) in enumerate(zip(sources, buffers))
    ]
    for copy in copies:
        copy.start()
    for copy in copies:
        copy.wait()
    pick = own_rows(rows, basis, lax.axis_index("tile") * rows)
    pick_half = own_rows(rows, middle, place_at * rows)
    row = lax.broadcasted_iota(jnp.int32, (rows, middle), 0) + lax.axis_index("tile") * rows
    column = lax.broadcasted_iota(jnp.int32, (rows, middle), 1)
    mine, others = column + half * middle, column + (1 - half) * middle
    lane = lax.broadcasted_iota(jnp.int32, (1, basis), 1)
    for shift in range(tiles):
        target = partner(shift, tiles)
        for spot in range(share):
            frag = target * share + spot
            size = sizes_ref[frag]
            terms = gamma_ref[frag] * charge_ref[pl.ds(frag, 1), :]
            terms = terms + jnp.where(pick, embed_ref[pl.ds(frag, 1), :], 0.0)
            field = jnp.sum(terms, axis=1, keepdims=True)
            at = lax.rem(place_at + shift, places) * share + spot
            if shift < places:
                core, core_far = swapped(half, core_near[at])
                over, over_far = swapped(half, over_near[at])
            else:
                core, over = core_there[at], over_there[at]
            inside = (row < size) & (mine < size)
            core, over = jnp.where(inside, core, 0.0), jnp.where(inside, over, 0.0)
            out = outs[shift]
            if shift < places:
                inside = (row < size) & (others < size)
                over_far = jnp.where(inside, over_far, 0.0)
                out[0, spot, :, :middle] = 0.5 * (core + over * field)
                out[0, spot, :, middle:] = jnp.where(inside, core_far, 0.0) + over_far * (0.5 * field)
                out[1, spot, :, :middle] = over
                out[1, spot, :, middle:] = over_far
            else:
                out[spot, :rows] = jnp.where(mine >= row, core, over)
                field_row = jnp.sum(jnp.where(pick_half, field, 0.0), axis=0, keepdims=True)
                diagonal = jnp.sum(jnp.where(pick_half, over, 0.0), axis=0, keepdims=True)
                rest = jnp.zeros((out.shape[1] - rows - 2, middle), jnp.float32)
                out[spot, rows:] = jnp.concatenate([field_row, diagonal, rest], axis=0)
            if shift == 0:
                facts = outs[-1]
                idle = swapped(half, (lane >= size).astype(jnp.float32))
                facts[spot : spot + 1, :middle] = idle[0]
                facts[spot : spot + 1, middle:] = idle[1]
                facts[share + spot : share + spot + 1, :] = pop_ref[pl.ds(frag, 1), :]
                spots = [place_ref[axis, pl.ds(frag, 1), :] for axis in range(3)]
                means = block_row(spots, 0) * (PC / basis)
                facts[2 * share + spot : 2 * share + spot + 1, :LANES] = means


def split(x):
    high = x.astype(jnp.bfloat16)
    rest = (x - high.astype(jnp.float32)).astype(jnp.bfloat16)
    coarse = (high * jnp.bfloat16(WHOLE_SCALE)).astype(COARSE)
    return high, coarse, (rest * jnp.bfloat16(REST_SCALE)).astype(COARSE)


def product(left, right):
    dot = functools.partial(jnp.dot, preferred_element_type=jnp.float32)
    rest = dot(left[1], right[2]) + dot(left[2], right[1])
    return dot(left[0], right[0]) + rest * (1.0 / (WHOLE_SCALE * REST_SCALE))


def density_kernel(tiles, facts_ref, *refs):
    places = tiles // 2
    near_parts, far_parts = refs[:places], refs[places:tiles]
    chunks, charge_ref = refs[tiles : 2 * tiles], refs[2 * tiles]
    x_ref, s_ref = refs[2 * tiles + 1 :]
    half, place_at, _ = seat(tiles)
    _, share, rows, basis = near_parts[0].shape
    middle = basis // 2
    for shift in range(places):
        source = lax.rem(place_at + places - shift, places) * rows
        span = pl.ds(pl.multiple_of(source, rows), rows)
        far_span = pl.ds(pl.multiple_of(source + middle, rows), rows)
        for spot in range(share):
            x_ref[spot, span, :] = near_parts[shift][0, spot]
            s_ref[spot, span, :] = near_parts[shift][1, spot]
            x_ref[spot, far_span, middle:] = far_parts[shift][spot, :rows]
    row = lax.broadcasted_iota(jnp.int32, (basis, basis), 0)
    column = lax.broadcasted_iota(jnp.int32, (basis, basis), 1)
    near, far = slice(0, middle), slice(middle, basis)
    for spot in range(share):
        extra = far_parts[0][spot, rows:]
        for part in far_parts[1:]:
            extra = extra + part[spot, rows:]
        field = extra[:1]
        corner, packed = x_ref[spot, near, near], x_ref[spot, far, far]
        turned = packed.T
        down, along = row[near, near], column[near, near]
        over = jnp.where(along < down, packed, jnp.where(along == down, extra[1:2], turned))
        last = 0.5 * (jnp.where(along >= down, packed, turned) + over * field)
        s_ref[spot, far, far] = over
        side = x_ref[spot, near, far] + s_ref[spot, near, far] * (0.5 * field)
        corner, last = corner + corner.T, last + last.T
        total = corner * corner + last * last + 2.0 * (side * side)
        scale = 1.0 / jnp.sqrt(jnp.sum(total, keepdims=True) + 1e-06)
        idle = jnp.where(row == column, facts_ref[spot : spot + 1, :], 0.0)
        x_ref[spot, near, near] = corner * scale + idle[near, near]
        x_ref[spot, near, far] = side * scale
        x_ref[spot, far, near] = side.T * scale
        x_ref[spot, far, far] = last * scale + idle[far, far]

    chunk = min(CHUNK, basis)
    spans = [(spot, slice(at, at + chunk)) for spot in range(share) for at in range(0, basis, chunk)]
    for _ in range(ITERS):
        estimates = [x_ref[spot] for spot in range(share)]
        parts = [split(x) for x in estimates]
        squares = []
        for spot, span in spans:
            left = [part[span] for part in parts[spot]]
            squares.append(split(0.5 * product(left, parts[spot])))
        for square, (spot, span) in zip(squares, spans):
            x_ref[spot, span] = 1.5 * estimates[spot][span] - product(square, parts[spot])

    for spot in range(share):
        density = jnp.where(row == column, 0.5, 0.0) - 0.5 * x_ref[spot]
        x_ref[spot] = density
        side = density[near, far] * s_ref[spot, near, far]
        corner = density[near, near] * s_ref[spot, near, near] + side.T
        last = density[far, far] * s_ref[spot, far, far] + side
        sums = [jnp.sum(block, axis=0, keepdims=True) for block in (corner, last)]
        charge = jnp.concatenate(swapped(half, jnp.concatenate(sums, axis=1)), axis=1)
        charge = charge - facts_ref[share + spot : share + spot + 1, :]
        blocks = block_row([charge], 3) + facts_ref[2 * share + spot : 2 * share + spot + 1, :LANES]
        whole = jnp.concatenate([charge, blocks], axis=1)
        charge_ref[:, spot : spot + 1, :] = jnp.broadcast_to(whole[None], (charge_ref.shape[0],) + whole.shape)
    for shift in range(tiles):
        first = partner(shift, tiles) % places * rows + (0 if shift < places else middle)
        span = pl.ds(pl.multiple_of(first, rows), rows)
        for spot in range(share):
            left, right = swapped(half, x_ref[spot, span, :])
            chunks[shift][spot, :, :middle] = left
            chunks[shift][spot, :, middle:] = right


def pieces_of(x):
    out = []
    for _ in range(3):
        piece = x.astype(jnp.bfloat16).astype(jnp.float32)
        out.append(piece)
        x = x - piece
    return out


PAIRS = ((0, 0), (0, 1), (1, 0), (0, 2), (1, 1), (2, 0))
DEPTH = 32


def geometry_kernel(around, near_ref, far_ref, own_ref, *refs):
    sources = refs[:around]
    left_out, right_out, near_hot, far_hot, side_ref, table_side = refs[-6:]
    frag_dev, near = near_ref.shape
    far = far_ref.shape[1]
    basis = own_ref.shape[2]
    lane = lax.broadcasted_iota(jnp.int32, (1, near_hot.shape[2]), 1)
    ones = jnp.ones((frag_dev, basis), jnp.float32)
    frag_at, reach = lax.axis_index("frag"), around // 2
    tiles, peers = lax.axis_size("tile"), lax.axis_size("frag")
    share = frag_dev // tiles

    def row_of(frag):
        inside = lax.rem(frag, frag_dev)
        return (inside // share * peers + frag // frag_dev) * share + lax.rem(inside, share)

    first_frag = (frag_at - reach) * frag_dev

    def fill(target, first, place_ref, scale, extra, which):
        places = [place_ref[axis] for axis in range(3)]
        rows = []
        for place in places:
            parts = pieces_of(place)
            rows += [scale * parts[pair[which]] for pair in PAIRS]
        norm = places[0] * places[0] + places[1] * places[1] + places[2] * places[2] + extra
        sides = [pieces_of(norm), [ones] * 3]
        rows += sides[which] + sides[1 - which]
        rows += [0.0 * ones] * (DEPTH - len(rows))
        for at, row in enumerate(rows):
            for frag in range(frag_dev):
                target[first + frag, at : at + 1, :] = row[frag : frag + 1, :]

    fill(side_ref, 0, own_ref, -2.0, 1.0, 0)
    left_out[...] = side_ref[...].astype(jnp.bfloat16)
    fill(table_side, reach * frag_dev, sources[0], 1.0, 0.0, 1)
    for at in range(1, around):
        step = (at - 1) % reach + 1
        side = lax.rem(frag_at // step + lax.axis_index("tile") + (at - 1) // reach, 2)
        spot = reach + step * (1 - 2 * side)
        fill(table_side, spot * frag_dev, sources[at], 1.0, 0.0, 1)
    for frag in range(frag_dev):
        for k in range(near):
            other = near_ref[frag, k]
            near_hot[frag, k : k + 1, :] = (lane == row_of(other)).astype(jnp.float32)
            right_out[frag, k] = table_side[other - first_frag].astype(jnp.bfloat16)
        for m in range(far):
            far_hot[frag, m : m + 1, :] = (lane == row_of(far_ref[frag, m])).astype(jnp.float32)


def gather_charges(charge_ref, near_hot, far_hot, near_charge, far_block):
    basis = near_charge.shape[2]
    table = charge_ref[...].reshape(-1, basis + LANES)
    for hot, gathered, part in (
        (near_hot, near_charge, table[:, :basis]),
        (far_hot, far_block, table[:, basis:]),
    ):
        every = hot[...].reshape(-1, hot.shape[2]).astype(jnp.bfloat16)
        pieces = [piece.astype(jnp.bfloat16) for piece in pieces_of(part)]
        sums = [jnp.dot(every, piece, preferred_element_type=jnp.float32) for piece in pieces]
        picked = sums[0] + sums[1] + sums[2]
        gathered[...] = picked.reshape(gathered.shape)


def esp_rows_of(first, count, own_ref, left_ref, right_ref, over_ref, near_charge, far_block):
    _, rows, basis = over_ref.shape
    near, far = near_charge.shape[1], far_block.shape[1]
    pick = own_rows(rows, basis, lax.axis_index("tile") * rows)
    quantities = [block_lanes(at) for at in range(4)]
    for frag in range(first, first + count):
        folded = jnp.zeros((basis, LANES), jnp.float32)
        for k in range(near):
            square = lax.dot_general(
                left_ref[frag],
                right_ref[frag, k],
                (((0,), (0,)), ((), ())),
                preferred_element_type=jnp.float32,
            )
            terms = lax.rsqrt(square) * near_charge[frag, k : k + 1, :]
            for start in range(0, basis, LANES):
                folded = folded + terms[:, start : start + LANES]
        blocks = jnp.zeros((PC, basis), jnp.float32)
        spots = [own_ref[axis, frag : frag + 1, :] for axis in range(3)]
        for m in range(far):
            row = far_block[frag, m : m + 1, :]
            x, y, z, charge = [
                jnp.sum(jnp.where(lanes, row, 0.0), axis=1, keepdims=True) for lanes in quantities
            ]
            total = (spots[0] - x) ** 2 + (spots[1] - y) ** 2 + (spots[2] - z) ** 2
            blocks = blocks + charge * lax.rsqrt(total + 1.0)
        potential = jnp.sum(folded.T, axis=0, keepdims=True) + jnp.sum(blocks, axis=0, keepdims=True)
        potential = (0.5 * SCREENING) * potential
        mine = jnp.sum(jnp.where(pick, potential, 0.0), axis=1, keepdims=True)
        yield frag, over_ref[frag] * (mine + potential)


def first_esp_kernel(charge_ref, near_hot, far_hot, *refs):
    inputs, (esp_ref, near_charge, far_block) = refs[:4], refs[4:]
    gather_charges(charge_ref, near_hot, far_hot, near_charge, far_block)
    for frag, rows in esp_rows_of(0, esp_ref.shape[0], *inputs, near_charge, far_block):
        esp_ref[frag] = rows


def last_esp_kernel(tiles, *refs):
    inputs, done_ref, chunks = refs[:6], refs[6], refs[7 : 7 + tiles]
    density_ref, esp_ref, rest_ref, sems = refs[7 + tiles :]
    share, done = chunks[0].shape[0], done_ref.shape[0]
    copies = [pltpu.make_async_copy(done_ref, esp_ref.at[pl.ds(0, done)], sems.at[tiles])]
    for shift in range(tiles):
        target = density_ref.at[pl.ds(partner(shift, tiles, -1) * share, share)]
        copies.append(pltpu.make_async_copy(chunks[shift], target, sems.at[shift]))
    for copy in copies:
        copy.start()
    rest = rest_ref.shape[0]
    for frag, rows in esp_rows_of(done, rest, *inputs):
        rest_ref[frag - done] = rows
    copies.append(pltpu.make_async_copy(rest_ref, esp_ref.at[pl.ds(done, rest)], sems.at[tiles + 1]))
    copies[-1].start()
    for copy in copies:
        copy.wait()


def call(kernel, outs, inputs, specs, scratch=(), cost=None, out_spec=VMEM):
    return pl.pallas_call(
        kernel,
        out_shape=outs,
        in_specs=specs,
        out_specs=[out_spec] * len(outs),
        scratch_shapes=list(scratch),
        cost_estimate=cost,
        compiler_params=pltpu.CompilerParams(vmem_limit_bytes=24 * 1024 * 1024),
    )(*inputs)


def exchanged(chunks):
    tiles = lax.axis_size("tile")
    places = tiles // 2
    moved = [chunks[0]]
    for shift in range(1, tiles):
        pairs = []
        for tile in range(tiles):
            half = tile // places if shift < places else 1 - tile // places
            pairs.append((tile, half * places + (tile + shift) % places))
        moved.append(lax.ppermute(chunks[shift], "tile", pairs))
    return moved


def neighbours(x, reach):
    peers, tiles = lax.axis_size("frag"), lax.axis_size("tile")
    found = []
    for step in range(1, reach + 1):
        pairs = []
        for low in range(peers - step):
            for tile in range(low // step % 2, tiles, 2):
                ends = low * tiles + tile, (low + step) * tiles + tile
                pairs += [ends, ends[::-1]]
        found.append(lax.ppermute(x, ("frag", "tile"), pairs))
    return found


def from_next_tile(x):
    tiles = lax.axis_size("tile")
    return lax.ppermute(x, "tile", [(tile, tile ^ 1) for tile in range(tiles)])


def per_device(
    core_fock,
    intersection,
    gamma_tile,
    charge_old,
    embed_old,
    core_pop,
    centres,
    frag_sizes,
    near_list,
    far_list,
):
    frag_dev, rows, basis = core_fock.shape
    tiles, peers = lax.axis_size("tile"), lax.axis_size("frag")
    devices, share = tiles * peers, frag_dev // tiles
    chunk = floats(share, rows, basis)
    places = jnp.transpose(centres, (1, 0, 2))
    inputs = (frag_sizes, charge_old, embed_old, core_pop, places, gamma_tile, intersection, core_fock)
    near_part = floats(2, share, rows, basis)
    far_part = floats(share, rows + 8, basis // 2)
    *sent, facts = call(
        functools.partial(half_fock_kernel, tiles),
        [near_part] * (tiles // 2) + [far_part] * (tiles // 2) + [floats(3 * share, basis)],
        [pltpu.with_memory_space_constraint(x, pltpu.HBM) for x in inputs],
        [HBM] * len(inputs),
        [pltpu.SMEM(frag_sizes.shape, jnp.int32)]
        + [pltpu.VMEM(x.shape, jnp.float32) for x in inputs[1:6]]
        + [pltpu.VMEM((frag_dev // 2, rows, width), jnp.float32) for width in (basis, basis, basis // 2, basis // 2)]
        + [pltpu.SemaphoreType.DMA((len(inputs) + 2,))],
    )
    sent = exchanged(sent)
    swaps = neighbours(places, -(-SPAN // frag_dev))
    *pieces, charges = call(
        functools.partial(density_kernel, tiles),
        [chunk] * tiles + [floats(devices, share, basis + LANES)],
        (facts, *sent),
        [VMEM] * (1 + tiles),
        [pltpu.VMEM((share, basis, basis), jnp.float32)] * 2,
        pl.CostEstimate(flops=0, bytes_accessed=0, transcendentals=0),
    )
    moved = exchanged(pieces)
    charges, swaps = lax.optimization_barrier((charges, swaps))
    sources = [places, *swaps, *[from_next_tile(x) for x in swaps]]
    charges = lax.all_to_all(charges, ("tile", "frag"), split_axis=0, concat_axis=0, tiled=True)
    near, far, frags = near_list.shape[1], far_list.shape[1], peers * frag_dev
    parts = call(
        functools.partial(geometry_kernel, len(sources)),
        [
            jax.ShapeDtypeStruct((frag_dev, DEPTH, basis), jnp.bfloat16),
            jax.ShapeDtypeStruct((frag_dev, near, DEPTH, basis), jnp.bfloat16),
            floats(frag_dev, near, frags),
            floats(frag_dev, far, frags),
        ],
        (near_list, far_list, places, *sources, pieces[0]),
        [SMEM, SMEM] + [VMEM] * (1 + len(sources)) + [ANY],
        [
            pltpu.VMEM((frag_dev, DEPTH, basis), jnp.float32),
            pltpu.VMEM((len(sources) * frag_dev, DEPTH, basis), jnp.float32),
        ],
        pl.CostEstimate(flops=0, bytes_accessed=0, transcendentals=0),
    )
    left, right, near_hot, far_hot = parts
    inputs = (places, left, right, intersection)
    done = frag_dev * 5 // 8
    rest = frag_dev - done
    esp_rows, near_charge, far_block = call(
        first_esp_kernel,
        [floats(done, rows, basis), floats(frag_dev, near, basis), floats(frag_dev, far, LANES)],
        (charges, near_hot, far_hot, *inputs),
        [VMEM] * 7,
        cost=pl.CostEstimate(flops=0, bytes_accessed=0, transcendentals=0),
    )
    density, esp_matrix = call(
        functools.partial(last_esp_kernel, tiles),
        [floats(frag_dev, rows, basis)] * 2,
        (*inputs, near_charge, far_block, esp_rows, *moved),
        [VMEM] * (7 + tiles),
        [pltpu.VMEM((rest, rows, basis), jnp.float32), pltpu.SemaphoreType.DMA((tiles + 2,))],
        pl.CostEstimate(flops=0, bytes_accessed=0, transcendentals=0),
        HBM,
    )
    return (density, esp_matrix)


def solution(mesh):
    in_specs = (
        P("frag", "tile", None),
        P("frag", "tile", None),
        P("frag", "tile", None),
        P("frag", None),
        P("frag", None),
        P("frag", None),
        P("frag", None, None),
        P("frag"),
        P("frag", None),
        P("frag", None),
    )
    out_specs = (P("frag", "tile", None), P("frag", "tile", None))
    return jax.shard_map(
        per_device, mesh=mesh, in_specs=in_specs, out_specs=out_specs, check_vma=False
    )
```

```python
import functools

import jax
import jax.numpy as jnp
from jax import lax
from jax.experimental import pallas as pl
from jax.experimental.pallas import tpu as pltpu
from jax.sharding import PartitionSpec as P

PC = 8
ITERS = 12
SCREENING = 0.25
SPAN = 8
LANES = 128
CHUNK = 128
COARSE = jnp.float8_e4m3fn
WHOLE_SCALE = 256.0
REST_SCALE = 65536.0
VMEM = pl.BlockSpec(memory_space=pltpu.VMEM)
SMEM = pl.BlockSpec(memory_space=pltpu.SMEM)
HBM = pl.BlockSpec(memory_space=pltpu.HBM)
ANY = pl.BlockSpec(memory_space=pl.ANY)


def floats(*shape):
    return jax.ShapeDtypeStruct(shape, jnp.float32)


def block_mask(basis):
    group = basis // PC
    block = lax.broadcasted_iota(jnp.int32, (PC, basis), 0)
    column = lax.broadcasted_iota(jnp.int32, (PC, basis), 1)
    return (column >= block * group) & (column < (block + 1) * group)


def block_lanes(at):
    block = lax.broadcasted_iota(jnp.int32, (PC, LANES), 0)
    lane = lax.broadcasted_iota(jnp.int32, (PC, LANES), 1)
    return lane == block + at * PC


def block_row(rows, first):
    mask = block_mask(rows[0].shape[1])
    total = jnp.zeros((PC, LANES), jnp.float32)
    for at, row in enumerate(rows):
        sums = jnp.sum(jnp.where(mask, row, 0.0), axis=1, keepdims=True)
        total = total + jnp.where(block_lanes(first + at), sums, 0.0)
    return jnp.sum(total, axis=0, keepdims=True)


def own_rows(rows, basis, first):
    row = lax.broadcasted_iota(jnp.int32, (rows, basis), 0)
    column = lax.broadcasted_iota(jnp.int32, (rows, basis), 1)
    return column == row + first


def seat(tiles):
    places = tiles // 2
    tile_at = lax.axis_index("tile")
    return tile_at // places, lax.rem(tile_at, places), places


def partner(shift, tiles, sign=1):
    half, place, places = seat(tiles)
    other = half if shift < places else 1 - half
    return other * places + lax.rem(place + places + sign * (shift % places), places)


def swapped(half, x):
    middle = x.shape[-1] // 2
    left, right = x[..., :middle], x[..., middle:]
    return jnp.where(half == 0, left, right), jnp.where(half == 0, right, left)


def half_fock_kernel(tiles, *refs):
    inputs, outs, buffers, sems = refs[:8], refs[8:-11], refs[-11:-1], refs[-1]
    sizes_ref, charge_ref, embed_ref, pop_ref, place_ref, gamma_ref = buffers[:6]
    over_near, core_near, over_there, core_there = buffers[6:]
    half, place_at, places = seat(tiles)
    count, rows, basis = over_near.shape
    share, middle = count // places, basis // 2
    here, there = pl.ds(half * count, count), pl.ds((1 - half) * count, count)
    columns = pl.ds(pl.multiple_of(half * middle, middle), middle)
    sources = [*inputs[:6], *[source.at[here] for source in inputs[6:]]]
    sources += [source.at[there, :, columns] for source in inputs[6:]]
    copies = [
        pltpu.make_async_copy(source, buffer, sems.at[at])
        for at, (source, buffer) in enumerate(zip(sources, buffers))
    ]
    for copy in copies:
        copy.start()
    for copy in copies:
        copy.wait()
    pick = own_rows(rows, basis, lax.axis_index("tile") * rows)
    pick_half = own_rows(rows, middle, place_at * rows)
    row = lax.broadcasted_iota(jnp.int32, (rows, middle), 0) + lax.axis_index("tile") * rows
    column = lax.broadcasted_iota(jnp.int32, (rows, middle), 1)
    mine, others = column + half * middle, column + (1 - half) * middle
    lane = lax.broadcasted_iota(jnp.int32, (1, basis), 1)
    for shift in range(tiles):
        target = partner(shift, tiles)
        for spot in range(share):
            frag = target * share + spot
            size = sizes_ref[frag]
            terms = gamma_ref[frag] * charge_ref[pl.ds(frag, 1), :]
            terms = terms + jnp.where(pick, embed_ref[pl.ds(frag, 1), :], 0.0)
            field = jnp.sum(terms, axis=1, keepdims=True)
            at = lax.rem(place_at + shift, places) * share + spot
            if shift < places:
                core, core_far = swapped(half, core_near[at])
                over, over_far = swapped(half, over_near[at])
            else:
                core, over = core_there[at], over_there[at]
            inside = (row < size) & (mine < size)
            core, over = jnp.where(inside, core, 0.0), jnp.where(inside, over, 0.0)
            out = outs[shift]
            if shift < places:
                inside = (row < size) & (others < size)
                over_far = jnp.where(inside, over_far, 0.0)
                out[0, spot, :, :middle] = 0.5 * (core + over * field)
                out[0, spot, :, middle:] = jnp.where(inside, core_far, 0.0) + over_far * (0.5 * field)
                out[1, spot, :, :middle] = over
                out[1, spot, :, middle:] = over_far
            else:
                out[spot, :rows] = jnp.where(mine >= row, core, over)
                field_row = jnp.sum(jnp.where(pick_half, field, 0.0), axis=0, keepdims=True)
                diagonal = jnp.sum(jnp.where(pick_half, over, 0.0), axis=0, keepdims=True)
                rest = jnp.zeros((out.shape[1] - rows - 2, middle), jnp.float32)
                out[spot, rows:] = jnp.concatenate([field_row, diagonal, rest], axis=0)
            if shift == 0:
                facts = outs[-1]
                idle = swapped(half, (lane >= size).astype(jnp.float32))
                facts[spot : spot + 1, :middle] = idle[0]
                facts[spot : spot + 1, middle:] = idle[1]
                facts[share + spot : share + spot + 1, :] = pop_ref[pl.ds(frag, 1), :]
                spots = [place_ref[axis, pl.ds(frag, 1), :] for axis in range(3)]
                means = block_row(spots, 4 * spot) * (PC / basis)
                facts[2 * share + spot : 2 * share + spot + 1, :LANES] = means


def split(x):
    high = x.astype(jnp.bfloat16)
    rest = (x - high.astype(jnp.float32)).astype(jnp.bfloat16)
    coarse = (high * jnp.bfloat16(WHOLE_SCALE)).astype(COARSE)
    return high, coarse, (rest * jnp.bfloat16(REST_SCALE)).astype(COARSE)


def product(left, right):
    dot = functools.partial(jnp.dot, preferred_element_type=jnp.float32)
    rest = dot(left[1], right[2]) + dot(left[2], right[1])
    return dot(left[0], right[0]) + rest * (1.0 / (WHOLE_SCALE * REST_SCALE))


def density_kernel(tiles, facts_ref, *refs):
    places = tiles // 2
    near_parts, far_parts = refs[:places], refs[places:tiles]
    chunks, charge_ref = refs[tiles : 2 * tiles], refs[2 * tiles]
    x_ref, s_ref = refs[2 * tiles + 1 :]
    half, place_at, _ = seat(tiles)
    _, share, rows, basis = near_parts[0].shape
    middle = basis // 2
    for shift in range(places):
        source = lax.rem(place_at + places - shift, places) * rows
        span = pl.ds(pl.multiple_of(source, rows), rows)
        far_span = pl.ds(pl.multiple_of(source + middle, rows), rows)
        for spot in range(share):
            x_ref[spot, span, :] = near_parts[shift][0, spot]
            s_ref[spot, span, :] = near_parts[shift][1, spot]
            x_ref[spot, far_span, middle:] = far_parts[shift][spot, :rows]
    row = lax.broadcasted_iota(jnp.int32, (basis, basis), 0)
    column = lax.broadcasted_iota(jnp.int32, (basis, basis), 1)
    near, far = slice(0, middle), slice(middle, basis)
    for spot in range(share):
        extra = far_parts[0][spot, rows:]
        for part in far_parts[1:]:
            extra = extra + part[spot, rows:]
        field = extra[:1]
        corner, packed = x_ref[spot, near, near], x_ref[spot, far, far]
        turned = packed.T
        down, along = row[near, near], column[near, near]
        over = jnp.where(along < down, packed, jnp.where(along == down, extra[1:2], turned))
        last = 0.5 * (jnp.where(along >= down, packed, turned) + over * field)
        s_ref[spot, far, far] = over
        side = x_ref[spot, near, far] + s_ref[spot, near, far] * (0.5 * field)
        corner, last = corner + corner.T, last + last.T
        total = corner * corner + last * last + 2.0 * (side * side)
        scale = 1.0 / jnp.sqrt(jnp.sum(total, keepdims=True) + 1e-06)
        idle = jnp.where(row == column, facts_ref[spot : spot + 1, :], 0.0)
        x_ref[spot, near, near] = corner * scale + idle[near, near]
        x_ref[spot, near, far] = side * scale
        x_ref[spot, far, near] = side.T * scale
        x_ref[spot, far, far] = last * scale + idle[far, far]

    chunk = min(CHUNK, basis)
    spans = [(spot, slice(at, at + chunk)) for spot in range(share) for at in range(0, basis, chunk)]
    for _ in range(ITERS):
        estimates = [x_ref[spot] for spot in range(share)]
        parts = [split(x) for x in estimates]
        squares = []
        for spot, span in spans:
            left = [part[span] for part in parts[spot]]
            squares.append(split(0.5 * product(left, parts[spot])))
        for square, (spot, span) in zip(squares, spans):
            x_ref[spot, span] = 1.5 * estimates[spot][span] - product(square, parts[spot])

    sent, total = [], jnp.zeros((1, LANES), jnp.float32)
    for spot in range(share):
        density = jnp.where(row == column, 0.5, 0.0) - 0.5 * x_ref[spot]
        x_ref[spot] = density
        side = density[near, far] * s_ref[spot, near, far]
        corner = density[near, near] * s_ref[spot, near, near] + side.T
        last = density[far, far] * s_ref[spot, far, far] + side
        sums = [jnp.sum(block, axis=0, keepdims=True) for block in (corner, last)]
        charge = jnp.concatenate(swapped(half, jnp.concatenate(sums, axis=1)), axis=1)
        charge = charge - facts_ref[share + spot : share + spot + 1, :]
        blocks = block_row([charge], 4 * spot + 3) + facts_ref[2 * share + spot : 2 * share + spot + 1, :LANES]
        sent.append(charge)
        total = total + blocks
    whole = jnp.concatenate([*sent, total], axis=1)
    charge_ref[...] = jnp.broadcast_to(whole[None], (charge_ref.shape[0],) + whole.shape)
    for shift in range(tiles):
        first = partner(shift, tiles) % places * rows + (0 if shift < places else middle)
        span = pl.ds(pl.multiple_of(first, rows), rows)
        for spot in range(share):
            left, right = swapped(half, x_ref[spot, span, :])
            chunks[shift][spot, :, :middle] = left
            chunks[shift][spot, :, middle:] = right


def pieces_of(x):
    out = []
    for _ in range(3):
        piece = x.astype(jnp.bfloat16).astype(jnp.float32)
        out.append(piece)
        x = x - piece
    return out


PAIRS = ((0, 0), (0, 1), (1, 0), (0, 2), (1, 1), (2, 0))
DEPTH = 32


def geometry_kernel(around, near_ref, far_ref, own_ref, *refs):
    sources = refs[:around]
    left_out, right_out, near_hot, far_hot, side_ref, table_side = refs[-6:]
    frag_dev, near = near_ref.shape
    far = far_ref.shape[1]
    basis = own_ref.shape[2]
    lane = lax.broadcasted_iota(jnp.int32, (1, near_hot.shape[2]), 1)
    ones = jnp.ones((frag_dev, basis), jnp.float32)
    frag_at, reach = lax.axis_index("frag"), around // 2
    tiles, peers = lax.axis_size("tile"), lax.axis_size("frag")
    share = frag_dev // tiles

    def row_of(frag):
        inside = lax.rem(frag, frag_dev)
        return (lax.rem(inside, share) * tiles + inside // share) * peers + frag // frag_dev

    first_frag = (frag_at - reach) * frag_dev

    def fill(target, first, place_ref, scale, extra, which):
        places = [place_ref[axis] for axis in range(3)]
        rows = []
        for place in places:
            parts = pieces_of(place)
            rows += [scale * parts[pair[which]] for pair in PAIRS]
        norm = places[0] * places[0] + places[1] * places[1] + places[2] * places[2] + extra
        sides = [pieces_of(norm), [ones] * 3]
        rows += sides[which] + sides[1 - which]
        rows += [0.0 * ones] * (DEPTH - len(rows))
        for at, row in enumerate(rows):
            for frag in range(frag_dev):
                target[first + frag, at : at + 1, :] = row[frag : frag + 1, :]

    fill(side_ref, 0, own_ref, -2.0, 1.0, 0)
    left_out[...] = side_ref[...].astype(jnp.bfloat16)
    fill(table_side, reach * frag_dev, sources[0], 1.0, 0.0, 1)
    for at in range(1, around):
        step = (at - 1) % reach + 1
        side = lax.rem(frag_at // step + lax.axis_index("tile") + (at - 1) // reach, 2)
        spot = reach + step * (1 - 2 * side)
        fill(table_side, spot * frag_dev, sources[at], 1.0, 0.0, 1)
    for frag in range(frag_dev):
        for k in range(near):
            other = near_ref[frag, k]
            near_hot[frag, k : k + 1, :] = (lane == row_of(other)).astype(jnp.float32)
            right_out[frag, k] = table_side[other - first_frag].astype(jnp.bfloat16)
        for m in range(far):
            far_hot[frag, m : m + 1, :] = (lane == row_of(far_ref[frag, m])).astype(jnp.float32)


def gather_charges(charge_ref, near_hot, far_hot, near_charge, far_block):
    basis = near_charge.shape[2]
    rows = charge_ref[...].reshape(charge_ref.shape[0], charge_ref.shape[2])
    share = rows.shape[1] // basis
    tail, wide = rows[:, share * basis :], 4 * PC
    charges = [rows[:, spot * basis : (spot + 1) * basis] for spot in range(share)]
    blocks = [tail]
    for spot in range(1, share):
        blocks.append(jnp.concatenate([tail[:, spot * wide :], tail[:, : spot * wide]], axis=1))
    for hot, gathered, part in (
        (near_hot, near_charge, jnp.concatenate(charges, axis=0)),
        (far_hot, far_block, jnp.concatenate(blocks, axis=0)),
    ):
        every = hot[...].reshape(-1, hot.shape[2])
        picked = jnp.dot(every, part, precision=lax.Precision.HIGHEST, preferred_element_type=jnp.float32)
        gathered[...] = picked.reshape(gathered.shape)


def esp_rows_of(first, count, own_ref, left_ref, right_ref, over_ref, near_charge, far_block):
    _, rows, basis = over_ref.shape
    near, far = near_charge.shape[1], far_block.shape[1]
    pick = own_rows(rows, basis, lax.axis_index("tile") * rows)
    quantities = [block_lanes(at) for at in range(4)]
    for frag in range(first, first + count):
        folded = jnp.zeros((basis, LANES), jnp.float32)
        for k in range(near):
            square = lax.dot_general(
                left_ref[frag],
                right_ref[frag, k],
                (((0,), (0,)), ((), ())),
                preferred_element_type=jnp.float32,
            )
            terms = lax.rsqrt(square) * near_charge[frag, k : k + 1, :]
            for start in range(0, basis, LANES):
                folded = folded + terms[:, start : start + LANES]
        blocks = jnp.zeros((PC, basis), jnp.float32)
        spots = [own_ref[axis, frag : frag + 1, :] for axis in range(3)]
        for m in range(far):
            row = far_block[frag, m : m + 1, :]
            x, y, z, charge = [
                jnp.sum(jnp.where(lanes, row, 0.0), axis=1, keepdims=True) for lanes in quantities
            ]
            total = (spots[0] - x) ** 2 + (spots[1] - y) ** 2 + (spots[2] - z) ** 2
            blocks = blocks + charge * lax.rsqrt(total + 1.0)
        potential = jnp.sum(folded.T, axis=0, keepdims=True) + jnp.sum(blocks, axis=0, keepdims=True)
        potential = (0.5 * SCREENING) * potential
        mine = jnp.sum(jnp.where(pick, potential, 0.0), axis=1, keepdims=True)
        yield frag, over_ref[frag] * (mine + potential)


def first_esp_kernel(charge_ref, near_hot, far_hot, *refs):
    inputs, (esp_ref, near_charge, far_block) = refs[:4], refs[4:]
    gather_charges(charge_ref, near_hot, far_hot, near_charge, far_block)
    for frag, rows in esp_rows_of(0, esp_ref.shape[0], *inputs, near_charge, far_block):
        esp_ref[frag] = rows


def last_esp_kernel(tiles, *refs):
    inputs, done_ref, chunks = refs[:6], refs[6], refs[7 : 7 + tiles]
    density_ref, esp_ref, rest_ref, sems = refs[7 + tiles :]
    share, done = chunks[0].shape[0], done_ref.shape[0]
    copies = [pltpu.make_async_copy(done_ref, esp_ref.at[pl.ds(0, done)], sems.at[tiles])]
    for shift in range(tiles):
        target = density_ref.at[pl.ds(partner(shift, tiles, -1) * share, share)]
        copies.append(pltpu.make_async_copy(chunks[shift], target, sems.at[shift]))
    for copy in copies:
        copy.start()
    rest = rest_ref.shape[0]
    for frag, rows in esp_rows_of(done, rest, *inputs):
        rest_ref[frag - done] = rows
    copies.append(pltpu.make_async_copy(rest_ref, esp_ref.at[pl.ds(done, rest)], sems.at[tiles + 1]))
    copies[-1].start()
    for copy in copies:
        copy.wait()


def call(kernel, outs, inputs, specs, scratch=(), cost=None, out_spec=VMEM):
    return pl.pallas_call(
        kernel,
        out_shape=outs,
        in_specs=specs,
        out_specs=[out_spec] * len(outs),
        scratch_shapes=list(scratch),
        cost_estimate=cost,
        compiler_params=pltpu.CompilerParams(vmem_limit_bytes=24 * 1024 * 1024),
    )(*inputs)


def exchanged(chunks):
    tiles = lax.axis_size("tile")
    places = tiles // 2
    moved = [chunks[0]]
    for shift in range(1, tiles):
        pairs = []
        for tile in range(tiles):
            half = tile // places if shift < places else 1 - tile // places
            pairs.append((tile, half * places + (tile + shift) % places))
        moved.append(lax.ppermute(chunks[shift], "tile", pairs))
    return moved


def neighbours(x, reach):
    peers, tiles = lax.axis_size("frag"), lax.axis_size("tile")
    found = []
    for step in range(1, reach + 1):
        pairs = []
        for low in range(peers - step):
            for tile in range(low // step % 2, tiles, 2):
                ends = low * tiles + tile, (low + step) * tiles + tile
                pairs += [ends, ends[::-1]]
        found.append(lax.ppermute(x, ("frag", "tile"), pairs))
    return found


def from_next_tile(x):
    tiles = lax.axis_size("tile")
    return lax.ppermute(x, "tile", [(tile, tile ^ 1) for tile in range(tiles)])


def per_device(
    core_fock,
    intersection,
    gamma_tile,
    charge_old,
    embed_old,
    core_pop,
    centres,
    frag_sizes,
    near_list,
    far_list,
):
    frag_dev, rows, basis = core_fock.shape
    tiles, peers = lax.axis_size("tile"), lax.axis_size("frag")
    devices, share = tiles * peers, frag_dev // tiles
    chunk = floats(share, rows, basis)
    places = jnp.transpose(centres, (1, 0, 2))
    inputs = (frag_sizes, charge_old, embed_old, core_pop, places, gamma_tile, intersection, core_fock)
    near_part = floats(2, share, rows, basis)
    far_part = floats(share, rows + 8, basis // 2)
    *sent, facts = call(
        functools.partial(half_fock_kernel, tiles),
        [near_part] * (tiles // 2) + [far_part] * (tiles // 2) + [floats(3 * share, basis)],
        [pltpu.with_memory_space_constraint(x, pltpu.HBM) for x in inputs],
        [HBM] * len(inputs),
        [pltpu.SMEM(frag_sizes.shape, jnp.int32)]
        + [pltpu.VMEM(x.shape, jnp.float32) for x in inputs[1:6]]
        + [pltpu.VMEM((frag_dev // 2, rows, width), jnp.float32) for width in (basis, basis, basis // 2, basis // 2)]
        + [pltpu.SemaphoreType.DMA((len(inputs) + 2,))],
    )
    sent = exchanged(sent)
    swaps = neighbours(places, -(-SPAN // frag_dev))
    *pieces, charges = call(
        functools.partial(density_kernel, tiles),
        [chunk] * tiles + [floats(devices, 1, share * basis + LANES)],
        (facts, *sent),
        [VMEM] * (1 + tiles),
        [pltpu.VMEM((share, basis, basis), jnp.float32)] * 2,
        pl.CostEstimate(flops=0, bytes_accessed=0, transcendentals=0),
    )
    moved = exchanged(pieces)
    charges, swaps = lax.optimization_barrier((charges, swaps))
    sources = [places, *swaps, *[from_next_tile(x) for x in swaps]]
    charges = lax.all_to_all(charges, ("tile", "frag"), split_axis=0, concat_axis=0, tiled=True)
    near, far, frags = near_list.shape[1], far_list.shape[1], peers * frag_dev
    parts = call(
        functools.partial(geometry_kernel, len(sources)),
        [
            jax.ShapeDtypeStruct((frag_dev, DEPTH, basis), jnp.bfloat16),
            jax.ShapeDtypeStruct((frag_dev, near, DEPTH, basis), jnp.bfloat16),
            floats(frag_dev, near, frags),
            floats(frag_dev, far, frags),
        ],
        (near_list, far_list, places, *sources, pieces[0]),
        [SMEM, SMEM] + [VMEM] * (1 + len(sources)) + [ANY],
        [
            pltpu.VMEM((frag_dev, DEPTH, basis), jnp.float32),
            pltpu.VMEM((len(sources) * frag_dev, DEPTH, basis), jnp.float32),
        ],
        pl.CostEstimate(flops=0, bytes_accessed=0, transcendentals=0),
    )
    left, right, near_hot, far_hot = parts
    inputs = (places, left, right, intersection)
    done = frag_dev * 3 // 4
    rest = frag_dev - done
    esp_rows, near_charge, far_block = call(
        first_esp_kernel,
        [floats(done, rows, basis), floats(frag_dev, near, basis), floats(frag_dev, far, LANES)],
        (charges, near_hot, far_hot, *inputs),
        [VMEM] * 7,
        cost=pl.CostEstimate(flops=0, bytes_accessed=0, transcendentals=0),
    )
    density, esp_matrix = call(
        functools.partial(last_esp_kernel, tiles),
        [floats(frag_dev, rows, basis)] * 2,
        (*inputs, near_charge, far_block, esp_rows, *moved),
        [VMEM] * (7 + tiles),
        [pltpu.VMEM((rest, rows, basis), jnp.float32), pltpu.SemaphoreType.DMA((tiles + 2,))],
        pl.CostEstimate(flops=0, bytes_accessed=0, transcendentals=0),
        HBM,
    )
    return (density, esp_matrix)


def solution(mesh):
    in_specs = (
        P("frag", "tile", None),
        P("frag", "tile", None),
        P("frag", "tile", None),
        P("frag", None),
        P("frag", None),
        P("frag", None),
        P("frag", None, None),
        P("frag"),
        P("frag", None),
        P("frag", None),
    )
    out_specs = (P("frag", "tile", None), P("frag", "tile", None))
    return jax.shard_map(
        per_device, mesh=mesh, in_specs=in_specs, out_specs=out_specs, check_vma=False
    )
```

```python
import functools

import jax
import jax.numpy as jnp
from jax import lax
from jax.experimental import pallas as pl
from jax.experimental.pallas import tpu as pltpu
from jax.sharding import PartitionSpec as P

PC = 8
ITERS = 12
SCREENING = 0.25
SPAN = 8
LANES = 128
CHUNK = 128
COARSE = jnp.float8_e4m3fn
WHOLE_SCALE = 256.0
REST_SCALE = 65536.0
VMEM = pl.BlockSpec(memory_space=pltpu.VMEM)
SMEM = pl.BlockSpec(memory_space=pltpu.SMEM)
HBM = pl.BlockSpec(memory_space=pltpu.HBM)
ANY = pl.BlockSpec(memory_space=pl.ANY)


def floats(*shape):
    return jax.ShapeDtypeStruct(shape, jnp.float32)


def block_mask(basis):
    group = basis // PC
    block = lax.broadcasted_iota(jnp.int32, (PC, basis), 0)
    column = lax.broadcasted_iota(jnp.int32, (PC, basis), 1)
    return (column >= block * group) & (column < (block + 1) * group)


def block_lanes(at):
    block = lax.broadcasted_iota(jnp.int32, (PC, LANES), 0)
    lane = lax.broadcasted_iota(jnp.int32, (PC, LANES), 1)
    return lane == block + at * PC


def block_row(rows, first):
    mask = block_mask(rows[0].shape[1])
    total = jnp.zeros((PC, LANES), jnp.float32)
    for at, row in enumerate(rows):
        sums = jnp.sum(jnp.where(mask, row, 0.0), axis=1, keepdims=True)
        total = total + jnp.where(block_lanes(first + at), sums, 0.0)
    return jnp.sum(total, axis=0, keepdims=True)


def own_rows(rows, basis, first):
    row = lax.broadcasted_iota(jnp.int32, (rows, basis), 0)
    column = lax.broadcasted_iota(jnp.int32, (rows, basis), 1)
    return column == row + first


def seat(tiles):
    places = tiles // 2
    tile_at = lax.axis_index("tile")
    return tile_at // places, lax.rem(tile_at, places), places


def partner(shift, tiles, sign=1):
    half, place, places = seat(tiles)
    other = half if shift < places else 1 - half
    return other * places + lax.rem(place + places + sign * (shift % places), places)


def swapped(half, x):
    middle = x.shape[-1] // 2
    left, right = x[..., :middle], x[..., middle:]
    return jnp.where(half == 0, left, right), jnp.where(half == 0, right, left)


def half_fock_kernel(tiles, *refs):
    inputs, outs, buffers, sems = refs[:8], refs[8:-11], refs[-11:-1], refs[-1]
    sizes_ref, charge_ref, embed_ref, pop_ref, place_ref, gamma_ref = buffers[:6]
    over_near, core_near, over_there, core_there = buffers[6:]
    half, place_at, places = seat(tiles)
    count, rows, basis = over_near.shape
    share, middle = count // places, basis // 2
    here, there = pl.ds(half * count, count), pl.ds((1 - half) * count, count)
    columns = pl.ds(pl.multiple_of(half * middle, middle), middle)
    sources = [*inputs[:6], *[source.at[here] for source in inputs[6:]]]
    sources += [source.at[there, :, columns] for source in inputs[6:]]
    copies = [
        pltpu.make_async_copy(source, buffer, sems.at[at])
        for at, (source, buffer) in enumerate(zip(sources, buffers))
    ]
    for copy in copies:
        copy.start()
    for copy in copies:
        copy.wait()
    pick = own_rows(rows, basis, lax.axis_index("tile") * rows)
    pick_half = own_rows(rows, middle, place_at * rows)
    row = lax.broadcasted_iota(jnp.int32, (rows, middle), 0) + lax.axis_index("tile") * rows
    column = lax.broadcasted_iota(jnp.int32, (rows, middle), 1)
    mine, others = column + half * middle, column + (1 - half) * middle
    lane = lax.broadcasted_iota(jnp.int32, (1, basis), 1)
    for shift in range(tiles):
        target = partner(shift, tiles)
        for spot in range(share):
            frag = target * share + spot
            size = sizes_ref[frag]
            terms = gamma_ref[frag] * charge_ref[pl.ds(frag, 1), :]
            terms = terms + jnp.where(pick, embed_ref[pl.ds(frag, 1), :], 0.0)
            field = jnp.sum(terms, axis=1, keepdims=True)
            at = lax.rem(place_at + shift, places) * share + spot
            if shift < places:
                core, core_far = swapped(half, core_near[at])
                over, over_far = swapped(half, over_near[at])
            else:
                core, over = core_there[at], over_there[at]
            inside = (row < size) & (mine < size)
            core, over = jnp.where(inside, core, 0.0), jnp.where(inside, over, 0.0)
            out = outs[shift]
            if shift < places:
                inside = (row < size) & (others < size)
                over_far = jnp.where(inside, over_far, 0.0)
                out[0, spot, :, :middle] = 0.5 * (core + over * field)
                out[0, spot, :, middle:] = jnp.where(inside, core_far, 0.0) + over_far * (0.5 * field)
                out[1, spot, :, :middle] = over
                out[1, spot, :, middle:] = over_far
            else:
                out[spot, :rows] = jnp.where(mine >= row, core, over)
                field_row = jnp.sum(jnp.where(pick_half, field, 0.0), axis=0, keepdims=True)
                diagonal = jnp.sum(jnp.where(pick_half, over, 0.0), axis=0, keepdims=True)
                rest = jnp.zeros((out.shape[1] - rows - 2, middle), jnp.float32)
                out[spot, rows:] = jnp.concatenate([field_row, diagonal, rest], axis=0)
            if shift == 0:
                facts = outs[-1]
                idle = swapped(half, (lane >= size).astype(jnp.float32))
                facts[spot : spot + 1, :middle] = idle[0]
                facts[spot : spot + 1, middle:] = idle[1]
                facts[share + spot : share + spot + 1, :] = pop_ref[pl.ds(frag, 1), :]
                spots = [place_ref[axis, pl.ds(frag, 1), :] for axis in range(3)]
                means = block_row(spots, 4 * spot) * (PC / basis)
                facts[2 * share + spot : 2 * share + spot + 1, :LANES] = means


def split(x):
    high = x.astype(jnp.bfloat16)
    rest = (x - high.astype(jnp.float32)).astype(jnp.bfloat16)
    coarse = (high * jnp.bfloat16(WHOLE_SCALE)).astype(COARSE)
    return high, coarse, (rest * jnp.bfloat16(REST_SCALE)).astype(COARSE)


def product(left, right):
    dot = functools.partial(jnp.dot, preferred_element_type=jnp.float32)
    rest = dot(left[1], right[2]) + dot(left[2], right[1])
    return dot(left[0], right[0]) + rest * (1.0 / (WHOLE_SCALE * REST_SCALE))


def density_kernel(tiles, facts_ref, *refs):
    places = tiles // 2
    near_parts, far_parts = refs[:places], refs[places:tiles]
    chunks, charge_ref = refs[tiles : 2 * tiles], refs[2 * tiles]
    x_ref, s_ref = refs[2 * tiles + 1 :]
    half, place_at, _ = seat(tiles)
    _, share, rows, basis = near_parts[0].shape
    middle = basis // 2
    for shift in range(places):
        source = lax.rem(place_at + places - shift, places) * rows
        span = pl.ds(pl.multiple_of(source, rows), rows)
        far_span = pl.ds(pl.multiple_of(source + middle, rows), rows)
        for spot in range(share):
            x_ref[spot, span, :] = near_parts[shift][0, spot]
            s_ref[spot, span, :] = near_parts[shift][1, spot]
            x_ref[spot, far_span, middle:] = far_parts[shift][spot, :rows]
    row = lax.broadcasted_iota(jnp.int32, (basis, basis), 0)
    column = lax.broadcasted_iota(jnp.int32, (basis, basis), 1)
    near, far = slice(0, middle), slice(middle, basis)
    for spot in range(share):
        extra = far_parts[0][spot, rows:]
        for part in far_parts[1:]:
            extra = extra + part[spot, rows:]
        field = extra[:1]
        corner, packed = x_ref[spot, near, near], x_ref[spot, far, far]
        turned = packed.T
        down, along = row[near, near], column[near, near]
        over = jnp.where(along < down, packed, jnp.where(along == down, extra[1:2], turned))
        last = 0.5 * (jnp.where(along >= down, packed, turned) + over * field)
        s_ref[spot, far, far] = over
        side = x_ref[spot, near, far] + s_ref[spot, near, far] * (0.5 * field)
        corner, last = corner + corner.T, last + last.T
        total = corner * corner + last * last + 2.0 * (side * side)
        scale = 1.0 / jnp.sqrt(jnp.sum(total, keepdims=True) + 1e-06)
        idle = jnp.where(row == column, facts_ref[spot : spot + 1, :], 0.0)
        x_ref[spot, near, near] = corner * scale + idle[near, near]
        x_ref[spot, near, far] = side * scale
        x_ref[spot, far, near] = side.T * scale
        x_ref[spot, far, far] = last * scale + idle[far, far]

    chunk = min(CHUNK, basis)
    spans = [(spot, slice(at, at + chunk)) for spot in range(share) for at in range(0, basis, chunk)]
    for _ in range(ITERS):
        estimates = [x_ref[spot] for spot in range(share)]
        parts = [split(x) for x in estimates]
        squares = []
        for spot, span in spans:
            left = [part[span] for part in parts[spot]]
            squares.append(split(0.5 * product(left, parts[spot])))
        for square, (spot, span) in zip(squares, spans):
            x_ref[spot, span] = 1.5 * estimates[spot][span] - product(square, parts[spot])

    sent, total = [], jnp.zeros((1, LANES), jnp.float32)
    for spot in range(share):
        density = jnp.where(row == column, 0.5, 0.0) - 0.5 * x_ref[spot]
        x_ref[spot] = density
        side = density[near, far] * s_ref[spot, near, far]
        corner = density[near, near] * s_ref[spot, near, near] + side.T
        last = density[far, far] * s_ref[spot, far, far] + side
        sums = [jnp.sum(block, axis=0, keepdims=True) for block in (corner, last)]
        charge = jnp.concatenate(swapped(half, jnp.concatenate(sums, axis=1)), axis=1)
        charge = charge - facts_ref[share + spot : share + spot + 1, :]
        blocks = block_row([charge], 4 * spot + 3) + facts_ref[2 * share + spot : 2 * share + spot + 1, :LANES]
        sent.append(charge)
        total = total + blocks
    whole = jnp.concatenate([*sent, total], axis=1)
    charge_ref[...] = jnp.broadcast_to(whole[None], (charge_ref.shape[0],) + whole.shape)
    for shift in range(tiles):
        first = partner(shift, tiles) % places * rows + (0 if shift < places else middle)
        span = pl.ds(pl.multiple_of(first, rows), rows)
        for spot in range(share):
            left, right = swapped(half, x_ref[spot, span, :])
            chunks[shift][spot, :, :middle] = left
            chunks[shift][spot, :, middle:] = right


def pieces_of(x):
    out = []
    for _ in range(3):
        piece = x.astype(jnp.bfloat16).astype(jnp.float32)
        out.append(piece)
        x = x - piece
    return out


PAIRS = ((0, 0), (0, 1), (1, 0), (0, 2), (1, 1), (2, 0))
DEPTH = 32


def geometry_kernel(around, near_ref, far_ref, own_ref, *refs):
    sources = refs[:around]
    left_out, right_out, near_hot, far_hot, side_ref, table_side = refs[-6:]
    frag_dev, near = near_ref.shape
    far = far_ref.shape[1]
    basis = own_ref.shape[2]
    lane = lax.broadcasted_iota(jnp.int32, (1, near_hot.shape[2]), 1)
    ones = jnp.ones((frag_dev, basis), jnp.float32)
    frag_at, reach = lax.axis_index("frag"), around // 2
    tiles, peers = lax.axis_size("tile"), lax.axis_size("frag")
    share = frag_dev // tiles

    def row_of(frag):
        inside = lax.rem(frag, frag_dev)
        return (lax.rem(inside, share) * tiles + inside // share) * peers + frag // frag_dev

    first_frag = (frag_at - reach) * frag_dev

    def fill(target, first, place_ref, scale, extra, which):
        places = [place_ref[axis] for axis in range(3)]
        rows = []
        for place in places:
            parts = pieces_of(place)
            rows += [scale * parts[pair[which]] for pair in PAIRS]
        norm = places[0] * places[0] + places[1] * places[1] + places[2] * places[2] + extra
        sides = [pieces_of(norm), [ones] * 3]
        rows += sides[which] + sides[1 - which]
        rows += [0.0 * ones] * (DEPTH - len(rows))
        for at, row in enumerate(rows):
            for frag in range(frag_dev):
                target[first + frag, at : at + 1, :] = row[frag : frag + 1, :]

    fill(side_ref, 0, own_ref, -2.0, 1.0, 0)
    left_out[...] = side_ref[...].astype(jnp.bfloat16)
    fill(table_side, reach * frag_dev, sources[0], 1.0, 0.0, 1)
    for at in range(1, around):
        step = (at - 1) % reach + 1
        side = lax.rem(frag_at // step + lax.axis_index("tile") + (at - 1) // reach, 2)
        spot = reach + step * (1 - 2 * side)
        fill(table_side, spot * frag_dev, sources[at], 1.0, 0.0, 1)
    for frag in range(frag_dev):
        for k in range(near):
            other = near_ref[frag, k]
            near_hot[frag, k : k + 1, :] = (lane == row_of(other)).astype(jnp.float32)
            right_out[frag, k] = table_side[other - first_frag].astype(jnp.bfloat16)
        for m in range(far):
            far_hot[frag, m : m + 1, :] = (lane == row_of(far_ref[frag, m])).astype(jnp.float32)


def gather_charges(charge_ref, near_hot, far_hot, near_charge, far_block):
    basis = near_charge.shape[2]
    rows = charge_ref[...].reshape(charge_ref.shape[0], charge_ref.shape[2])
    share = rows.shape[1] // basis
    tail, wide = rows[:, share * basis :], 4 * PC
    charges = [rows[:, spot * basis : (spot + 1) * basis] for spot in range(share)]
    blocks = [tail]
    for spot in range(1, share):
        blocks.append(jnp.concatenate([tail[:, spot * wide :], tail[:, : spot * wide]], axis=1))
    for hot, gathered, part in (
        (near_hot, near_charge, jnp.concatenate(charges, axis=0)),
        (far_hot, far_block, jnp.concatenate(blocks, axis=0)),
    ):
        every = hot[...].reshape(-1, hot.shape[2]).astype(jnp.bfloat16)
        pieces = [piece.astype(jnp.bfloat16) for piece in pieces_of(part)]
        sums = [jnp.dot(every, piece, preferred_element_type=jnp.float32) for piece in pieces]
        picked = sums[0] + sums[1] + sums[2]
        gathered[...] = picked.reshape(gathered.shape)


def esp_rows_of(first, count, own_ref, left_ref, right_ref, over_ref, near_charge, far_block):
    _, rows, basis = over_ref.shape
    near, far = near_charge.shape[1], far_block.shape[1]
    pick = own_rows(rows, basis, lax.axis_index("tile") * rows)
    quantities = [block_lanes(at) for at in range(4)]
    for frag in range(first, first + count):
        folded = jnp.zeros((basis, LANES), jnp.float32)
        for k in range(near):
            square = lax.dot_general(
                left_ref[frag],
                right_ref[frag, k],
                (((0,), (0,)), ((), ())),
                preferred_element_type=jnp.float32,
            )
            terms = lax.rsqrt(square) * near_charge[frag, k : k + 1, :]
            for start in range(0, basis, LANES):
                folded = folded + terms[:, start : start + LANES]
        blocks = jnp.zeros((PC, basis), jnp.float32)
        spots = [own_ref[axis, frag : frag + 1, :] for axis in range(3)]
        for m in range(far):
            row = far_block[frag, m : m + 1, :]
            x, y, z, charge = [
                jnp.sum(jnp.where(lanes, row, 0.0), axis=1, keepdims=True) for lanes in quantities
            ]
            total = (spots[0] - x) ** 2 + (spots[1] - y) ** 2 + (spots[2] - z) ** 2
            blocks = blocks + charge * lax.rsqrt(total + 1.0)
        potential = jnp.sum(folded.T, axis=0, keepdims=True) + jnp.sum(blocks, axis=0, keepdims=True)
        potential = (0.5 * SCREENING) * potential
        mine = jnp.sum(jnp.where(pick, potential, 0.0), axis=1, keepdims=True)
        yield frag, over_ref[frag] * (mine + potential)


def first_esp_kernel(charge_ref, near_hot, far_hot, *refs):
    inputs, (esp_ref, near_charge, far_block) = refs[:4], refs[4:]
    gather_charges(charge_ref, near_hot, far_hot, near_charge, far_block)
    for frag, rows in esp_rows_of(0, esp_ref.shape[0], *inputs, near_charge, far_block):
        esp_ref[frag] = rows


def last_esp_kernel(tiles, *refs):
    inputs, done_ref, chunks = refs[:6], refs[6], refs[7 : 7 + tiles]
    density_ref, esp_ref, rest_ref, sems = refs[7 + tiles :]
    share, done = chunks[0].shape[0], done_ref.shape[0]
    copies = [pltpu.make_async_copy(done_ref, esp_ref.at[pl.ds(0, done)], sems.at[tiles])]
    for shift in range(tiles):
        target = density_ref.at[pl.ds(partner(shift, tiles, -1) * share, share)]
        copies.append(pltpu.make_async_copy(chunks[shift], target, sems.at[shift]))
    for copy in copies:
        copy.start()
    rest = rest_ref.shape[0]
    for frag, rows in esp_rows_of(done, rest, *inputs):
        rest_ref[frag - done] = rows
    copies.append(pltpu.make_async_copy(rest_ref, esp_ref.at[pl.ds(done, rest)], sems.at[tiles + 1]))
    copies[-1].start()
    for copy in copies:
        copy.wait()


def call(kernel, outs, inputs, specs, scratch=(), cost=None, out_spec=VMEM):
    return pl.pallas_call(
        kernel,
        out_shape=outs,
        in_specs=specs,
        out_specs=[out_spec] * len(outs),
        scratch_shapes=list(scratch),
        cost_estimate=cost,
        compiler_params=pltpu.CompilerParams(vmem_limit_bytes=24 * 1024 * 1024),
    )(*inputs)


def exchanged(chunks):
    tiles = lax.axis_size("tile")
    places = tiles // 2
    moved = [chunks[0]]
    for shift in range(1, tiles):
        pairs = []
        for tile in range(tiles):
            half = tile // places if shift < places else 1 - tile // places
            pairs.append((tile, half * places + (tile + shift) % places))
        moved.append(lax.ppermute(chunks[shift], "tile", pairs))
    return moved


def neighbours(x, reach):
    peers, tiles = lax.axis_size("frag"), lax.axis_size("tile")
    found = []
    for step in range(1, reach + 1):
        pairs = []
        for low in range(peers - step):
            for tile in range(low // step % 2, tiles, 2):
                ends = low * tiles + tile, (low + step) * tiles + tile
                pairs += [ends, ends[::-1]]
        found.append(lax.ppermute(x, ("frag", "tile"), pairs))
    return found


def from_next_tile(x):
    tiles = lax.axis_size("tile")
    return lax.ppermute(x, "tile", [(tile, tile ^ 1) for tile in range(tiles)])


def per_device(
    core_fock,
    intersection,
    gamma_tile,
    charge_old,
    embed_old,
    core_pop,
    centres,
    frag_sizes,
    near_list,
    far_list,
):
    frag_dev, rows, basis = core_fock.shape
    tiles, peers = lax.axis_size("tile"), lax.axis_size("frag")
    devices, share = tiles * peers, frag_dev // tiles
    chunk = floats(share, rows, basis)
    places = jnp.transpose(centres, (1, 0, 2))
    inputs = (frag_sizes, charge_old, embed_old, core_pop, places, gamma_tile, intersection, core_fock)
    near_part = floats(2, share, rows, basis)
    far_part = floats(share, rows + 8, basis // 2)
    *sent, facts = call(
        functools.partial(half_fock_kernel, tiles),
        [near_part] * (tiles // 2) + [far_part] * (tiles // 2) + [floats(3 * share, basis)],
        [pltpu.with_memory_space_constraint(x, pltpu.HBM) for x in inputs],
        [HBM] * len(inputs),
        [pltpu.SMEM(frag_sizes.shape, jnp.int32)]
        + [pltpu.VMEM(x.shape, jnp.float32) for x in inputs[1:6]]
        + [pltpu.VMEM((frag_dev // 2, rows, width), jnp.float32) for width in (basis, basis, basis // 2, basis // 2)]
        + [pltpu.SemaphoreType.DMA((len(inputs) + 2,))],
    )
    sent = exchanged(sent)
    swaps = neighbours(places, -(-SPAN // frag_dev))
    *pieces, charges = call(
        functools.partial(density_kernel, tiles),
        [chunk] * tiles + [floats(devices, 1, share * basis + LANES)],
        (facts, *sent),
        [VMEM] * (1 + tiles),
        [pltpu.VMEM((share, basis, basis), jnp.float32)] * 2,
        pl.CostEstimate(flops=0, bytes_accessed=0, transcendentals=0),
    )
    moved = exchanged(pieces)
    charges, swaps = lax.optimization_barrier((charges, swaps))
    sources = [places, *swaps, *[from_next_tile(x) for x in swaps]]
    charges = lax.all_to_all(charges, ("tile", "frag"), split_axis=0, concat_axis=0, tiled=True)
    near, far, frags = near_list.shape[1], far_list.shape[1], peers * frag_dev
    parts = call(
        functools.partial(geometry_kernel, len(sources)),
        [
            jax.ShapeDtypeStruct((frag_dev, DEPTH, basis), jnp.bfloat16),
            jax.ShapeDtypeStruct((frag_dev, near, DEPTH, basis), jnp.bfloat16),
            floats(frag_dev, near, frags),
            floats(frag_dev, far, frags),
        ],
        (near_list, far_list, places, *sources, pieces[0]),
        [SMEM, SMEM] + [VMEM] * (1 + len(sources)) + [ANY],
        [
            pltpu.VMEM((frag_dev, DEPTH, basis), jnp.float32),
            pltpu.VMEM((len(sources) * frag_dev, DEPTH, basis), jnp.float32),
        ],
        pl.CostEstimate(flops=0, bytes_accessed=0, transcendentals=0),
    )
    left, right, near_hot, far_hot = parts
    inputs = (places, left, right, intersection)
    done = frag_dev * 3 // 4
    rest = frag_dev - done
    esp_rows, near_charge, far_block = call(
        first_esp_kernel,
        [floats(done, rows, basis), floats(frag_dev, near, basis), floats(frag_dev, far, LANES)],
        (charges, near_hot, far_hot, *inputs),
        [VMEM] * 7,
        cost=pl.CostEstimate(flops=0, bytes_accessed=0, transcendentals=0),
    )
    density, esp_matrix = call(
        functools.partial(last_esp_kernel, tiles),
        [floats(frag_dev, rows, basis)] * 2,
        (*inputs, near_charge, far_block, esp_rows, *moved),
        [VMEM] * (7 + tiles),
        [pltpu.VMEM((rest, rows, basis), jnp.float32), pltpu.SemaphoreType.DMA((tiles + 2,))],
        pl.CostEstimate(flops=0, bytes_accessed=0, transcendentals=0),
        HBM,
    )
    return (density, esp_matrix)


def solution(mesh):
    in_specs = (
        P("frag", "tile", None),
        P("frag", "tile", None),
        P("frag", "tile", None),
        P("frag", None),
        P("frag", None),
        P("frag", None),
        P("frag", None, None),
        P("frag"),
        P("frag", None),
        P("frag", None),
    )
    out_specs = (P("frag", "tile", None), P("frag", "tile", None))
    return jax.shard_map(
        per_device, mesh=mesh, in_specs=in_specs, out_specs=out_specs, check_vma=False
    )
```
